32 devices in a mesh: lat: 4 (over z), lon: 4 (over y, x), batch: 2 (over core).
Axes of the slice: x: 2, y: 2, z: 4, core: 2. Of those that a mesh axis runs over, the one named last changes fastest.
Arguments:
- inputs: bfloat16 [2, 32, 720, 256], P('batch', 'lat', 'lon'), may hold values from -8.6 to 8.6
- gain_one: float32 [256], replicated, may hold values from 0.5 to 1.5
- shift_one: float32 [256], replicated, may hold values from -4 to 4
- spectral: bfloat16 [368, 2, 256, 256], P(('lat', 'lon')), may hold values from -0.25 to 0.25
- gain_two: float32 [256], replicated, may hold values from 0.5 to 1.5
- shift_two: float32 [256], replicated, may hold values from -4 to 4
- w_up: bfloat16 [256, 512], replicated, may hold values from -0.375 to 0.375
- b_up: float32 [512], replicated, may hold values from -6 to 6
- w_down: bfloat16 [512, 256], replicated, may hold values from -0.25 to 0.25
- b_down: float32 [256], replicated, may hold values from -4 to 4
- crops: int32 [2, 4], P('batch'), may hold values from 0 to 720, as said below
- cotangent: bfloat16 [2, 32, 720, 256], P('batch', 'lat', 'lon'), may hold values from -6 to 6
- run_mean: float32 [256], replicated, may hold values from -6 to 6
- run_var: float32 [256], replicated, may hold values from 0.5 to 2
- momentum: float32 [], replicated, may hold values from 0.2 to 0.8
Outputs:
- output: bfloat16 [2, 32, 720, 256], P('batch', 'lat', 'lon')
- d_inputs: float32 [2, 32, 720, 256], P('batch', 'lat', 'lon')
- d_gain_one: float32 [256], replicated
- d_shift_one: float32 [256], replicated
- d_spectral: float32 [368, 2, 256, 256], P(('lat', 'lon'))
- d_gain_two: float32 [256], replicated
- d_shift_two: float32 [256], replicated
- d_w_up: float32 [256, 512], replicated
- d_b_up: float32 [512], replicated
- d_w_down: float32 [512, 256], replicated
- d_b_down: float32 [256], replicated
- new_mean: float32 [256], replicated
- new_var: float32 [256], replicated
The draws below stay inside these ranges and needn't reach their ends.
Inputs may be any that keep to these rules, and one draw needn't show every extreme that they name: `crops`: each crop's end row exceeds 32 - 8 and its first row is below 8; each crop's first column is below 240 and its end column exceeds 720 - 720 // 3; one sample's crop is the whole band.
All inputs are finite; a program needn't handle non-finite values.
Results may differ from the reference program's by a relative error of at most 0.02.
Values may be sent and summed in bfloat16 or wider, within the bound.
No kernel may reach another device: no remote copies, remote signals or barrier semaphores. Data moves between devices by JAX's collectives and lax.ppermute only.
A program may use at most 192 MiB of HBM per device.

```python
import math
import jax
import jax.numpy as jnp
from jax import lax

GRID_ROWS = 360
NLON = 720
M = 360
L = 360
C = 256
HID = 512
LAT_DEV = 8
NLAT = 32
M_PAD = 360
L_PAD = 368
B = 2


def draw_crops(key, part):
    key = jax.random.fold_in(key, 11)
    subkeys = jax.random.split(key, 5)
    lat_start = jax.random.randint(subkeys[0], (B,), 0, LAT_DEV)
    lat_end = NLAT - jax.random.randint(subkeys[1], (B,), 0, LAT_DEV)
    lon_start = jax.random.randint(subkeys[2], (B,), 0, NLON // 3)
    lon_end = NLON - jax.random.randint(subkeys[3], (B,), 0, NLON // 3)
    whole_one = jax.random.randint(subkeys[4], (), 0, B)
    chosen = jnp.arange(B) == whole_one
    lat_start = jnp.where(chosen, 0, lat_start)
    lat_end = jnp.where(chosen, NLAT, lat_end)
    lon_start = jnp.where(chosen, 0, lon_start)
    lon_end = jnp.where(chosen, NLON, lon_end)
    return jnp.stack([lat_start, lat_end, lon_start, lon_end], 1).astype(jnp.int32)


def draw_inputs(key, part):
    key = jax.random.fold_in(key, 5)
    subkeys = jax.random.split(key, 3)
    noise = jnp.clip(jax.random.normal(subkeys[0], (B, NLAT, NLON, C), jnp.float32), -6.0, 6.0)
    amplitude = jax.random.uniform(subkeys[1], (C,), jnp.float32, 0.8, 2.0)
    phase = jax.random.uniform(subkeys[2], (C,), jnp.float32, -math.pi, math.pi)
    column = jnp.arange(NLON).astype(jnp.float32) * (2.0 * math.pi / NLON)
    wave = amplitude[None, :] * jnp.cos(column[:, None] + phase[None, :])
    return (noise + wave[None, None, :, :]).astype(jnp.bfloat16)


def block_scale(stream_key, shape, cuts, smallest, top_value):
    factor_of = 1.0
    for axis_at, parts in cuts:
        draws = jax.random.uniform(jax.random.fold_in(jax.random.fold_in(stream_key, 6), axis_at), (parts,), jnp.float32, smallest / len(cuts), top_value / len(cuts))
        factor_of = factor_of * jnp.repeat(jnp.exp(draws), shape[axis_at] // parts).reshape((-1,) + (1,) * (len(shape) - 1 - axis_at))
    return factor_of


def normal_values(rng, shape, scale, limit, cuts=(), kind=jnp.bfloat16):
    entries = jax.random.normal(rng, shape, jnp.float32) * scale
    if len(cuts) > 0:
        entries = block_scale(rng, shape, cuts, -0.22, 0.18) * entries
    return jnp.clip(entries, min=-limit, max=limit).astype(kind)


def setup_inputs(seed: int = 0) -> dict:
    seeds = jax.random.split(jax.random.key(seed), 16)
    return {
        "inputs": draw_inputs(jax.random.fold_in(seeds[15], 71), 0),
        "gain_one": jnp.clip(1.0 + 0.1 * jax.random.normal(seeds[1], (C,), jnp.float32), 0.5, 1.5),
        "shift_one": normal_values(seeds[2], (C,), 0.3, 4.0, (), jnp.float32),
        "spectral": normal_values(seeds[3], (L_PAD, 2, C, C), (2 * C) ** -0.5, 0.25, ((0, 16),)),
        "gain_two": jnp.clip(1.0 + 0.1 * jax.random.normal(seeds[4], (C,), jnp.float32), 0.5, 1.5),
        "shift_two": normal_values(seeds[5], (C,), 0.3, 4.0, (), jnp.float32),
        "w_up": normal_values(seeds[6], (C, HID), C ** -0.5, 0.375),
        "b_up": normal_values(seeds[7], (HID,), 0.5, 6.0, (), jnp.float32),
        "w_down": normal_values(seeds[8], (HID, C), HID ** -0.5, 0.25),
        "b_down": normal_values(seeds[9], (C,), 0.3, 4.0, (), jnp.float32),
        "crops": draw_crops(jax.random.fold_in(seeds[15], 71), 0),
        "cotangent": normal_values(seeds[11], (B, NLAT, NLON, C), 1.0, 6.0, ((0, 2), (1, 4), (2, 4))),
        "run_mean": normal_values(seeds[12], (C,), 0.5, 6.0, (), jnp.float32),
        "run_var": jnp.clip(jax.random.uniform(seeds[13], (C,), jnp.float32, 0.5, 2.0), 0.5, 2.0),
        "momentum": jnp.clip(jax.random.uniform(seeds[14], (), jnp.float32, 0.2, 0.8), 0.2, 0.8),
    }


epsilon = 1e-05

@jax.custom_vjp
def low(v):
    return lax.optimization_barrier(v.astype(jnp.bfloat16)).astype(jnp.float32)

@jax.custom_vjp
def low_back(v):
    return v

def low_keep(v):
    return (low(v), None)

def low_pass(kept, grad):
    return (grad,)

def back_keep(v):
    return (v, None)

def back_low(kept, grad):
    return (low(grad),)
low.defvjp(low_keep, low_pass)
low_back.defvjp(back_keep, back_low)

def both_ways(values):
    return low_back(low(values))

def layer_norm(values, gain, shift):
    centre = values - lax.optimization_barrier(jnp.mean(values, -1, keepdims=True))
    spread = lax.optimization_barrier(jnp.mean(centre * centre, -1, keepdims=True))
    return centre * lax.rsqrt(spread + epsilon) * gain + shift

def fourier_tables(points, modes):
    column = jnp.arange(points, dtype=jnp.int32)
    order = jnp.arange(modes, dtype=jnp.int32)
    phase = column[:, None] * order[None, :] % points
    angle = phase.astype(jnp.float32) * (2.0 * math.pi / points)
    cosine = jnp.cos(angle)
    sine = jnp.sin(angle)
    scale = 1.0 / math.sqrt(points)
    forward_tab = jnp.stack([cosine * scale, -sine * scale], 1)
    factor = jnp.where(order == 0, 1.0, 2.0).astype(jnp.float32)
    inverse_tab = jnp.stack([(cosine * factor[None, :]).T, (-sine * factor[None, :]).T], 0)
    return (forward_tab.astype(jnp.bfloat16), inverse_tab.astype(jnp.bfloat16))

def grid_angles(rows_total):
    first_row = (GRID_ROWS - rows_total) // 2
    colatitude = (jnp.arange(rows_total, dtype=jnp.float32) + (first_row + 0.5)) * (math.pi / GRID_ROWS)
    return (jnp.cos(colatitude), jnp.sin(colatitude))

def legendre(orders, cosines, sine_vals, degrees):
    order_col = orders[:, None]
    cos_row = cosines[None, :]
    log_start = 0.5 * (jnp.log((2.0 * order_col + 1.0) / (4.0 * math.pi)) + lax.lgamma(order_col + 0.5) - lax.lgamma(order_col + 1.0) - 0.5 * math.log(math.pi)) + order_col * jnp.log(sine_vals[None, :])
    diagonal_start = jnp.exp(log_start)
    second_start = cos_row * jnp.sqrt(2.0 * order_col + 3.0) * diagonal_start
    zeros_grid = jnp.zeros_like(diagonal_start)

    def advance(state, degree):
        before, latest = state
        upper_ratio = jnp.sqrt((4.0 * degree * degree - 1.0) / jnp.maximum(degree * degree - order_col * order_col, 1.0))
        lower_ratio = jnp.sqrt(jnp.maximum((degree - 1.0) * (degree - 1.0) - order_col * order_col, 0.0) / jnp.maximum(4.0 * (degree - 1.0) * (degree - 1.0) - 1.0, 1.0))
        general = upper_ratio * (cos_row * latest - lower_ratio * before)
        current = jnp.where(degree < order_col, 0.0, jnp.where(degree == order_col, diagonal_start, jnp.where(degree == order_col + 1.0, second_start, general)))
        return ((latest, current), current)
    ignored, stacked = lax.scan(advance, (zeros_grid, zeros_grid), jnp.arange(degrees).astype(cosines.dtype))
    stacked = jnp.transpose(stacked, (1, 0, 2))
    degree_index = jnp.arange(degrees).astype(cosines.dtype)
    keep = (orders[:, None, None] < M) & (degree_index[None, :, None] < L)
    return jnp.where(keep, stacked, 0.0)

def reference(inputs, gain_one, shift_one, spectral, gain_two, shift_two, w_up, b_up, w_down, b_down, crops, cotangent, run_mean, run_var, momentum):
    highest = lax.Precision.HIGHEST
    forward_tab, inverse_tab = fourier_tables(NLON, M_PAD)
    forward_tab = forward_tab.astype(jnp.float32)
    inverse_tab = inverse_tab.astype(jnp.float32)
    cosines, sine_vals = grid_angles(NLAT)
    orders = jnp.arange(M_PAD).astype(jnp.float32)
    poly = legendre(orders, cosines, sine_vals, L_PAD)
    quadrature = sine_vals * (math.pi / GRID_ROWS) * (2.0 * math.pi / math.sqrt(NLON))
    analysis = (poly * quadrature[None, None, :]).astype(jnp.bfloat16).astype(jnp.float32)
    synthesis = poly.astype(jnp.bfloat16).astype(jnp.float32)

    def forward(input_wide, g_one, s_one, spec, g_two, s_two, up_mat, up_bias, down_mat, down_bias):
        normed = both_ways(layer_norm(input_wide, g_one, s_one))
        fourier = both_ways(jnp.einsum('bijc,jrm->birmc', normed, forward_tab, precision=highest))
        coeffs = both_ways(jnp.einsum('mli,birmc->bmlrc', analysis, fourier, precision=highest))
        real_part = jnp.einsum('bmlc,lcd->bmld', coeffs[:, :, :, 0], spec[:, 0], precision=highest) - jnp.einsum('bmlc,lcd->bmld', coeffs[:, :, :, 1], spec[:, 1], precision=highest)
        imag_part = jnp.einsum('bmlc,lcd->bmld', coeffs[:, :, :, 0], spec[:, 1], precision=highest) + jnp.einsum('bmlc,lcd->bmld', coeffs[:, :, :, 1], spec[:, 0], precision=highest)
        mixed_modes = both_ways(jnp.stack([real_part, imag_part], 3))
        grid_modes = both_ways(jnp.einsum('mli,bmlrc->birmc', synthesis, mixed_modes, precision=highest))
        spread = both_ways(jnp.einsum('birmc,rmj->bijc', grid_modes, inverse_tab, precision=highest))
        skipped = input_wide + spread
        normed_two = low(layer_norm(skipped, g_two, s_two))
        preact = low_back(jnp.einsum('bijc,ch->bijh', normed_two, up_mat, precision=highest) + up_bias)
        activated = low(jax.nn.gelu(preact))
        return skipped + jnp.einsum('bijh,hc->bijc', activated, down_mat, precision=highest) + down_bias
    result, pullback = jax.vjp(forward, inputs.astype(jnp.float32), gain_one, shift_one, spectral.astype(jnp.float32), gain_two, shift_two, w_up.astype(jnp.float32), b_up, w_down.astype(jnp.float32), b_down)
    gradients = pullback(cotangent.astype(jnp.float32))
    row_index = jnp.arange(NLAT, dtype=jnp.int32)
    col_index = jnp.arange(NLON, dtype=jnp.int32)
    inside_rows = (row_index[None, :] >= crops[:, 0:1]) & (row_index[None, :] < crops[:, 1:2])
    inside_cols = (col_index[None, :] >= crops[:, 2:3]) & (col_index[None, :] < crops[:, 3:4])
    mask_grid = (inside_rows[:, :, None] & inside_cols[:, None, :]).astype(jnp.float32)[..., None]
    valid_count = jnp.sum(mask_grid)
    batch_mean = lax.optimization_barrier(jnp.sum(mask_grid * result, (0, 1, 2))) / valid_count
    batch_var = lax.optimization_barrier(jnp.sum(mask_grid * result * result, (0, 1, 2))) / valid_count - batch_mean * batch_mean
    new_mean = (1.0 - momentum) * run_mean + momentum * batch_mean
    new_var = (1.0 - momentum) * run_var + momentum * batch_var
    return (result.astype(jnp.bfloat16), gradients[0], gradients[1], gradients[2], gradients[3], gradients[4], gradients[5], gradients[6], gradients[7], gradients[8], gradients[9], new_mean, new_var)
```

```python
import math

import jax
import jax.numpy as jnp
from jax import lax
from jax.experimental import pallas as pl
from jax.experimental.pallas import tpu as pltpu
from jax.sharding import PartitionSpec as P

GRID_ROWS = 360
M = 360
L = 360


epsilon = 1e-05
GROUP = 16


def layer_norm(values, gain, shift):
    centre = values - jnp.mean(values, -1, keepdims=True)
    spread = jnp.mean(centre * centre, -1, keepdims=True)
    return centre * lax.rsqrt(spread + epsilon) * gain + shift


def xor_pairs(count, bit):
    return [(i, i ^ bit) for i in range(count)]


def ring_pairs(count, step):
    return [(i, (i + step) % count) for i in range(count)]


def swap_cores(values):
    return lax.ppermute(values, "batch", [(0, 1), (1, 0)])


def turned(cosine, sine, quarter_turns):
    turns = quarter_turns % 4
    real = jnp.where(turns == 0, cosine, jnp.where(turns == 1, -sine, jnp.where(turns == 2, -cosine, sine)))
    imag = jnp.where(turns == 0, -sine, jnp.where(turns == 1, -cosine, jnp.where(turns == 2, sine, cosine)))
    return real, imag


def dft_tables(points, parts, kept, slots):
    cols = points // parts
    slot = jnp.arange(parts * slots, dtype=jnp.int32)
    order = slot // slots * kept + slot % slots
    valid = slot % slots < kept
    column = jnp.arange(cols, dtype=jnp.int32)

    def base(order, valid, column):
        angle = (order * column % points).astype(jnp.float32) * (2.0 * math.pi / points)
        real = jnp.where(valid, jnp.cos(angle), 0.0)
        imag = jnp.where(valid, jnp.sin(angle), 0.0)
        return lax.optimization_barrier((real.astype(jnp.bfloat16), imag.astype(jnp.bfloat16)))

    part = jnp.arange(parts, dtype=jnp.int32)[:, None, None]
    cosine, sine = base(order[:, None], valid[:, None], column[None, :])
    to_modes = jnp.concatenate(turned(cosine[None], sine[None], part * order[None, :, None]), 1)
    cosine, sine = base(order[None, :], valid[None, :], column[:, None])
    to_columns = jnp.concatenate(turned(cosine[None], sine[None], part * order[None, None, :]), 2)
    return to_modes, to_columns


def legendre_kernel(owned_half, starts_ref, upper_ref, lower_ref, order_ref, cos_ref, diag_ref, second_ref, out_ref, all_ref):
    degrees = all_ref.shape[0]
    cosines = cos_ref[...]
    diagonal = diag_ref[...]
    second = second_ref[...]
    order = order_ref[...]

    def advance(degree, state):
        before, latest = state
        level = degree.astype(jnp.float32)
        upper = upper_ref[pl.ds(degree, 1), :]
        lower = lower_ref[pl.ds(degree, 1), :]
        general = upper * (cosines * latest - lower * before)
        current = jnp.where(
            level < order,
            0.0,
            jnp.where(level == order, diagonal, jnp.where(level == order + 1.0, second, general)),
        )
        all_ref[pl.ds(degree, 1)] = current[None]
        return latest, current

    unroll = 8 if degrees % 8 == 0 else 1

    def several(step, state):
        for at in range(unroll):
            state = advance(step * unroll + at, state)
        return state

    zeros = cosines * 0.0
    lax.fori_loop(0, degrees // unroll, several, (zeros, zeros))
    blocks = out_ref.shape[0] // owned_half
    for block in range(blocks):

        def copy(at, carry, block=block):
            degree = starts_ref[block] + at
            value = all_ref[pl.ds(degree, 1)]
            keep = (degree < L) & (at >= starts_ref[blocks])
            out_ref[pl.ds(at * blocks + block, 1)] = jnp.where(keep, value, 0.0)
            return carry

        lax.fori_loop(0, owned_half, copy, 0)


def legendre(starts, skip, orders, valid, cosines, sine_vals, degrees, owned_half):
    order_row = orders[None, :]
    sine_col = sine_vals[:, None]
    log_start = 0.5 * (
        jnp.log((2.0 * order_row + 1.0) / (4.0 * math.pi))
        + lax.lgamma(order_row + 0.5)
        - lax.lgamma(order_row + 1.0)
        - 0.5 * math.log(math.pi)
    ) + order_row * jnp.log(sine_col)
    diagonal = jnp.where(valid[None, :], jnp.exp(log_start), 0.0)
    second = cosines[:, None] * jnp.sqrt(2.0 * order_row + 3.0) * diagonal
    degree = jnp.arange(degrees, dtype=jnp.float32)[:, None]
    upper = jnp.sqrt((4.0 * degree * degree - 1.0) / jnp.maximum(degree * degree - order_row * order_row, 1.0))
    lower = jnp.sqrt(
        jnp.maximum((degree - 1.0) * (degree - 1.0) - order_row * order_row, 0.0)
        / jnp.maximum(4.0 * (degree - 1.0) * (degree - 1.0) - 1.0, 1.0)
    )
    shape = diagonal.shape
    blocks = starts.shape[0]
    return pl.pallas_call(
        lambda *refs: legendre_kernel(owned_half, *refs),
        out_shape=jax.ShapeDtypeStruct((blocks * owned_half,) + shape, jnp.float32),
        in_specs=[pl.BlockSpec(memory_space=pltpu.SMEM)] + [pl.BlockSpec(memory_space=pltpu.VMEM)] * 6,
        out_specs=pl.BlockSpec(memory_space=pltpu.VMEM),
        scratch_shapes=[pltpu.VMEM((degrees,) + shape, jnp.float32)],
        compiler_params=pltpu.CompilerParams(vmem_limit_bytes=24 * 2**20),
        name="legendre",
    )(
        jnp.concatenate([starts, skip[None]]).astype(jnp.int32),
        upper,
        lower,
        jnp.broadcast_to(order_row, shape),
        jnp.broadcast_to(cosines[:, None], shape),
        diagonal,
        second,
    )


def block_tables(poly, slots):
    degrees, rows, _ = poly.shape
    groups = slots // GROUP
    low = poly[:, :, :slots].astype(jnp.bfloat16).reshape(degrees, rows, groups, GROUP)

    def expand(table, depth):
        lanes = depth * GROUP
        lane = jnp.arange(lanes, dtype=jnp.int32)
        repeat = (jnp.arange(depth, dtype=jnp.int32)[:, None] == lane[None, :] // GROUP).astype(jnp.bfloat16)
        flat = table.reshape(-1, depth)
        wide = jnp.dot(flat, repeat, preferred_element_type=jnp.float32)
        row = jnp.arange(flat.shape[0], dtype=jnp.int32)
        same = row[:, None] % GROUP == lane[None, :] % GROUP
        return jnp.where(same, wide, 0.0).astype(jnp.bfloat16).reshape(groups, -1, lanes)

    return expand(low.transpose(2, 0, 3, 1), rows), expand(low.transpose(2, 1, 3, 0), degrees)


def dft_kernel(table_ref, values_ref, scale_ref, out_ref):
    parts = table_ref.shape[0]
    slots = out_ref.shape[2]
    width = values_ref.shape[3]
    total = jnp.dot(table_ref[0], values_ref[0, 0], preferred_element_type=jnp.float32)
    for part in range(1, parts):
        total += jnp.dot(table_ref[part], values_ref[part, 0], preferred_element_type=jnp.float32)
    half = total.shape[0] // 2
    scale = scale_ref[0]
    for owner in range(out_ref.shape[0]):
        at = owner * slots
        kept = scale[at : at + slots]
        out_ref[owner, 0, :, :width] = (total[at : at + slots] * kept).astype(jnp.bfloat16)
        out_ref[owner, 0, :, width:] = (total[half + at : half + at + slots] * kept).astype(jnp.bfloat16)


def dft(table, values, scale, slots):
    parts, rows, cols, width = values.shape
    return pl.pallas_call(
        dft_kernel,
        grid=(rows,),
        out_shape=jax.ShapeDtypeStruct((parts, rows, slots, 2 * width), jnp.bfloat16),
        in_specs=[
            pl.BlockSpec(table.shape, lambda i: (0, 0, 0)),
            pl.BlockSpec((parts, 1, cols, width), lambda i: (0, i, 0, 0)),
            pl.BlockSpec((1,) + scale.shape[1:], lambda i: (i, 0, 0)),
        ],
        out_specs=pl.BlockSpec((parts, 1, slots, 2 * width), lambda i: (0, i, 0, 0)),
        compiler_params=pltpu.CompilerParams(vmem_limit_bytes=40 * 2**20),
        name="dft",
    )(table, values, scale)


def inverse_dft_kernel(doubled, table_ref, modes_ref, scale_ref, out_ref):
    parts = table_ref.shape[0]
    width = out_ref.shape[3]
    modes = modes_ref[:, 0]
    flat = jnp.concatenate([modes[:, :, :width].reshape(-1, width), modes[:, :, width:].reshape(-1, width)], 0)
    for part in range(parts):
        total = jnp.dot(table_ref[part], flat, preferred_element_type=jnp.float32)
        if doubled:
            total = 2.0 * total - modes[0, 0:1, :width].astype(jnp.float32)
        else:
            total = total * scale_ref[0]
        out_ref[part, 0] = total.astype(jnp.bfloat16)


def inverse_dft(table, modes, scale, doubled):
    parts, rows, slots, wide = modes.shape
    cols = table.shape[1]
    width = wide // 2
    return pl.pallas_call(
        lambda *refs: inverse_dft_kernel(doubled, *refs),
        grid=(rows,),
        out_shape=jax.ShapeDtypeStruct((parts, rows, cols, width), jnp.bfloat16),
        in_specs=[
            pl.BlockSpec(table.shape, lambda i: (0, 0, 0)),
            pl.BlockSpec((parts, 1, slots, wide), lambda i: (0, i, 0, 0)),
            pl.BlockSpec((1, 1, width), lambda i: (i, 0, 0)),
        ],
        out_specs=pl.BlockSpec((parts, 1, cols, width), lambda i: (0, i, 0, 0)),
        compiler_params=pltpu.CompilerParams(vmem_limit_bytes=40 * 2**20),
        name="inverse_dft",
    )(table, modes, scale)


def analyse_kernel(samples, table_ref, *refs):
    out_ref = refs[-1]
    per = (len(refs) - 1) // samples
    for sample in range(samples):
        rows = jnp.concatenate(
            [ref[...].reshape(-1, ref.shape[-1]) for ref in refs[sample * per : sample * per + per]], 0
        )
        total = jnp.dot(table_ref[0], rows, preferred_element_type=jnp.float32)
        out_ref[:, sample] = total.reshape(-1, GROUP, total.shape[-1]).astype(jnp.bfloat16)


def analyse(table, own, other):
    rows, slots, wide = own[0].shape
    groups = slots // GROUP
    degrees = table.shape[1] // GROUP
    shard = pl.BlockSpec((rows, GROUP, wide), lambda g: (0, g, 0))
    return pl.pallas_call(
        lambda *refs: analyse_kernel(2, *refs),
        grid=(groups,),
        out_shape=jax.ShapeDtypeStruct((degrees, 2, slots, wide), jnp.bfloat16),
        in_specs=[pl.BlockSpec((1,) + table.shape[1:], lambda g: (g, 0, 0))] + [shard] * (len(own) + len(other)),
        out_specs=pl.BlockSpec((degrees, 2, GROUP, wide), lambda g: (0, 0, g, 0)),
        compiler_params=pltpu.CompilerParams(vmem_limit_bytes=40 * 2**20),
        name="analyse",
    )(table, *own, *other)


def synthesise_kernel(doubled, table_ref, modes_ref, *out_refs):
    per = len(out_refs) // 2
    group = pl.program_id(0)
    for sample in range(2):
        modes = modes_ref[:, sample]
        total = jnp.dot(
            table_ref[0], modes.reshape(-1, modes.shape[-1]), preferred_element_type=jnp.float32
        ).astype(jnp.bfloat16)
        for at in range(per):
            ref = out_refs[sample * per + at]
            count = ref.shape[0] * GROUP
            ref[...] = total[at * count : at * count + count].reshape(ref.shape)


def synthesise(table, modes, parts):
    degrees, _, slots, wide = modes.shape
    groups = slots // GROUP
    rows = table.shape[1] // GROUP // parts
    shard = pl.BlockSpec((rows, GROUP, wide), lambda g: (0, g, 0))
    out = pl.pallas_call(
        lambda *refs: synthesise_kernel(False, *refs),
        grid=(groups,),
        out_shape=[jax.ShapeDtypeStruct((rows, slots, wide), jnp.bfloat16)] * (2 * parts),
        in_specs=[
            pl.BlockSpec((1,) + table.shape[1:], lambda g: (g, 0, 0)),
            pl.BlockSpec((degrees, 2, GROUP, wide), lambda g: (0, 0, g, 0)),
        ],
        out_specs=[shard] * (2 * parts),
        compiler_params=pltpu.CompilerParams(vmem_limit_bytes=40 * 2**20),
        name="synthesise",
    )(table, modes)
    return out[:parts], out[parts:]


def mix_kernel(coeffs_ref, *refs):
    weights, out_ref = refs[:-1], refs[-1]
    for block, weight_ref in enumerate(weights):
        width = weight_ref.shape[-1]
        real = coeffs_ref[block, :, :width]
        imag = coeffs_ref[block, :, width:]
        w_real = weight_ref[0, 0]
        w_imag = weight_ref[0, 1]
        dot = lambda a, b: jnp.dot(a, b, preferred_element_type=jnp.float32)
        out_ref[block, :, :width] = (dot(real, w_real) - dot(imag, w_imag)).astype(jnp.bfloat16)
        out_ref[block, :, width:] = (dot(real, w_imag) + dot(imag, w_real)).astype(jnp.bfloat16)


def mix(coeffs, weights):
    blocks = len(weights)
    degrees, rows, wide = coeffs.shape
    half = degrees // blocks
    weight = pl.BlockSpec((1,) + weights[0].shape[1:], lambda t: (t, 0, 0, 0))
    modes = pl.BlockSpec((blocks, rows, wide), lambda t: (t, 0, 0))
    return pl.pallas_call(
        mix_kernel,
        grid=(half,),
        out_shape=jax.ShapeDtypeStruct(coeffs.shape, jnp.bfloat16),
        in_specs=[modes] + [weight] * blocks,
        out_specs=modes,
        compiler_params=pltpu.CompilerParams(vmem_limit_bytes=40 * 2**20),
        name="mix",
    )(coeffs, *weights)


def mix_back_kernel(coeffs_ref, d_mixed_ref, *refs):
    blocks = coeffs_ref.shape[0]
    weights, out_ref, grads = refs[:blocks], refs[blocks], refs[blocks + 1 :]
    along = lambda a, b: lax.dot_general(a, b, (((1,), (1,)), ((), ())), preferred_element_type=jnp.float32)
    across = lambda a, b: lax.dot_general(a, b, (((0,), (0,)), ((), ())), preferred_element_type=jnp.float32)
    for block in range(blocks):
        width = weights[block].shape[-1]
        real = d_mixed_ref[block, :, :width]
        imag = d_mixed_ref[block, :, width:]
        c_real = coeffs_ref[block, :, :width]
        c_imag = coeffs_ref[block, :, width:]
        w_real = weights[block][0, 0]
        w_imag = weights[block][0, 1]
        out_ref[block, :, :width] = (along(real, w_real) + along(imag, w_imag)).astype(jnp.bfloat16)
        out_ref[block, :, width:] = (along(imag, w_real) - along(real, w_imag)).astype(jnp.bfloat16)
        grads[block][0, 0] = (across(c_real, real) + across(c_imag, imag)).astype(jnp.bfloat16)
        grads[block][0, 1] = (across(c_real, imag) - across(c_imag, real)).astype(jnp.bfloat16)


def mix_back(coeffs, d_mixed, weights):
    blocks = len(weights)
    degrees, rows, wide = coeffs.shape
    half = degrees // blocks
    weight = pl.BlockSpec((1,) + weights[0].shape[1:], lambda t: (t, 0, 0, 0))
    modes = pl.BlockSpec((blocks, rows, wide), lambda t: (t, 0, 0))
    out = pl.pallas_call(
        mix_back_kernel,
        grid=(half,),
        out_shape=[jax.ShapeDtypeStruct(coeffs.shape, jnp.bfloat16)]
        + [jax.ShapeDtypeStruct(w.shape, jnp.bfloat16) for w in weights],
        in_specs=[modes, modes] + [weight] * blocks,
        out_specs=[modes] + [weight] * blocks,
        compiler_params=pltpu.CompilerParams(vmem_limit_bytes=40 * 2**20),
        name="mix_back",
    )(coeffs, d_mixed, *weights)
    return out[0], out[1:]


def gather_rows(shard):
    count = lax.axis_size("lat")
    own = [shard]
    other = [swap_cores(shard)]
    for _ in range(1, count):
        own.append(lax.ppermute(own[-1], "lat", ring_pairs(count, 1)))
        other.append(swap_cores(own[-1]))
    return own, other


def scatter_rows(own, other):
    count = lax.axis_size("lat")
    arrived = None
    for slot in range(count - 1, -1, -1):
        total = own[slot].astype(jnp.float32) + swap_cores(other[slot]).astype(jnp.float32)
        if arrived is not None:
            total = total + arrived.astype(jnp.float32)
        total = total.astype(jnp.bfloat16)
        if slot > 0:
            arrived = lax.ppermute(total, "lat", ring_pairs(count, -1))
    return total


def gather_weights(own):
    count = lax.axis_size("lon")
    cut = own.shape[0] // 2
    first, last = own[:cut], own[cut:]
    near = [lax.ppermute(part, "lon", xor_pairs(count, 1)) for part in (first, last)]
    far = [lax.ppermute(part, "lon", xor_pairs(count, 2)) for part in (first, last)]
    both = [
        lax.ppermute(near[0], "lon", xor_pairs(count, 2)),
        lax.ppermute(far[1], "lon", xor_pairs(count, 1)),
    ]
    return [own] + [jnp.concatenate(pair, 0) for pair in (near, far, both)]


def scatter_weights(parts):
    count = lax.axis_size("lon")
    cut = parts[0].shape[0] // 2
    wide = lambda v: v.astype(jnp.float32)
    near = lambda v: lax.ppermute(v, "lon", xor_pairs(count, 1))
    far = lambda v: lax.ppermute(v, "lon", xor_pairs(count, 2))
    first = [part[:cut] for part in parts]
    last = [part[cut:] for part in parts]
    first_one, first_three = near(first[1]), near(first[3])
    last_two, last_three = far(last[2]), far(last[3])
    first_two = far((wide(first[2]) + wide(first_three)).astype(jnp.bfloat16))
    last_one = near((wide(last[1]) + wide(last_three)).astype(jnp.bfloat16))
    return jnp.concatenate(
        [
            (wide(first[0]) + wide(first_one) + wide(first_two)).astype(jnp.bfloat16),
            (wide(last[0]) + wide(last_one) + wide(last_two)).astype(jnp.bfloat16),
        ],
        0,
    )


def trade(values):
    return lax.all_to_all(values, "lon", split_axis=0, concat_axis=0, tiled=True)


def band_shards(
    inputs,
    gain_one,
    shift_one,
    spectral,
    gain_two,
    shift_two,
    w_up,
    b_up,
    w_down,
    b_down,
    crops,
    cotangent,
    run_mean,
    run_var,
    momentum,
):
    lat_count = lax.axis_size("lat")
    lon_count = lax.axis_size("lon")
    plane = lax.axis_index("lat")
    chip = lax.axis_index("lon")
    core = lax.axis_index("batch")
    rows_dev = inputs.shape[1]
    cols_dev = inputs.shape[2]
    width = inputs.shape[3]
    rows_chip = rows_dev // lon_count
    lat_rows = rows_dev * lat_count
    lon_cols = cols_dev * lon_count
    modes_dev = M // lon_count
    slots = (modes_dev + GROUP - 1) // GROUP * GROUP
    owned = spectral.shape[0]
    half = (owned + 1) // 2
    first_degree = core * (owned - half)
    skip = core * (2 * half - owned)

    weights = gather_weights(lax.dynamic_slice_in_dim(spectral, first_degree, half, 0))

    to_modes, to_columns = dft_tables(lon_cols, lon_count, modes_dev, slots)
    first_row = (GRID_ROWS - lat_rows) // 2
    slot_plane = (plane - jnp.arange(lat_count, dtype=jnp.int32)) % lat_count
    row = (slot_plane[:, None] * rows_dev + jnp.arange(rows_dev, dtype=jnp.int32)[None, :]).reshape(-1)
    colatitude = (row.astype(jnp.float32) + (first_row + 0.5)) * (math.pi / GRID_ROWS)
    lane = jnp.arange(128, dtype=jnp.int32)
    valid = lane < modes_dev
    orders = (chip * modes_dev + jnp.minimum(lane, modes_dev - 1)).astype(jnp.float32)
    owners = plane * lon_count + (chip ^ jnp.arange(lon_count, dtype=jnp.int32))
    degrees_all = owned * lat_count * lon_count
    poly = legendre(
        owners * owned + first_degree, skip, orders, valid, jnp.cos(colatitude), jnp.sin(colatitude), degrees_all, half
    )
    analysis, synthesis = block_tables(poly, slots)
    own_row = plane * rows_dev + chip * rows_chip + jnp.arange(rows_chip, dtype=jnp.int32)
    own_angle = (own_row.astype(jnp.float32) + (first_row + 0.5)) * (math.pi / GRID_ROWS)
    quadrature = jnp.sin(own_angle) * ((math.pi / GRID_ROWS) * (2.0 * math.pi / math.sqrt(lon_cols)) / math.sqrt(lon_cols))
    row_scale = jnp.broadcast_to(quadrature[:, None, None], (rows_chip, lon_count * slots, 1))
    column_scale = jnp.broadcast_to(quadrature[:, None, None], (rows_chip, 1, width))
    twice = jnp.where(jnp.arange(lon_count * slots, dtype=jnp.int32) == 0, 1.0, 2.0)
    mode_scale = jnp.broadcast_to(twice[None, :, None], (rows_chip, lon_count * slots, 1))

    by_row = (lon_count, rows_chip, cols_dev, width)
    whole = (rows_dev, cols_dev, width)
    input_wide = inputs[0].astype(jnp.float32)
    normed_one, norm_one_back = jax.vjp(layer_norm, input_wide, gain_one, shift_one)
    columns = trade(normed_one.astype(jnp.bfloat16).reshape(by_row))
    shard = trade(dft(to_modes, columns, row_scale, slots)).reshape(rows_dev, slots, 2 * width)
    coeffs = analyse(analysis, *gather_rows(shard))
    flat = (coeffs.shape[0], 2 * slots, 2 * width)
    coeffs_flat = coeffs.reshape(flat)
    mixed = mix(coeffs_flat, weights).reshape(coeffs.shape)
    grid = scatter_rows(*synthesise(synthesis, mixed, lat_count))
    grid = trade(grid.reshape(lon_count, rows_chip, slots, 2 * width))
    spread = trade(inverse_dft(to_columns, grid, column_scale, True)).reshape(whole)

    skipped = input_wide + spread.astype(jnp.float32)
    normed_two, norm_two_back = jax.vjp(layer_norm, skipped, gain_two, shift_two)
    normed_two_low = normed_two.astype(jnp.bfloat16)
    preact = jnp.einsum("ijc,ch->ijh", normed_two_low, w_up, preferred_element_type=jnp.float32) + b_up
    activated, gelu_back = jax.vjp(jax.nn.gelu, preact)
    activated_low = activated.astype(jnp.bfloat16)
    result = (
        skipped + jnp.einsum("ijh,hc->ijc", activated_low, w_down, preferred_element_type=jnp.float32) + b_down
    )
    output = result.astype(jnp.bfloat16)[None]
    bounds = crops[0]
    row_global = plane * rows_dev + jnp.arange(rows_dev, dtype=jnp.int32)
    col_global = chip * cols_dev + jnp.arange(cols_dev, dtype=jnp.int32)
    inside_rows = (row_global >= bounds[0]) & (row_global < bounds[1])
    inside_cols = (col_global >= bounds[2]) & (col_global < bounds[3])
    mask_grid = (inside_rows[:, None] & inside_cols[None, :]).astype(jnp.float32)[:, :, None]
    valid_count = jnp.sum(mask_grid)
    first_moment = jnp.sum(mask_grid * result, (0, 1))
    second_moment = jnp.sum(mask_grid * result * result, (0, 1))
    cotangent = cotangent[0]
    grad_wide = cotangent.astype(jnp.float32)
    d_down = jnp.einsum("ijh,ijc->hc", activated_low, cotangent, preferred_element_type=jnp.float32)
    d_down_bias = jnp.sum(grad_wide, (0, 1))
    d_activated = jnp.einsum("ijc,hc->ijh", cotangent, w_down, preferred_element_type=jnp.float32)
    d_preact = gelu_back(d_activated)[0].astype(jnp.bfloat16)
    d_up = jnp.einsum("ijc,ijh->ch", normed_two_low, d_preact, preferred_element_type=jnp.float32)
    d_up_bias = jnp.sum(d_preact.astype(jnp.float32), (0, 1))
    d_normed_two = jnp.einsum("ijh,ch->ijc", d_preact, w_up, preferred_element_type=jnp.float32)
    d_skipped, d_gain_two, d_shift_two = norm_two_back(d_normed_two)
    d_skipped = d_skipped + grad_wide
    d_spread = d_skipped.astype(jnp.bfloat16)

    d_columns = trade(d_spread.reshape(by_row))
    d_shard = trade(dft(to_modes, d_columns, mode_scale, slots)).reshape(rows_dev, slots, 2 * width)
    d_mixed = analyse(analysis, *gather_rows(d_shard)).reshape(flat)
    d_coeffs, d_weights = mix_back(coeffs_flat, d_mixed, weights)
    d_modes = scatter_rows(*synthesise(synthesis, d_coeffs.reshape(coeffs.shape), lat_count))
    d_modes = trade(d_modes.reshape(lon_count, rows_chip, slots, 2 * width))
    d_normed_one = trade(inverse_dft(to_columns, d_modes, column_scale, False)).reshape(whole)
    d_input_norm, d_gain_one, d_shift_one = norm_one_back(d_normed_one.astype(jnp.float32))
    d_inputs = (d_input_norm + d_skipped)[None]

    d_half = scatter_weights(d_weights)
    d_other = swap_cores(d_half)
    low = jnp.where(core == 0, d_half, d_other)
    high = jnp.where(core == 0, d_other, d_half)
    d_spectral = jnp.concatenate([low, high[2 * half - owned :]], 0).astype(jnp.float32)

    everywhere = ("lat", "lon", "batch")
    d_up, d_down = lax.psum((d_up, d_down), everywhere)
    d_up_bias, d_down_bias, d_gain_two, d_shift_two, valid_count, first_moment, second_moment = lax.psum(
        (d_up_bias, d_down_bias, d_gain_two, d_shift_two, valid_count, first_moment, second_moment), everywhere
    )
    d_gain_one, d_shift_one = lax.psum((d_gain_one, d_shift_one), everywhere)
    batch_mean = first_moment / valid_count
    batch_var = second_moment / valid_count - batch_mean * batch_mean
    new_mean = (1.0 - momentum) * run_mean + momentum * batch_mean
    new_var = (1.0 - momentum) * run_var + momentum * batch_var
    return (
        output,
        d_inputs,
        d_gain_one,
        d_shift_one,
        d_spectral,
        d_gain_two,
        d_shift_two,
        d_up,
        d_up_bias,
        d_down,
        d_down_bias,
        new_mean,
        new_var,
    )


def fourier_tables(points, modes):
    column = jnp.arange(points, dtype=jnp.int32)
    order = jnp.arange(modes, dtype=jnp.int32)
    phase = column[:, None] * order[None, :] % points
    angle = phase.astype(jnp.float32) * (2.0 * math.pi / points)
    cosine = jnp.cos(angle)
    sine = jnp.sin(angle)
    scale = 1.0 / math.sqrt(points)
    forward_tab = jnp.stack([cosine * scale, -sine * scale], 1)
    factor = jnp.where(order == 0, 1.0, 2.0).astype(jnp.float32)
    inverse_tab = jnp.stack([(cosine * factor[None, :]).T, (-sine * factor[None, :]).T], 0)
    return (forward_tab.astype(jnp.bfloat16), inverse_tab.astype(jnp.bfloat16))


def grid_angles(rows_total):
    first_row = (GRID_ROWS - rows_total) // 2
    colatitude = (jnp.arange(rows_total, dtype=jnp.float32) + (first_row + 0.5)) * (
        math.pi / GRID_ROWS
    )
    return (jnp.cos(colatitude), jnp.sin(colatitude))


def legendre_scan(orders, cosines, sine_vals, degrees):
    order_col = orders[:, None]
    cos_row = cosines[None, :]
    log_start = 0.5 * (
        jnp.log((2.0 * order_col + 1.0) / (4.0 * math.pi))
        + lax.lgamma(order_col + 0.5)
        - lax.lgamma(order_col + 1.0)
        - 0.5 * math.log(math.pi)
    ) + order_col * jnp.log(sine_vals[None, :])
    diagonal_start = jnp.exp(log_start)
    second_start = cos_row * jnp.sqrt(2.0 * order_col + 3.0) * diagonal_start
    zeros_grid = jnp.zeros_like(diagonal_start)

    def advance(state, degree):
        before, latest = state
        upper_ratio = jnp.sqrt(
            (4.0 * degree * degree - 1.0)
            / jnp.maximum(degree * degree - order_col * order_col, 1.0)
        )
        lower_ratio = jnp.sqrt(
            jnp.maximum((degree - 1.0) * (degree - 1.0) - order_col * order_col, 0.0)
            / jnp.maximum(4.0 * (degree - 1.0) * (degree - 1.0) - 1.0, 1.0)
        )
        general = upper_ratio * (cos_row * latest - lower_ratio * before)
        current = jnp.where(
            degree < order_col,
            0.0,
            jnp.where(
                degree == order_col,
                diagonal_start,
                jnp.where(degree == order_col + 1.0, second_start, general),
            ),
        )
        return ((latest, current), current)

    ignored, stacked = lax.scan(
        advance, (zeros_grid, zeros_grid), jnp.arange(degrees).astype(cosines.dtype)
    )
    stacked = jnp.transpose(stacked, (1, 0, 2))
    degree_index = jnp.arange(degrees).astype(cosines.dtype)
    keep = (orders[:, None, None] < M) & (degree_index[None, :, None] < L)
    return jnp.where(keep, stacked, 0.0)


def mix_modes(coeffs, spectral):
    product = jnp.einsum("bmlrc,lscd->bmlrsd", coeffs, spectral, preferred_element_type=jnp.float32)
    real_part = product[:, :, :, 0, 0] - product[:, :, :, 1, 1]
    imag_part = product[:, :, :, 0, 1] + product[:, :, :, 1, 0]
    return jnp.stack([real_part, imag_part], 3).astype(jnp.bfloat16)


def coeff_back(d_mixed, spectral):
    returned = jnp.einsum(
        "bmlsd,lrcd->bmlsrc", d_mixed, spectral, preferred_element_type=jnp.float32
    )
    d_real = returned[:, :, :, 0, 0] + returned[:, :, :, 1, 1]
    d_imag = returned[:, :, :, 1, 0] - returned[:, :, :, 0, 1]
    return jnp.stack([d_real, d_imag], 3).astype(jnp.bfloat16)


def weight_back(coeffs, d_mixed):
    outer_sum = jnp.einsum(
        "bmlrc,bmlsd->lrscd", coeffs, d_mixed, preferred_element_type=jnp.float32
    )
    d_weight_real = outer_sum[:, 0, 0] + outer_sum[:, 1, 1]
    d_weight_imag = outer_sum[:, 0, 1] - outer_sum[:, 1, 0]
    return jnp.stack([d_weight_real, d_weight_imag], 1)


def degree_shards(
    inputs,
    gain_one,
    shift_one,
    spectral,
    gain_two,
    shift_two,
    w_up,
    b_up,
    w_down,
    b_down,
    crops,
    cotangent,
    run_mean,
    run_var,
    momentum,
):
    lat_count = lax.axis_size("lat")
    lon_count = lax.axis_size("lon")
    rows_dev = inputs.shape[1]
    cols_dev = inputs.shape[2]
    width = inputs.shape[3]
    lat_rows = rows_dev * lat_count
    lon_cols = cols_dev * lon_count
    modes_dev = (M + lat_count - 1) // lat_count
    modes_all = modes_dev * lat_count
    quarter = width // lon_count
    owned = spectral.shape[0]
    degrees_all = owned * lat_count * lon_count
    forward_tab, inverse_tab = fourier_tables(lon_cols, modes_all)
    cosines, sine_vals = grid_angles(lat_rows)
    orders = (lax.axis_index("lat") * modes_dev + jnp.arange(modes_dev, dtype=jnp.int32)).astype(
        jnp.float32
    )
    poly = legendre_scan(orders, cosines, sine_vals, degrees_all)
    quadrature = sine_vals * (math.pi / GRID_ROWS) * (2.0 * math.pi / math.sqrt(lon_cols))
    analysis = (poly * quadrature[None, None, :]).astype(jnp.bfloat16)
    synthesis = (
        poly.astype(jnp.bfloat16)
        .reshape(modes_dev, lat_count, lon_count, owned, lat_rows)
        .transpose(0, 2, 1, 3, 4)
    )
    input_wide = inputs.astype(jnp.float32)
    normed_one, norm_one_back = jax.vjp(layer_norm, input_wide, gain_one, shift_one)
    normed_low = normed_one.astype(jnp.bfloat16)
    fourier = jnp.einsum(
        "bijc,jrm->birmc",
        lax.all_to_all(normed_low, "lon", split_axis=3, concat_axis=2, tiled=True),
        forward_tab,
        preferred_element_type=jnp.float32,
    ).astype(jnp.bfloat16)
    portion = lax.all_to_all(fourier, "lat", split_axis=3, concat_axis=1, tiled=True)
    coeffs = jnp.einsum(
        "mli,birmc->bmlrc", analysis, portion, preferred_element_type=jnp.float32
    ).astype(jnp.bfloat16)
    coeffs = coeffs.reshape(1, modes_dev, lat_count, lon_count, owned, 2, portion.shape[4])
    owned_coeffs = lax.all_to_all(
        lax.all_to_all(coeffs, "lat", split_axis=2, concat_axis=1, tiled=True),
        "lon",
        split_axis=3,
        concat_axis=6,
        tiled=True,
    )
    coeffs_owned = owned_coeffs.reshape(1, modes_all, owned, 2, width)
    mixed_modes = mix_modes(coeffs_owned, spectral).reshape(1, modes_all, 1, 1, owned, 2, width)
    returned = lax.all_to_all(
        lax.all_to_all(mixed_modes, "lat", split_axis=1, concat_axis=3, tiled=True),
        "lon",
        split_axis=6,
        concat_axis=2,
        tiled=True,
    )
    grid_modes = jnp.einsum(
        "mjkqi,bmjkqrc->birmc", synthesis, returned, preferred_element_type=jnp.float32
    ).astype(jnp.bfloat16)
    spread = jnp.einsum(
        "birmc,rmj->bijc",
        lax.all_to_all(grid_modes, "lat", split_axis=1, concat_axis=3, tiled=True),
        inverse_tab,
        preferred_element_type=jnp.float32,
    ).astype(jnp.bfloat16)
    spectral_out = lax.all_to_all(spread, "lon", split_axis=2, concat_axis=3, tiled=True)
    skipped = input_wide + spectral_out.astype(jnp.float32)
    normed_two, norm_two_back = jax.vjp(layer_norm, skipped, gain_two, shift_two)
    normed_two_low = normed_two.astype(jnp.bfloat16)
    preact = (
        jnp.einsum("bijc,ch->bijh", normed_two_low, w_up, preferred_element_type=jnp.float32) + b_up
    )
    activated, gelu_back = jax.vjp(jax.nn.gelu, preact)
    activated_low = activated.astype(jnp.bfloat16)
    result = (
        skipped
        + jnp.einsum("bijh,hc->bijc", activated_low, w_down, preferred_element_type=jnp.float32)
        + b_down
    )
    output = result.astype(jnp.bfloat16)
    bounds = crops[0]
    row_global = lax.axis_index("lat") * rows_dev + jnp.arange(rows_dev, dtype=jnp.int32)
    col_global = lax.axis_index("lon") * cols_dev + jnp.arange(cols_dev, dtype=jnp.int32)
    inside_rows = (row_global >= bounds[0]) & (row_global < bounds[1])
    inside_cols = (col_global >= bounds[2]) & (col_global < bounds[3])
    mask_grid = (inside_rows[:, None] & inside_cols[None, :]).astype(jnp.float32)[None, :, :, None]
    valid_count = jnp.sum(mask_grid)
    first_moment = jnp.sum(mask_grid * result, (0, 1, 2))
    second_moment = jnp.sum(mask_grid * result * result, (0, 1, 2))
    grad_wide = cotangent.astype(jnp.float32)
    d_down = jnp.einsum(
        "bijh,bijc->hc", activated_low, cotangent, preferred_element_type=jnp.float32
    )
    d_down_bias = jnp.sum(grad_wide, (0, 1, 2))
    d_activated = jnp.einsum("bijc,hc->bijh", cotangent, w_down, preferred_element_type=jnp.float32)
    d_preact = gelu_back(d_activated)[0].astype(jnp.bfloat16)
    d_up = jnp.einsum("bijc,bijh->ch", normed_two_low, d_preact, preferred_element_type=jnp.float32)
    d_up_bias = jnp.sum(d_preact.astype(jnp.float32), (0, 1, 2))
    d_normed_two = jnp.einsum("bijh,ch->bijc", d_preact, w_up, preferred_element_type=jnp.float32)
    d_skipped, d_gain_two, d_shift_two = norm_two_back(d_normed_two)
    d_skipped = d_skipped + grad_wide
    d_spread = d_skipped.astype(jnp.bfloat16)
    d_grid = jnp.einsum(
        "bijc,rmj->birmc",
        lax.all_to_all(d_spread, "lon", split_axis=3, concat_axis=2, tiled=True),
        inverse_tab,
        preferred_element_type=jnp.float32,
    ).astype(jnp.bfloat16)
    d_returned = jnp.einsum(
        "mjkqi,birmc->bmjkqrc",
        synthesis,
        lax.all_to_all(d_grid, "lat", split_axis=3, concat_axis=1, tiled=True),
        preferred_element_type=jnp.float32,
    ).astype(jnp.bfloat16)
    d_mixed = lax.all_to_all(
        lax.all_to_all(d_returned, "lat", split_axis=3, concat_axis=1, tiled=True),
        "lon",
        split_axis=2,
        concat_axis=6,
        tiled=True,
    ).reshape(1, modes_all, owned, 2, width)
    d_coeffs = coeff_back(d_mixed, spectral)
    d_spectral = lax.psum(weight_back(coeffs_owned, d_mixed).astype(jnp.bfloat16), "batch").astype(
        jnp.float32
    )
    d_coeffs_wide = d_coeffs.reshape(1, modes_all, 1, 1, owned, 2, width)
    d_modes = lax.all_to_all(
        lax.all_to_all(d_coeffs_wide, "lat", split_axis=1, concat_axis=2, tiled=True),
        "lon",
        split_axis=6,
        concat_axis=3,
        tiled=True,
    ).reshape(1, modes_dev, degrees_all, 2, quarter)
    d_fourier = jnp.einsum(
        "mli,bmlrc->birmc", analysis, d_modes, preferred_element_type=jnp.float32
    ).astype(jnp.bfloat16)
    d_columns = jnp.einsum(
        "birmc,jrm->bijc",
        lax.all_to_all(d_fourier, "lat", split_axis=1, concat_axis=3, tiled=True),
        forward_tab,
        preferred_element_type=jnp.float32,
    ).astype(jnp.bfloat16)
    d_normed_one = lax.all_to_all(d_columns, "lon", split_axis=2, concat_axis=3, tiled=True).astype(
        jnp.float32
    )
    d_input_norm, d_gain_one, d_shift_one = norm_one_back(d_normed_one)
    d_inputs = d_input_norm + d_skipped
    summed = lax.psum(
        (
            d_up,
            d_down,
            d_up_bias,
            d_down_bias,
            d_gain_one,
            d_shift_one,
            d_gain_two,
            d_shift_two,
            valid_count,
            first_moment,
            second_moment,
        ),
        ("lat", "lon", "batch"),
    )
    batch_mean = summed[9] / summed[8]
    batch_var = summed[10] / summed[8] - batch_mean * batch_mean
    new_mean = (1.0 - momentum) * run_mean + momentum * batch_mean
    new_var = (1.0 - momentum) * run_var + momentum * batch_var
    return (
        output,
        d_inputs,
        summed[4],
        summed[5],
        d_spectral,
        summed[6],
        summed[7],
        summed[0],
        summed[2],
        summed[1],
        summed[3],
        new_mean,
        new_var,
    )


def shards(inputs, *rest):
    rows_dev = inputs.shape[1]
    lon_count = lax.axis_size("lon")
    banded = (
        lon_count == 4
        and lax.axis_size("batch") == 2
        and rows_dev % lon_count == 0
        and M % lon_count == 0
        and M // lon_count <= 128
        and rows_dev * lax.axis_size("lat") <= 32
    )
    return (band_shards if banded else degree_shards)(inputs, *rest)


def solution(mesh):
    return jax.shard_map(
        shards,
        mesh=mesh,
        in_specs=(
            P("batch", "lat", "lon", None),
            P(),
            P(),
            P(("lat", "lon"), None, None, None),
            P(),
            P(),
            P(),
            P(),
            P(),
            P(),
            P("batch", None),
            P("batch", "lat", "lon", None),
            P(),
            P(),
            P(),
        ),
        out_specs=(
            P("batch", "lat", "lon", None),
            P("batch", "lat", "lon", None),
            P(),
            P(),
            P(("lat", "lon"), None, None, None),
            P(),
            P(),
            P(),
            P(),
            P(),
            P(),
            P(),
            P(),
        ),
        check_vma=False,
    )
```

```python
import math

import jax
import jax.numpy as jnp
from jax import lax
from jax.experimental import pallas as pl
from jax.experimental.pallas import tpu as pltpu
from jax.sharding import PartitionSpec as P

GRID_ROWS = 360
M = 360
L = 360


epsilon = 1e-05
GROUP = 16
CHUNKS = 2


def layer_norm(values, gain, shift):
    centre = values - jnp.mean(values, -1, keepdims=True)
    spread = jnp.mean(centre * centre, -1, keepdims=True)
    return centre * lax.rsqrt(spread + epsilon) * gain + shift


def xor_pairs(count, bit):
    return [(i, i ^ bit) for i in range(count)]


def ring_pairs(count, step):
    return [(i, (i + step) % count) for i in range(count)]


def swap_cores(values):
    return lax.ppermute(values, "batch", xor_pairs(2, 1))


def near(values):
    return lax.ppermute(values, "lon", xor_pairs(4, 1))


def far(values):
    return lax.ppermute(values, "lon", xor_pairs(4, 2))


def after(values, earlier):
    return lax.optimization_barrier((values, earlier))[0]


def trade(values):
    return lax.all_to_all(values, "lon", split_axis=0, concat_axis=0, tiled=True)


def sum_everywhere(values):
    values = values + swap_cores(values)
    for name, shift in (("lon", lambda at, k: at ^ k), ("lat", lambda at, k: (at - k) % lax.axis_size("lat"))):
        count = lax.axis_size(name)
        pairs = xor_pairs if name == "lon" else ring_pairs
        pieces = jnp.stack([values] + [lax.ppermute(values, name, pairs(count, k)) for k in range(1, count)], 0)
        at = lax.axis_index(name)
        values = lax.dynamic_index_in_dim(pieces, shift(at, 0), 0, keepdims=False)
        for place in range(1, count):
            values = values + lax.dynamic_index_in_dim(pieces, shift(at, place), 0, keepdims=False)
    return values


def dot(a, b):
    return jnp.dot(a, b, preferred_element_type=jnp.float32)


def dot_along(a, b):
    return lax.dot_general(a, b, (((1,), (1,)), ((), ())), preferred_element_type=jnp.float32)


def dot_across(a, b):
    return lax.dot_general(a, b, (((0,), (0,)), ((), ())), preferred_element_type=jnp.float32)


def low(values):
    return values.astype(jnp.bfloat16)


def wide(values):
    return values.astype(jnp.float32)


def cost(microseconds):
    return pl.CostEstimate(flops=0, transcendentals=0, bytes_accessed=0)


def params(megabytes):
    return pltpu.CompilerParams(vmem_limit_bytes=megabytes * 2**20)


def turned(cosine, sine, quarter_turns):
    turns = quarter_turns % 4
    real = jnp.where(turns == 0, cosine, jnp.where(turns == 1, -sine, jnp.where(turns == 2, -cosine, sine)))
    imag = jnp.where(turns == 0, -sine, jnp.where(turns == 1, -cosine, jnp.where(turns == 2, sine, cosine)))
    return real, imag


def dft_tables(points, parts, order, valid, axis):
    cols = points // parts
    column = jnp.arange(cols, dtype=jnp.int32)
    if axis == 1:
        order, valid, column = order[:, None], valid[:, None], column[None, :]
    else:
        order, valid, column = order[None, :], valid[None, :], column[:, None]
    angle = (order * column % points).astype(jnp.float32) * (2.0 * math.pi / points)
    cosine = jnp.where(valid, jnp.cos(angle), 0.0)
    sine = jnp.where(valid, jnp.sin(angle), 0.0)
    cosine, sine = lax.optimization_barrier((cosine, sine))
    part = jnp.arange(parts, dtype=jnp.int32)[:, None, None]
    real, imag = turned(cosine[None], sine[None], part * order[None])
    scales = (1.0 / math.sqrt(points), jnp.where(order == 0, 1.0, 2.0)[None])
    return [jnp.concatenate([low(real * scale), low(imag * scale)], axis) for scale in scales]


def legendre_kernel(cut, starts_ref, upper_ref, lower_ref, order_ref, cos_ref, diag_ref, second_ref, out_ref, all_ref):
    degrees = all_ref.shape[0]
    cosines = cos_ref[...]
    diagonal = diag_ref[...]
    second = second_ref[...]
    order = order_ref[...]

    def advance(degree, state):
        before, latest = state
        level = degree.astype(jnp.float32)
        upper = upper_ref[pl.ds(degree, 1), :]
        lower = lower_ref[pl.ds(degree, 1), :]
        general = upper * (cosines * latest - lower * before)
        current = jnp.where(
            level < order,
            0.0,
            jnp.where(level == order, diagonal, jnp.where(level == order + 1.0, second, general)),
        )
        all_ref[pl.ds(degree, 1)] = current[None]
        return latest, current

    unroll = 8 if degrees % 8 == 0 else 1

    def several(step, state):
        for at in range(unroll):
            state = advance(step * unroll + at, state)
        return state

    zeros = cosines * 0.0
    lax.fori_loop(0, degrees // unroll, several, (zeros, zeros))
    blocks = out_ref.shape[0] // (2 * cut)
    for block in range(blocks):
        for half in range(2):

            def copy(at, carry, block=block, half=half):
                degree = starts_ref[block] + half * cut + at
                value = all_ref[pl.ds(degree, 1)]
                keep = (degree < L) & (half * cut + at >= starts_ref[blocks])
                out_ref[pl.ds((at * 2 + half) * blocks + block, 1)] = jnp.where(keep, value, 0.0)
                return carry

            lax.fori_loop(0, cut, copy, 0)


def legendre(starts, skip, orders, valid, cosines, sine_vals, degrees, cut):
    order_row = orders[None, :]
    sine_col = sine_vals[:, None]
    log_start = 0.5 * (
        jnp.log((2.0 * order_row + 1.0) / (4.0 * math.pi))
        + lax.lgamma(order_row + 0.5)
        - lax.lgamma(order_row + 1.0)
        - 0.5 * math.log(math.pi)
    ) + order_row * jnp.log(sine_col)
    diagonal = jnp.where(valid[None, :], jnp.exp(log_start), 0.0)
    second = cosines[:, None] * jnp.sqrt(2.0 * order_row + 3.0) * diagonal
    degree = jnp.arange(degrees, dtype=jnp.float32)[:, None]
    upper = jnp.sqrt((4.0 * degree * degree - 1.0) / jnp.maximum(degree * degree - order_row * order_row, 1.0))
    lower = jnp.sqrt(
        jnp.maximum((degree - 1.0) * (degree - 1.0) - order_row * order_row, 0.0)
        / jnp.maximum(4.0 * (degree - 1.0) * (degree - 1.0) - 1.0, 1.0)
    )
    shape = diagonal.shape
    return pl.pallas_call(
        lambda *refs: legendre_kernel(cut, *refs),
        out_shape=jax.ShapeDtypeStruct((starts.shape[0] * 2 * cut,) + shape, jnp.float32),
        in_specs=[pl.BlockSpec(memory_space=pltpu.SMEM)] + [pl.BlockSpec(memory_space=pltpu.VMEM)] * 6,
        out_specs=pl.BlockSpec(memory_space=pltpu.VMEM),
        scratch_shapes=[pltpu.VMEM((degrees,) + shape, jnp.float32)],
        cost_estimate=cost(4),
        compiler_params=params(24),
        name="legendre",
    )(
        jnp.concatenate([starts, skip[None]]).astype(jnp.int32),
        upper,
        lower,
        jnp.broadcast_to(order_row, shape),
        jnp.broadcast_to(cosines[:, None], shape),
        diagonal,
        second,
    )


def block_tables(poly, slots):
    degrees, rows, _ = poly.shape
    groups = slots // GROUP
    values = low(poly[:, :, :slots]).reshape(degrees, rows, groups, GROUP)

    def expand(table, depth):
        lanes = depth * GROUP
        lane = jnp.arange(lanes, dtype=jnp.int32)
        repeat = low(jnp.arange(depth, dtype=jnp.int32)[:, None] == lane[None, :] // GROUP)
        flat = table.reshape(-1, depth)
        row = jnp.arange(flat.shape[0], dtype=jnp.int32)
        same = row[:, None] % GROUP == lane[None, :] % GROUP
        return low(jnp.where(same, dot(flat, repeat), 0.0)).reshape(groups, -1, lanes)

    return expand(values.transpose(2, 0, 3, 1), rows), expand(values.transpose(2, 1, 3, 0), degrees)


def normalise(values):
    centre = values - jnp.mean(values, -1, keepdims=True)
    factor = lax.rsqrt(jnp.mean(centre * centre, -1, keepdims=True) + epsilon)
    return centre * factor, factor


def normalise_back(normal, factor, grad):
    return factor * (
        grad - jnp.mean(grad, -1, keepdims=True) - normal * jnp.mean(grad * normal, -1, keepdims=True)
    )


def column_sum(values):
    return jnp.sum(values, 0, keepdims=True)


def store_modes(total, refs, factor=None):
    owners, _, slots, double = refs[0].shape
    width = double // 2
    half = total.shape[0] // 2
    if factor is not None:
        total = total * factor
    total = low(total)
    for chunk, ref in enumerate(refs):
        for owner in range(owners):
            at = (chunk * owners + owner) * slots
            ref[owner, 0, :, :width] = total[at : at + slots]
            ref[owner, 0, :, width:] = total[half + at : half + at + slots]


def load_modes(refs, flat_ref):
    owners, _, slots, double = refs[0].shape
    width = double // 2
    half = flat_ref.shape[0] // 2
    for chunk, ref in enumerate(refs):
        for owner in range(owners):
            at = (chunk * owners + owner) * slots
            flat_ref[at : at + slots] = ref[owner, 0, :, :width]
            flat_ref[half + at : half + at + slots] = ref[owner, 0, :, width:]


def modes_spec(parts, slots, double):
    return pl.BlockSpec((parts, 1, slots, double), lambda i, *p: (0, i, 0, 0))


def enter_kernel(weight_ref, table_ref, values_ref, gain_ref, shift_ref, *out_refs):
    parts = table_ref.shape[0]
    total = 0.0
    for part in range(parts):
        normal, _ = normalise(wide(values_ref[part, 0]))
        total += dot(table_ref[part], low(normal * gain_ref[...] + shift_ref[...]))
    store_modes(total, out_refs, weight_ref[pl.program_id(0)])


def enter(weight, table, values, gain, shift, slots, chunks):
    parts, rows, cols, width = values.shape
    vector = pl.BlockSpec((1, width), lambda i: (0, 0))
    return pl.pallas_call(
        enter_kernel,
        grid=(rows,),
        out_shape=[jax.ShapeDtypeStruct((parts, rows, slots, 2 * width), jnp.bfloat16)] * chunks,
        in_specs=[
            pl.BlockSpec(memory_space=pltpu.SMEM),
            pl.BlockSpec(table.shape, lambda i: (0, 0, 0)),
            pl.BlockSpec((parts, 1, cols, width), lambda i: (0, i, 0, 0)),
            vector,
            vector,
        ],
        out_specs=[modes_spec(parts, slots, 2 * width)] * chunks,
        cost_estimate=cost(4),
        compiler_params=params(32),
        name="enter",
    )(weight, table, values, gain[None], shift[None])


def gelu_parts(values):
    slope = math.sqrt(2.0 / math.pi)
    square = values * values
    tangent = jnp.tanh(slope * values * (1.0 + 0.044715 * square))
    half = 0.5 * (1.0 + tangent)
    grad = half + 0.5 * values * (1.0 - tangent * tangent) * slope * (1.0 + 3.0 * 0.044715 * square)
    return values * half, grad


def feed_kernel(chunks, where_ref, *refs):
    modes_refs, refs = refs[:chunks], refs[chunks:]
    (columns_ref, modes_table_ref, values_ref, cotangent_ref), refs = refs[:4], refs[4:]
    (gain_ref, shift_ref, up_ref, up_bias_ref, down_ref, down_bias_ref), refs = refs[:6], refs[6:]
    grid_refs, refs = refs[:chunks], refs[chunks:]
    output_ref, d_skipped_ref, sums_ref, flat_ref, total_ref = refs
    row, part = pl.program_id(0), pl.program_id(1)
    width = values_ref.shape[-1]
    cols = values_ref.shape[-2]
    hidden = up_ref.shape[-1]

    @pl.when(part == 0)
    def _():
        load_modes(modes_refs, flat_ref)

    @pl.when((part == 0) & (row == 0))
    def _():
        sums_ref[...] = jnp.zeros_like(sums_ref)

    spread = low(dot(columns_ref[0], flat_ref[...]))
    skipped = wide(values_ref[0, 0]) + wide(spread)
    normal, factor = normalise(skipped)
    normed = low(normal * gain_ref[...] + shift_ref[...])
    activated, slope = gelu_parts(dot(normed, up_ref[...]) + up_bias_ref[...])
    activated = low(activated)
    result = skipped + dot(activated, down_ref[...]) + down_bias_ref[...]
    output_ref[0, 0] = low(result)
    row_at = where_ref[4] + row
    column_at = where_ref[5] + part * cols + lax.broadcasted_iota(jnp.int32, (cols, 1), 0)
    inside = (column_at >= where_ref[2]) & (column_at < where_ref[3])
    inside = inside & (row_at >= where_ref[0]) & (row_at < where_ref[1])
    kept = jnp.where(inside, result, 0.0)

    cotangent = cotangent_ref[0, 0]
    d_preact = low(dot_along(cotangent, down_ref[...]) * slope)
    d_normed = dot_along(d_preact, up_ref[...])
    d_skipped = wide(cotangent) + normalise_back(normal, factor, d_normed * gain_ref[...])
    d_skipped_ref[0, 0] = d_skipped
    term = dot(modes_table_ref[0], low(d_skipped))

    @pl.when(part == 0)
    def _():
        total_ref[...] = term

    @pl.when(part > 0)
    def _():
        total_ref[...] += term

    @pl.when(part == pl.num_programs(1) - 1)
    def _():
        store_modes(total_ref[...], grid_refs)

    d_up = dot_across(normed, d_preact)
    for at in range(hidden // width):
        sums_ref[at * width : at * width + width] += d_up[:, at * width : at * width + width]
    sums_ref[hidden : 2 * hidden] += dot_across(activated, cotangent)
    at = 2 * hidden
    d_bias = column_sum(wide(d_preact))
    vectors = [d_bias[:, j * width : j * width + width] for j in range(hidden // width)] + [
        column_sum(wide(cotangent)),
        column_sum(d_normed * normal),
        column_sum(d_normed),
        column_sum(kept),
        column_sum(kept * kept),
    ]
    for j, vector in enumerate(vectors):
        sums_ref[at + j : at + j + 1] += vector


def feed(where, modes, columns, modes_table, values, cotangent, gain, shift, w_up, b_up, w_down, b_down):
    parts, rows, cols, width = values.shape
    chunks = len(modes)
    slots = modes[0].shape[2]
    hidden = w_up.shape[1]
    lanes = modes_table.shape[1]
    cells = pl.BlockSpec((1, 1, cols, width), lambda i, p: (p, i, 0, 0))
    grid = modes_spec(parts, slots, 2 * width)
    whole = lambda shape: pl.BlockSpec(shape, lambda i, p: (0,) * len(shape))
    sums = ((2 * hidden + hidden // width + 5 + 63) // 64 * 64, width)
    out = pl.pallas_call(
        lambda *refs: feed_kernel(chunks, *refs),
        grid=(rows, parts),
        out_shape=[jax.ShapeDtypeStruct(m.shape, jnp.bfloat16) for m in modes]
        + [
            jax.ShapeDtypeStruct(values.shape, jnp.bfloat16),
            jax.ShapeDtypeStruct(values.shape, jnp.float32),
            jax.ShapeDtypeStruct(sums, jnp.float32),
        ],
        in_specs=[pl.BlockSpec(memory_space=pltpu.SMEM)]
        + [grid] * chunks
        + [
            pl.BlockSpec((1,) + columns.shape[1:], lambda i, p: (p, 0, 0)),
            pl.BlockSpec((1,) + modes_table.shape[1:], lambda i, p: (p, 0, 0)),
            cells,
            cells,
            whole((1, width)),
            whole((1, width)),
            whole(w_up.shape),
            whole((1, hidden)),
            whole(w_down.shape),
            whole((1, width)),
        ],
        out_specs=[grid] * chunks + [cells, cells, whole(sums)],
        scratch_shapes=[pltpu.VMEM((lanes, width), jnp.bfloat16), pltpu.VMEM((lanes, width), jnp.float32)],
        cost_estimate=cost(18),
        compiler_params=params(60),
        name="feed",
    )(
        where,
        *modes,
        columns,
        modes_table,
        values,
        cotangent,
        gain[None],
        shift[None],
        w_up,
        b_up[None],
        w_down,
        b_down[None],
    )
    return out[:chunks], out[chunks], out[chunks + 1], out[chunks + 2]


def leave_kernel(chunks, weight_ref, *refs):
    modes_refs, refs = refs[:chunks], refs[chunks:]
    columns_ref, values_ref, d_skipped_ref, gain_ref, out_ref, sums_ref, flat_ref = refs
    row, part = pl.program_id(0), pl.program_id(1)

    @pl.when(part == 0)
    def _():
        load_modes(modes_refs, flat_ref)

    @pl.when((part == 0) & (row == 0))
    def _():
        sums_ref[...] = jnp.zeros_like(sums_ref)

    d_normed = wide(low(dot(columns_ref[0], flat_ref[...]) * weight_ref[row]))
    normal, factor = normalise(wide(values_ref[0, 0]))
    out_ref[0, 0] = low(normalise_back(normal, factor, d_normed * gain_ref[...]) + d_skipped_ref[0, 0])
    sums_ref[0:1] += column_sum(d_normed * normal)
    sums_ref[1:2] += column_sum(d_normed)


def leave(weight, modes, columns, values, d_skipped, gain):
    parts, rows, cols, width = values.shape
    chunks = len(modes)
    cells = pl.BlockSpec((1, 1, cols, width), lambda i, p: (p, i, 0, 0))
    return pl.pallas_call(
        lambda *refs: leave_kernel(chunks, *refs),
        grid=(rows, parts),
        out_shape=[jax.ShapeDtypeStruct(values.shape, jnp.bfloat16), jax.ShapeDtypeStruct((8, width), jnp.float32)],
        in_specs=[pl.BlockSpec(memory_space=pltpu.SMEM)]
        + [modes_spec(parts, modes[0].shape[2], 2 * width)] * chunks
        + [
            pl.BlockSpec((1,) + columns.shape[1:], lambda i, p: (p, 0, 0)),
            cells,
            cells,
            pl.BlockSpec((1, width), lambda i, p: (0, 0)),
        ],
        out_specs=[cells, pl.BlockSpec((8, width), lambda i, p: (0, 0))],
        scratch_shapes=[pltpu.VMEM((columns.shape[2], width), jnp.bfloat16)],
        cost_estimate=cost(5),
        compiler_params=params(32),
        name="leave",
    )(weight, *modes, columns, values, d_skipped, gain[None])


def analyse_kernel(table_ref, *refs):
    out_ref = refs[-1]
    per = (len(refs) - 1) // 2
    for sample in range(2):
        rows = [ref[...].reshape(-1, ref.shape[-1]) for ref in refs[sample * per : sample * per + per]]
        total = dot(table_ref[0], jnp.concatenate(rows, 0))
        out_ref[:, sample] = low(total).reshape(-1, GROUP, total.shape[-1])


def analyse(table, chunk, own, other):
    rows, slots, double = own[0].shape
    groups = slots // GROUP
    degrees = table.shape[1] // GROUP
    shard = pl.BlockSpec((rows, GROUP, double), lambda g: (0, g, 0))
    return pl.pallas_call(
        analyse_kernel,
        grid=(groups,),
        out_shape=jax.ShapeDtypeStruct((degrees, 2, slots, double), jnp.bfloat16),
        in_specs=[pl.BlockSpec((1,) + table.shape[1:], lambda g: (chunk * groups + g, 0, 0))]
        + [shard] * (len(own) + len(other)),
        out_specs=pl.BlockSpec((degrees, 2, GROUP, double), lambda g: (0, 0, g, 0)),
        cost_estimate=cost(6),
        compiler_params=params(60),
        name="analyse",
    )(table, *own, *other)


def synthesise_kernel(table_ref, modes_ref, *out_refs):
    for sample, ref in enumerate(out_refs):
        modes = modes_ref[:, sample]
        total = low(dot(table_ref[0], modes.reshape(-1, modes.shape[-1])))
        ref[...] = total.reshape(ref.shape)


def synthesise(table, chunk, modes, parts):
    degrees, _, slots, double = modes.shape
    groups = slots // GROUP
    rows = table.shape[1] // GROUP // parts
    shard = pl.BlockSpec((parts, rows, GROUP, double), lambda g: (0, 0, g, 0))
    return pl.pallas_call(
        synthesise_kernel,
        grid=(groups,),
        out_shape=[jax.ShapeDtypeStruct((parts, rows, slots, double), jnp.bfloat16)] * 2,
        in_specs=[
            pl.BlockSpec((1,) + table.shape[1:], lambda g: (chunk * groups + g, 0, 0)),
            pl.BlockSpec((degrees, 2, GROUP, double), lambda g: (0, 0, g, 0)),
        ],
        out_specs=[shard] * 2,
        cost_estimate=cost(6),
        compiler_params=params(60),
        name="synthesise",
    )(table, modes)


def complex_weight(weight_ref):
    real, imag = weight_ref[0, 0], weight_ref[0, 1]
    return jnp.concatenate([jnp.concatenate([real, imag], 1), jnp.concatenate([-imag, real], 1)], 0)


def degree_rows(refs, degree):
    return jnp.concatenate([ref[degree].reshape(-1, ref.shape[-1]) for ref in refs], 0)


def split_rows(total, refs, degree):
    at = 0
    for ref in refs:
        count = ref.shape[1] * ref.shape[2]
        ref[degree] = total[at : at + count].reshape(ref.shape[1:])
        at += count


def mix_kernel(chunks, *refs):
    modes_refs, weights, out_refs = refs[:chunks], refs[chunks:-chunks], refs[-chunks:]
    for degree, weight_ref in enumerate(weights):
        split_rows(low(dot(degree_rows(modes_refs, degree), complex_weight(weight_ref))), out_refs, degree)


def degree_spec(modes, per):
    return pl.BlockSpec((per,) + modes.shape[1:], lambda t: (t, 0, 0, 0))


def weight_spec(weight):
    return pl.BlockSpec((1,) + weight.shape[1:], lambda t: (t, 0, 0, 0))


def mix(modes, weights, cut):
    specs = [degree_spec(m, len(weights)) for m in modes]
    return pl.pallas_call(
        lambda *refs: mix_kernel(len(modes), *refs),
        grid=(cut,),
        out_shape=[jax.ShapeDtypeStruct(m.shape, jnp.bfloat16) for m in modes],
        in_specs=specs + [weight_spec(weight) for weight in weights],
        out_specs=specs,
        cost_estimate=cost(13),
        compiler_params=params(60),
        name="mix",
    )(*modes, *weights)


def mix_back_kernel(chunks, *refs):
    coeffs_refs, modes_refs, refs = refs[:chunks], refs[chunks : 2 * chunks], refs[2 * chunks :]
    weights, out_refs, targets = refs[: -chunks - 6], refs[-chunks - 6 : -6], refs[-6:]
    first, first_two, last, last_one, near_first, far_last = targets
    targets = [
        first.at[0],
        near_first.at[1, 0],
        first_two.at[0],
        near_first.at[0, 0],
        last.at[0],
        last_one.at[0],
        far_last.at[1, 0],
        far_last.at[0, 0],
    ]
    for degree, (weight_ref, ref) in enumerate(zip(weights, targets)):
        d_mixed = degree_rows(modes_refs, degree)
        split_rows(low(dot_along(d_mixed, complex_weight(weight_ref))), out_refs, degree)
        width = ref.shape[-1]
        total = dot_across(degree_rows(coeffs_refs, degree), d_mixed)
        ref[0] = low(total[:width, :width] + total[width:, width:])
        ref[1] = low(total[:width, width:] - total[width:, :width])


def mix_back(coeffs, d_mixed, weights, cut):
    chunks = len(coeffs)
    width = coeffs[0].shape[-1] // 2
    shape = (cut, 2, width, width)
    specs = [degree_spec(m, len(weights)) for m in coeffs]
    out = pl.pallas_call(
        lambda *refs: mix_back_kernel(chunks, *refs),
        grid=(cut,),
        out_shape=[jax.ShapeDtypeStruct(m.shape, jnp.bfloat16) for m in coeffs]
        + [jax.ShapeDtypeStruct(shape, jnp.bfloat16)] * 4
        + [jax.ShapeDtypeStruct((2,) + shape, jnp.bfloat16)] * 2,
        in_specs=specs + specs + [weight_spec(weight) for weight in weights],
        out_specs=specs
        + [pl.BlockSpec((1,) + shape[1:], lambda t: (t, 0, 0, 0))] * 4
        + [pl.BlockSpec((2, 1) + shape[1:], lambda t: (0, t, 0, 0, 0))] * 2,
        cost_estimate=cost(20),
        compiler_params=params(60),
        name="mix_back",
    )(*coeffs, *d_mixed, *weights)
    return list(out[:chunks]), out[chunks : chunks + 4], out[-2], out[-1]


def gather_rows(shards, gate):
    count = lax.axis_size("lat")
    own = [[shard] for shard in shards]
    for step in range(1, count):
        earlier = gate(step, own)
        sent = [rows[-1] for rows in own]
        if earlier is not None:
            sent = after(sent, earlier)
        own = [rows + [lax.ppermute(rows_sent, "lat", ring_pairs(count, 1))] for rows, rows_sent in zip(own, sent)]
    return [(rows, [swap_cores(slot) for slot in rows]) for rows in own]


def scatter_rows(own, other, gate=None, last_gate=None):
    count = lax.axis_size("lat")
    other = swap_cores(other)
    arrived = None
    for slot in range(count - 1, -1, -1):
        total = wide(own[slot]) + wide(other[slot])
        if arrived is not None:
            total = total + wide(arrived)
        total = low(total)
        if slot == 1:
            midway = total
        if slot > 0:
            arrived = lax.ppermute(total, "lat", ring_pairs(count, -1))
            if slot == 3 and gate is not None:
                arrived = after(arrived, gate)
            if slot == 2 and last_gate is not None:
                arrived = after(arrived, last_gate)
    return total, midway


def gather_weights(own):
    cut = own.shape[0] // 2
    first, last = own[:cut], own[cut:]
    return first, last, near(first), far(last)


def scatter_weights(near_first, far_last):
    return near(near_first), far(far_last)


def finish_weight_sum(parts, one, two, later):
    first, first_two, last, last_one = parts
    from_two = far(low(wide(first_two) + wide(one[0])))
    from_one = near(low(wide(last_one) + wide(two[0])))
    from_two, from_one = after((from_two, from_one), later)
    return jnp.concatenate(
        [low(wide(first) + wide(one[1]) + wide(from_two)), low(wide(last) + wide(two[1]) + wide(from_one))], 0
    )


class PartSum:
    def __init__(self, values):
        core = lax.axis_index("batch")
        half = values.shape[0] // 2
        self.mine = lax.dynamic_slice_in_dim(values, core * half, half, 0)
        self.other = swap_cores(lax.dynamic_slice_in_dim(values, (1 - core) * half, half, 0))

    def cores(self):
        return self.mine + self.other

    def cross(self, value, k):
        return lax.ppermute(value, "lon", xor_pairs(4, k))

    def chips(self, values):
        chip = lax.axis_index("lon")
        part = values.shape[0] // 4
        for_chip = lambda k: lax.dynamic_slice_in_dim(values, (chip ^ k) * part, part, 0)
        return for_chip(0) + self.cross(for_chip(1), 1) + self.cross(for_chip(2), 2) + self.cross(for_chip(3), 3)

    def planes(self, total, bit, gate):
        if bit >= lax.axis_size("lat"):
            return total
        return total + after(lax.ppermute(total, "lat", xor_pairs(lax.axis_size("lat"), bit)), gate)

    def share(self, total, gate):
        chip = lax.axis_index("lon")
        pieces = jnp.stack([total] + after([self.cross(total, k) for k in (1, 2, 3)], gate), 0)
        return jnp.concatenate(
            [lax.dynamic_index_in_dim(pieces, chip ^ k, 0, keepdims=False) for k in range(4)], 0
        )

    def finish(self, mine, other):
        core = lax.axis_index("batch")
        return jnp.concatenate([jnp.where(core == 0, mine, other), jnp.where(core == 0, other, mine)], 0)


def band_shards(
    inputs,
    gain_one,
    shift_one,
    spectral,
    gain_two,
    shift_two,
    w_up,
    b_up,
    w_down,
    b_down,
    crops,
    cotangent,
    run_mean,
    run_var,
    momentum,
):
    lat_count = lax.axis_size("lat")
    lon_count = lax.axis_size("lon")
    plane = lax.axis_index("lat")
    chip = lax.axis_index("lon")
    core = lax.axis_index("batch")
    rows_dev = inputs.shape[1]
    cols_dev = inputs.shape[2]
    width = inputs.shape[3]
    rows_chip = rows_dev // lon_count
    lat_rows = rows_dev * lat_count
    lon_cols = cols_dev * lon_count
    modes_dev = M // lon_count
    slots = (modes_dev + CHUNKS * GROUP - 1) // (CHUNKS * GROUP) * GROUP
    owned = spectral.shape[0]
    cut = (owned + 3) // 4
    half = 2 * cut
    first_degree = core * (owned - half)
    skip = core * (2 * half - owned)
    by_row = (lon_count, rows_chip, cols_dev, width)
    by_chip = (lon_count, rows_chip, slots, 2 * width)

    own_weights = lax.dynamic_slice_in_dim(spectral, first_degree, half, 0)
    first_hop = gather_weights(own_weights)
    values = trade(inputs.reshape(by_row))

    at = jnp.arange(CHUNKS * lon_count * slots, dtype=jnp.int32)
    in_chip = at // (lon_count * slots) * slots + at % slots
    valid = in_chip < modes_dev
    order = jnp.where(valid, at // slots % lon_count * modes_dev + in_chip, 0)
    to_modes, to_modes_back = dft_tables(lon_cols, lon_count, order, valid, 1)
    to_columns_back, to_columns = dft_tables(lon_cols, lon_count, order, valid, 2)
    first_row = (GRID_ROWS - lat_rows) // 2
    slot_plane = (plane - jnp.arange(lat_count, dtype=jnp.int32)) % lat_count
    row = (slot_plane[:, None] * rows_dev + jnp.arange(rows_dev, dtype=jnp.int32)[None, :]).reshape(-1)
    colatitude = (row.astype(jnp.float32) + (first_row + 0.5)) * (math.pi / GRID_ROWS)
    lane = jnp.arange(128, dtype=jnp.int32)
    orders = (chip * modes_dev + jnp.minimum(lane, modes_dev - 1)).astype(jnp.float32)
    owners = plane * lon_count + (chip ^ jnp.arange(lon_count, dtype=jnp.int32))
    poly = legendre(
        owners * owned + first_degree,
        skip,
        orders,
        lane < modes_dev,
        jnp.cos(colatitude),
        jnp.sin(colatitude),
        owned * lat_count * lon_count,
        cut,
    )
    analysis, synthesis = block_tables(poly, CHUNKS * slots)
    own_row = plane * rows_dev + chip * rows_chip
    angle = (own_row + jnp.arange(rows_chip, dtype=jnp.int32)).astype(jnp.float32) + (first_row + 0.5)
    quadrature = jnp.sin(angle * (math.pi / GRID_ROWS)) * ((math.pi / GRID_ROWS) * (2.0 * math.pi / math.sqrt(lon_cols)))

    by_plane = lambda chunks: [trade(chunk).reshape(rows_dev, slots, 2 * width) for chunk in chunks]
    values = after(values, (poly, analysis))
    shards_in = after(by_plane(enter(quadrature, to_modes, values, gain_one, shift_one, slots, CHUNKS)), first_hop)
    first, last, near_first, far_last = after(first_hop, shards_in)
    second_hop = (near(last), far(first))
    third_hop = (far(after(near_first, second_hop)), near(after(far_last, second_hop)))
    late = {2: synthesis, 3: (to_columns, to_modes_back, to_columns_back)}
    rows_in = gather_rows(shards_in, lambda step, own: late.get(step))
    weights = [first, near_first, second_hop[1], third_hop[0], last, second_hop[0], far_last, third_hop[1]]
    coeffs = [analyse(analysis, chunk, *pair) for chunk, pair in enumerate(rows_in)]
    grads = trade(after(cotangent, (coeffs, weights)).reshape(by_row))
    mixed = mix(coeffs, weights, cut)
    grid = [
        trade(scatter_rows(*synthesise(synthesis, chunk, modes, lat_count), gate=grads)[0].reshape(by_chip))
        for chunk, modes in enumerate(mixed)
    ]

    where = jnp.concatenate([crops[0], own_row[None], jnp.zeros((1,), jnp.int32)])
    d_grid, output, d_skipped, sums = feed(
        where, grid, to_columns, to_modes_back, values, grads, gain_two, shift_two, w_up, b_up, w_down, b_down
    )
    bounds = crops[0]
    count_rows = jnp.minimum(bounds[1], own_row + rows_chip) - jnp.maximum(bounds[0], own_row)
    count_cols = jnp.minimum(bounds[3], lon_cols) - jnp.maximum(bounds[2], 0)
    valid_count = (jnp.maximum(count_rows, 0) * jnp.maximum(count_cols, 0)).astype(jnp.float32)
    count_row = sums.shape[0] - 1
    sums = sums + jnp.where(jnp.arange(sums.shape[0]) == count_row, valid_count, 0.0)[:, None]

    shards_back = by_plane(d_grid)
    traded = []

    def gate(step, own):
        if step == 2:
            traded.append(trade(after(output, [rows[1] for rows in own])))
        return traded[0] if step == 3 else None

    rows_back = gather_rows(shards_back, gate)
    output = traded[0].reshape(inputs.shape)
    level = PartSum(after(sums, shards_back))
    sums = level.chips(level.cores())
    d_mixed = [analyse(analysis, 0, *rows_back[0])]
    sums = level.planes(sums, 1, d_mixed)
    d_mixed.append(analyse(analysis, 1, *after(rows_back[1], d_mixed)))
    sums = level.planes(sums, 2, d_mixed)
    d_coeffs, d_weights, near_first, far_last = mix_back(coeffs, after(d_mixed, sums), weights, cut)
    sums = level.share(sums, d_weights)
    other_sums = swap_cores(sums)
    d_coeffs[1] = after(d_coeffs[1], other_sums)
    sums = level.finish(sums, other_sums)
    d_hop = scatter_weights(near_first, far_last)
    d_modes = [
        scatter_rows(*synthesise(synthesis, chunk, modes, lat_count), last_gate=d_hop)
        for chunk, modes in enumerate(d_coeffs)
    ]
    d_hop = after(d_hop, [midway for _, midway in d_modes])
    d_modes = [trade(modes.reshape(by_chip)) for modes, _ in d_modes]
    d_inputs, d_norm = leave(quadrature, d_modes, to_columns_back, values, d_skipped, gain_one)
    d_half = finish_weight_sum(d_weights, *d_hop, d_inputs)
    d_inputs = wide(trade(d_inputs)).reshape(inputs.shape)
    d_norm = sum_everywhere(d_norm)
    d_other = swap_cores(d_half)
    lower = jnp.where(core == 0, d_half, d_other)
    upper = jnp.where(core == 0, d_other, d_half)
    d_spectral = wide(jnp.concatenate([lower, upper[2 * half - owned :]], 0))

    hidden = w_up.shape[1]
    d_up = jnp.concatenate([sums[j * width : j * width + width] for j in range(hidden // width)], 1)
    d_down = sums[hidden : 2 * hidden]
    vectors = sums[2 * hidden :]
    pieces = hidden // width
    d_up_bias = vectors[:pieces].reshape(-1)
    d_down_bias, d_gain_two, d_shift_two, first_moment, second_moment = [vectors[pieces + j] for j in range(5)]
    count = sums[count_row, 0]
    batch_mean = first_moment / count
    batch_var = second_moment / count - batch_mean * batch_mean
    new_mean = (1.0 - momentum) * run_mean + momentum * batch_mean
    new_var = (1.0 - momentum) * run_var + momentum * batch_var
    return (
        output,
        d_inputs,
        d_norm[0],
        d_norm[1],
        d_spectral,
        d_gain_two,
        d_shift_two,
        d_up,
        d_up_bias,
        d_down,
        d_down_bias,
        new_mean,
        new_var,
    )


def fourier_tables(points, modes):
    column = jnp.arange(points, dtype=jnp.int32)
    order = jnp.arange(modes, dtype=jnp.int32)
    phase = column[:, None] * order[None, :] % points
    angle = phase.astype(jnp.float32) * (2.0 * math.pi / points)
    cosine = jnp.cos(angle)
    sine = jnp.sin(angle)
    scale = 1.0 / math.sqrt(points)
    forward_tab = jnp.stack([cosine * scale, -sine * scale], 1)
    factor = jnp.where(order == 0, 1.0, 2.0).astype(jnp.float32)
    inverse_tab = jnp.stack([(cosine * factor[None, :]).T, (-sine * factor[None, :]).T], 0)
    return (forward_tab.astype(jnp.bfloat16), inverse_tab.astype(jnp.bfloat16))


def grid_angles(rows_total):
    first_row = (GRID_ROWS - rows_total) // 2
    colatitude = (jnp.arange(rows_total, dtype=jnp.float32) + (first_row + 0.5)) * (
        math.pi / GRID_ROWS
    )
    return (jnp.cos(colatitude), jnp.sin(colatitude))


def legendre_scan(orders, cosines, sine_vals, degrees):
    order_col = orders[:, None]
    cos_row = cosines[None, :]
    log_start = 0.5 * (
        jnp.log((2.0 * order_col + 1.0) / (4.0 * math.pi))
        + lax.lgamma(order_col + 0.5)
        - lax.lgamma(order_col + 1.0)
        - 0.5 * math.log(math.pi)
    ) + order_col * jnp.log(sine_vals[None, :])
    diagonal_start = jnp.exp(log_start)
    second_start = cos_row * jnp.sqrt(2.0 * order_col + 3.0) * diagonal_start
    zeros_grid = jnp.zeros_like(diagonal_start)

    def advance(state, degree):
        before, latest = state
        upper_ratio = jnp.sqrt(
            (4.0 * degree * degree - 1.0)
            / jnp.maximum(degree * degree - order_col * order_col, 1.0)
        )
        lower_ratio = jnp.sqrt(
            jnp.maximum((degree - 1.0) * (degree - 1.0) - order_col * order_col, 0.0)
            / jnp.maximum(4.0 * (degree - 1.0) * (degree - 1.0) - 1.0, 1.0)
        )
        general = upper_ratio * (cos_row * latest - lower_ratio * before)
        current = jnp.where(
            degree < order_col,
            0.0,
            jnp.where(
                degree == order_col,
                diagonal_start,
                jnp.where(degree == order_col + 1.0, second_start, general),
            ),
        )
        return ((latest, current), current)

    ignored, stacked = lax.scan(
        advance, (zeros_grid, zeros_grid), jnp.arange(degrees).astype(cosines.dtype)
    )
    stacked = jnp.transpose(stacked, (1, 0, 2))
    degree_index = jnp.arange(degrees).astype(cosines.dtype)
    keep = (orders[:, None, None] < M) & (degree_index[None, :, None] < L)
    return jnp.where(keep, stacked, 0.0)


def mix_modes(coeffs, spectral):
    product = jnp.einsum("bmlrc,lscd->bmlrsd", coeffs, spectral, preferred_element_type=jnp.float32)
    real_part = product[:, :, :, 0, 0] - product[:, :, :, 1, 1]
    imag_part = product[:, :, :, 0, 1] + product[:, :, :, 1, 0]
    return jnp.stack([real_part, imag_part], 3).astype(jnp.bfloat16)


def coeff_back(d_mixed, spectral):
    returned = jnp.einsum(
        "bmlsd,lrcd->bmlsrc", d_mixed, spectral, preferred_element_type=jnp.float32
    )
    d_real = returned[:, :, :, 0, 0] + returned[:, :, :, 1, 1]
    d_imag = returned[:, :, :, 1, 0] - returned[:, :, :, 0, 1]
    return jnp.stack([d_real, d_imag], 3).astype(jnp.bfloat16)


def weight_back(coeffs, d_mixed):
    outer_sum = jnp.einsum(
        "bmlrc,bmlsd->lrscd", coeffs, d_mixed, preferred_element_type=jnp.float32
    )
    d_weight_real = outer_sum[:, 0, 0] + outer_sum[:, 1, 1]
    d_weight_imag = outer_sum[:, 0, 1] - outer_sum[:, 1, 0]
    return jnp.stack([d_weight_real, d_weight_imag], 1)


def degree_shards(
    inputs,
    gain_one,
    shift_one,
    spectral,
    gain_two,
    shift_two,
    w_up,
    b_up,
    w_down,
    b_down,
    crops,
    cotangent,
    run_mean,
    run_var,
    momentum,
):
    lat_count = lax.axis_size("lat")
    lon_count = lax.axis_size("lon")
    rows_dev = inputs.shape[1]
    cols_dev = inputs.shape[2]
    width = inputs.shape[3]
    lat_rows = rows_dev * lat_count
    lon_cols = cols_dev * lon_count
    modes_dev = (M + lat_count - 1) // lat_count
    modes_all = modes_dev * lat_count
    quarter = width // lon_count
    owned = spectral.shape[0]
    degrees_all = owned * lat_count * lon_count
    forward_tab, inverse_tab = fourier_tables(lon_cols, modes_all)
    cosines, sine_vals = grid_angles(lat_rows)
    orders = (lax.axis_index("lat") * modes_dev + jnp.arange(modes_dev, dtype=jnp.int32)).astype(
        jnp.float32
    )
    poly = legendre_scan(orders, cosines, sine_vals, degrees_all)
    quadrature = sine_vals * (math.pi / GRID_ROWS) * (2.0 * math.pi / math.sqrt(lon_cols))
    analysis = (poly * quadrature[None, None, :]).astype(jnp.bfloat16)
    synthesis = (
        poly.astype(jnp.bfloat16)
        .reshape(modes_dev, lat_count, lon_count, owned, lat_rows)
        .transpose(0, 2, 1, 3, 4)
    )
    input_wide = inputs.astype(jnp.float32)
    normed_one, norm_one_back = jax.vjp(layer_norm, input_wide, gain_one, shift_one)
    normed_low = normed_one.astype(jnp.bfloat16)
    fourier = jnp.einsum(
        "bijc,jrm->birmc",
        lax.all_to_all(normed_low, "lon", split_axis=3, concat_axis=2, tiled=True),
        forward_tab,
        preferred_element_type=jnp.float32,
    ).astype(jnp.bfloat16)
    portion = lax.all_to_all(fourier, "lat", split_axis=3, concat_axis=1, tiled=True)
    coeffs = jnp.einsum(
        "mli,birmc->bmlrc", analysis, portion, preferred_element_type=jnp.float32
    ).astype(jnp.bfloat16)
    coeffs = coeffs.reshape(1, modes_dev, lat_count, lon_count, owned, 2, portion.shape[4])
    owned_coeffs = lax.all_to_all(
        lax.all_to_all(coeffs, "lat", split_axis=2, concat_axis=1, tiled=True),
        "lon",
        split_axis=3,
        concat_axis=6,
        tiled=True,
    )
    coeffs_owned = owned_coeffs.reshape(1, modes_all, owned, 2, width)
    mixed_modes = mix_modes(coeffs_owned, spectral).reshape(1, modes_all, 1, 1, owned, 2, width)
    returned = lax.all_to_all(
        lax.all_to_all(mixed_modes, "lat", split_axis=1, concat_axis=3, tiled=True),
        "lon",
        split_axis=6,
        concat_axis=2,
        tiled=True,
    )
    grid_modes = jnp.einsum(
        "mjkqi,bmjkqrc->birmc", synthesis, returned, preferred_element_type=jnp.float32
    ).astype(jnp.bfloat16)
    spread = jnp.einsum(
        "birmc,rmj->bijc",
        lax.all_to_all(grid_modes, "lat", split_axis=1, concat_axis=3, tiled=True),
        inverse_tab,
        preferred_element_type=jnp.float32,
    ).astype(jnp.bfloat16)
    spectral_out = lax.all_to_all(spread, "lon", split_axis=2, concat_axis=3, tiled=True)
    skipped = input_wide + spectral_out.astype(jnp.float32)
    normed_two, norm_two_back = jax.vjp(layer_norm, skipped, gain_two, shift_two)
    normed_two_low = normed_two.astype(jnp.bfloat16)
    preact = (
        jnp.einsum("bijc,ch->bijh", normed_two_low, w_up, preferred_element_type=jnp.float32) + b_up
    )
    activated, gelu_back = jax.vjp(jax.nn.gelu, preact)
    activated_low = activated.astype(jnp.bfloat16)
    result = (
        skipped
        + jnp.einsum("bijh,hc->bijc", activated_low, w_down, preferred_element_type=jnp.float32)
        + b_down
    )
    output = result.astype(jnp.bfloat16)
    bounds = crops[0]
    row_global = lax.axis_index("lat") * rows_dev + jnp.arange(rows_dev, dtype=jnp.int32)
    col_global = lax.axis_index("lon") * cols_dev + jnp.arange(cols_dev, dtype=jnp.int32)
    inside_rows = (row_global >= bounds[0]) & (row_global < bounds[1])
    inside_cols = (col_global >= bounds[2]) & (col_global < bounds[3])
    mask_grid = (inside_rows[:, None] & inside_cols[None, :]).astype(jnp.float32)[None, :, :, None]
    valid_count = jnp.sum(mask_grid)
    first_moment = jnp.sum(mask_grid * result, (0, 1, 2))
    second_moment = jnp.sum(mask_grid * result * result, (0, 1, 2))
    grad_wide = cotangent.astype(jnp.float32)
    d_down = jnp.einsum(
        "bijh,bijc->hc", activated_low, cotangent, preferred_element_type=jnp.float32
    )
    d_down_bias = jnp.sum(grad_wide, (0, 1, 2))
    d_activated = jnp.einsum("bijc,hc->bijh", cotangent, w_down, preferred_element_type=jnp.float32)
    d_preact = gelu_back(d_activated)[0].astype(jnp.bfloat16)
    d_up = jnp.einsum("bijc,bijh->ch", normed_two_low, d_preact, preferred_element_type=jnp.float32)
    d_up_bias = jnp.sum(d_preact.astype(jnp.float32), (0, 1, 2))
    d_normed_two = jnp.einsum("bijh,ch->bijc", d_preact, w_up, preferred_element_type=jnp.float32)
    d_skipped, d_gain_two, d_shift_two = norm_two_back(d_normed_two)
    d_skipped = d_skipped + grad_wide
    d_spread = d_skipped.astype(jnp.bfloat16)
    d_grid = jnp.einsum(
        "bijc,rmj->birmc",
        lax.all_to_all(d_spread, "lon", split_axis=3, concat_axis=2, tiled=True),
        inverse_tab,
        preferred_element_type=jnp.float32,
    ).astype(jnp.bfloat16)
    d_returned = jnp.einsum(
        "mjkqi,birmc->bmjkqrc",
        synthesis,
        lax.all_to_all(d_grid, "lat", split_axis=3, concat_axis=1, tiled=True),
        preferred_element_type=jnp.float32,
    ).astype(jnp.bfloat16)
    d_mixed = lax.all_to_all(
        lax.all_to_all(d_returned, "lat", split_axis=3, concat_axis=1, tiled=True),
        "lon",
        split_axis=2,
        concat_axis=6,
        tiled=True,
    ).reshape(1, modes_all, owned, 2, width)
    d_coeffs = coeff_back(d_mixed, spectral)
    d_spectral = lax.psum(weight_back(coeffs_owned, d_mixed).astype(jnp.bfloat16), "batch").astype(
        jnp.float32
    )
    d_coeffs_wide = d_coeffs.reshape(1, modes_all, 1, 1, owned, 2, width)
    d_modes = lax.all_to_all(
        lax.all_to_all(d_coeffs_wide, "lat", split_axis=1, concat_axis=2, tiled=True),
        "lon",
        split_axis=6,
        concat_axis=3,
        tiled=True,
    ).reshape(1, modes_dev, degrees_all, 2, quarter)
    d_fourier = jnp.einsum(
        "mli,bmlrc->birmc", analysis, d_modes, preferred_element_type=jnp.float32
    ).astype(jnp.bfloat16)
    d_columns = jnp.einsum(
        "birmc,jrm->bijc",
        lax.all_to_all(d_fourier, "lat", split_axis=1, concat_axis=3, tiled=True),
        forward_tab,
        preferred_element_type=jnp.float32,
    ).astype(jnp.bfloat16)
    d_normed_one = lax.all_to_all(d_columns, "lon", split_axis=2, concat_axis=3, tiled=True).astype(
        jnp.float32
    )
    d_input_norm, d_gain_one, d_shift_one = norm_one_back(d_normed_one)
    d_inputs = d_input_norm + d_skipped
    summed = lax.psum(
        (
            d_up,
            d_down,
            d_up_bias,
            d_down_bias,
            d_gain_one,
            d_shift_one,
            d_gain_two,
            d_shift_two,
            valid_count,
            first_moment,
            second_moment,
        ),
        ("lat", "lon", "batch"),
    )
    batch_mean = summed[9] / summed[8]
    batch_var = summed[10] / summed[8] - batch_mean * batch_mean
    new_mean = (1.0 - momentum) * run_mean + momentum * batch_mean
    new_var = (1.0 - momentum) * run_var + momentum * batch_var
    return (
        output,
        d_inputs,
        summed[4],
        summed[5],
        d_spectral,
        summed[6],
        summed[7],
        summed[0],
        summed[2],
        summed[1],
        summed[3],
        new_mean,
        new_var,
    )


def shards(inputs, *rest):
    rows_dev = inputs.shape[1]
    lon_count = lax.axis_size("lon")
    banded = (
        lon_count == 4
        and lax.axis_size("batch") == 2
        and rows_dev % lon_count == 0
        and M % lon_count == 0
        and M // lon_count <= 128
        and rest[2].shape[0] % 4 in (0, 3)
        and rows_dev * lax.axis_size("lat") <= 32
    )
    return (band_shards if banded else degree_shards)(inputs, *rest)


def solution(mesh):
    return jax.shard_map(
        shards,
        mesh=mesh,
        in_specs=(
            P("batch", "lat", "lon", None),
            P(),
            P(),
            P(("lat", "lon"), None, None, None),
            P(),
            P(),
            P(),
            P(),
            P(),
            P(),
            P("batch", None),
            P("batch", "lat", "lon", None),
            P(),
            P(),
            P(),
        ),
        out_specs=(
            P("batch", "lat", "lon", None),
            P("batch", "lat", "lon", None),
            P(),
            P(),
            P(("lat", "lon"), None, None, None),
            P(),
            P(),
            P(),
            P(),
            P(),
            P(),
            P(),
            P(),
        ),
        check_vma=False,
    )
```

```python
import math

import jax
import jax.numpy as jnp
from jax import lax
from jax.experimental import pallas as pl
from jax.experimental.pallas import tpu as pltpu
from jax.sharding import PartitionSpec as P

GRID_ROWS = 360
M = 360
L = 360


epsilon = 1e-05
GROUP = 8
CHUNKS = 2
PER_STEP = 3


def layer_norm(values, gain, shift):
    centre = values - jnp.mean(values, -1, keepdims=True)
    spread = jnp.mean(centre * centre, -1, keepdims=True)
    return centre * lax.rsqrt(spread + epsilon) * gain + shift


def xor_pairs(count, bit):
    return [(i, i ^ bit) for i in range(count)]


def ring_pairs(count, step):
    return [(i, (i + step) % count) for i in range(count)]


def swap_cores(values):
    return lax.ppermute(values, "batch", xor_pairs(2, 1))


def near(values):
    return lax.ppermute(values, "lon", xor_pairs(4, 1))


def far(values):
    return lax.ppermute(values, "lon", xor_pairs(4, 2))


def after(values, earlier):
    return lax.optimization_barrier((values, earlier))[0]


def trade(values):
    return lax.all_to_all(values, "lon", split_axis=0, concat_axis=0, tiled=True)


def cross(values, k):
    return lax.ppermute(values, "lon", xor_pairs(4, k))


def trade_pieces(pieces):
    return [pieces[0]] + [cross(pieces[k], k) for k in (1, 2, 3)]


def gathered(values, name):
    count = lax.axis_size(name)
    pairs = xor_pairs if name == "lon" else ring_pairs
    return [values] + [lax.ppermute(values, name, pairs(count, k)) for k in range(1, count)]


def in_order(pieces, name):
    at, count = lax.axis_index(name), len(pieces)
    pieces = jnp.stack(pieces, 0)
    where = lambda place: at ^ place if name == "lon" else (at - place) % count
    return [lax.dynamic_index_in_dim(pieces, where(place), 0, keepdims=False) for place in range(count)]


def sum_over_planes(values):
    return sum(in_order(gathered(values, "lat"), "lat"))


def dot(a, b):
    return jnp.dot(a, b, preferred_element_type=jnp.float32)


def dot_along(a, b):
    return lax.dot_general(a, b, (((1,), (1,)), ((), ())), preferred_element_type=jnp.float32)


def dot_across(a, b):
    return lax.dot_general(a, b, (((0,), (0,)), ((), ())), preferred_element_type=jnp.float32)


def low(values):
    return values.astype(jnp.bfloat16)


def wide(values):
    return values.astype(jnp.float32)


NO_COST = pl.CostEstimate(flops=0, transcendentals=0, bytes_accessed=0)


def params(megabytes):
    return pltpu.CompilerParams(vmem_limit_bytes=megabytes * 2**20)


def turned(cosine, sine, quarter_turns):
    turns = quarter_turns % 4
    real = jnp.where(turns == 0, cosine, jnp.where(turns == 1, -sine, jnp.where(turns == 2, -cosine, sine)))
    imag = jnp.where(turns == 0, -sine, jnp.where(turns == 1, -cosine, jnp.where(turns == 2, sine, cosine)))
    return real, imag


def dft_tables(points, parts, order, valid, axis):
    cols = points // parts
    column = jnp.arange(cols, dtype=jnp.int32)
    if axis == 1:
        order, valid, column = order[:, None], valid[:, None], column[None, :]
    else:
        order, valid, column = order[None, :], valid[None, :], column[:, None]
    angle = (order * column % points).astype(jnp.float32) * (2.0 * math.pi / points)
    cosine = jnp.where(valid, jnp.cos(angle), 0.0)
    sine = jnp.where(valid, jnp.sin(angle), 0.0)
    cosine, sine = lax.optimization_barrier((cosine, sine))
    part = jnp.arange(parts, dtype=jnp.int32)[:, None, None]
    real, imag = turned(cosine[None], sine[None], part * order[None])
    scales = (1.0 / math.sqrt(points), jnp.where(order == 0, 1.0, 2.0)[None])
    return [jnp.concatenate([low(real * scale), low(imag * scale)], axis) for scale in scales]


def legendre_kernel(cut, starts_ref, upper_ref, lower_ref, order_ref, cos_ref, diag_ref, second_ref, out_ref, all_ref):
    degrees = all_ref.shape[0]
    cosines = cos_ref[...]
    diagonal = diag_ref[...]
    second = second_ref[...]
    order = order_ref[...]

    def advance(degree, state):
        before, latest = state
        level = degree.astype(jnp.float32)
        upper = upper_ref[pl.ds(degree, 1), :]
        lower = lower_ref[pl.ds(degree, 1), :]
        general = upper * (cosines * latest - lower * before)
        current = jnp.where(
            level < order,
            0.0,
            jnp.where(level == order, diagonal, jnp.where(level == order + 1.0, second, general)),
        )
        all_ref[pl.ds(degree, 1)] = current[None]
        return latest, current

    unroll = 8 if degrees % 8 == 0 else 1

    def several(step, state):
        for at in range(unroll):
            state = advance(step * unroll + at, state)
        return state

    zeros = cosines * 0.0
    lax.fori_loop(0, degrees // unroll, several, (zeros, zeros))
    blocks = out_ref.shape[0] // (2 * cut)
    for block in range(blocks):
        for half in range(2):

            def copy(at, carry, block=block, half=half):
                degree = starts_ref[block] + half * cut + at
                value = all_ref[pl.ds(degree, 1)]
                keep = (degree < L) & (half * cut + at >= starts_ref[blocks])
                out_ref[pl.ds((at * 2 + half) * blocks + block, 1)] = jnp.where(keep, value, 0.0)
                return carry

            lax.fori_loop(0, cut, copy, 0)


def legendre(starts, skip, orders, valid, cosines, sine_vals, degrees, cut):
    order_row = orders[None, :]
    sine_col = sine_vals[:, None]
    log_start = 0.5 * (
        jnp.log((2.0 * order_row + 1.0) / (4.0 * math.pi))
        + lax.lgamma(order_row + 0.5)
        - lax.lgamma(order_row + 1.0)
        - 0.5 * math.log(math.pi)
    ) + order_row * jnp.log(sine_col)
    diagonal = jnp.where(valid[None, :], jnp.exp(log_start), 0.0)
    second = cosines[:, None] * jnp.sqrt(2.0 * order_row + 3.0) * diagonal
    degree = jnp.arange(degrees, dtype=jnp.float32)[:, None]
    upper = jnp.sqrt((4.0 * degree * degree - 1.0) / jnp.maximum(degree * degree - order_row * order_row, 1.0))
    lower = jnp.sqrt(
        jnp.maximum((degree - 1.0) * (degree - 1.0) - order_row * order_row, 0.0)
        / jnp.maximum(4.0 * (degree - 1.0) * (degree - 1.0) - 1.0, 1.0)
    )
    shape = diagonal.shape
    return pl.pallas_call(
        lambda *refs: legendre_kernel(cut, *refs),
        out_shape=jax.ShapeDtypeStruct((starts.shape[0] * 2 * cut,) + shape, jnp.float32),
        in_specs=[pl.BlockSpec(memory_space=pltpu.SMEM)] + [pl.BlockSpec(memory_space=pltpu.VMEM)] * 6,
        out_specs=pl.BlockSpec(memory_space=pltpu.VMEM),
        scratch_shapes=[pltpu.VMEM((degrees,) + shape, jnp.float32)],
        cost_estimate=NO_COST,
        compiler_params=params(24),
        name="legendre",
    )(
        jnp.concatenate([starts, skip[None]]).astype(jnp.int32),
        upper,
        lower,
        jnp.broadcast_to(order_row, shape),
        jnp.broadcast_to(cosines[:, None], shape),
        diagonal,
        second,
    )


def block_tables(poly, slots):
    degrees, rows, _ = poly.shape
    groups = slots // GROUP
    values = low(poly[:, :, :slots]).reshape(degrees, rows, groups, GROUP)

    def expand(table, depth):
        lanes = depth * GROUP
        lane = jnp.arange(lanes, dtype=jnp.int32)
        repeat = low(jnp.arange(depth, dtype=jnp.int32)[:, None] == lane[None, :] // GROUP)
        flat = table.reshape(-1, depth)
        row = jnp.arange(flat.shape[0], dtype=jnp.int32)
        same = row[:, None] % GROUP == lane[None, :] % GROUP
        return low(jnp.where(same, dot(flat, repeat), 0.0)).reshape(groups, -1, lanes)

    return expand(values.transpose(2, 0, 3, 1), rows), expand(values.transpose(2, 1, 3, 0), degrees)


def normalise(values):
    centre = values - jnp.mean(values, -1, keepdims=True)
    factor = lax.rsqrt(jnp.mean(centre * centre, -1, keepdims=True) + epsilon)
    return centre * factor, factor


def normalise_back(normal, factor, grad):
    return factor * (
        grad - jnp.mean(grad, -1, keepdims=True) - normal * jnp.mean(grad * normal, -1, keepdims=True)
    )


def column_sum(values):
    return jnp.sum(values, 0, keepdims=True)


def store_modes(totals, refs):
    groups, _, double = refs[0].shape
    width = double // 2
    slots = groups * GROUP
    for part in range(2):
        for owner, ref in enumerate(refs):
            at = (part * len(refs) + owner) * slots
            rows = [total[at : at + slots].reshape(groups, GROUP, width) for total in totals]
            ref[:, :, part * width : part * width + width] = low(jnp.concatenate(rows, 1))


def load_modes(refs, flat_ref):
    groups, _, double = refs[0].shape
    width = double // 2
    slots = groups * GROUP
    rows = flat_ref.shape[0]
    half = flat_ref.shape[1] // 2
    for piece, ref in enumerate(refs):
        owner, chunk = piece // CHUNKS, piece % CHUNKS
        at = (owner * CHUNKS + chunk) * slots
        modes = wide(ref[...]).reshape(groups, rows, GROUP, double)
        for row in range(rows):
            flat = low(modes[:, row].reshape(slots, double))
            flat_ref[row, at : at + slots] = flat[:, :width]
            flat_ref[row, half + at : half + at + slots] = flat[:, width:]


def whole_spec(array):
    return pl.BlockSpec(array.shape, lambda *at: (0,) * len(array.shape))


def enter_kernel(weight_ref, table_ref, values_ref, gain_ref, shift_ref, *out_refs):
    totals = []
    for row in range(values_ref.shape[1]):
        total = 0.0
        for part in range(table_ref.shape[0]):
            normal, _ = normalise(wide(values_ref[part, row]))
            total += dot(table_ref[part], low(normal * gain_ref[...] + shift_ref[...]))
        totals.append(total * weight_ref[row])
    store_modes(totals, out_refs)


def enter(weight, table, values, gain, shift, groups):
    parts, rows, cols, width = values.shape
    arrays = [table, values, gain[None], shift[None]]
    return pl.pallas_call(
        enter_kernel,
        out_shape=[jax.ShapeDtypeStruct((groups, rows * GROUP, 2 * width), jnp.bfloat16)] * parts,
        in_specs=[pl.BlockSpec(memory_space=pltpu.SMEM)] + [pl.BlockSpec(memory_space=pltpu.VMEM)] * 4,
        out_specs=[pl.BlockSpec(memory_space=pltpu.VMEM)] * parts,
        cost_estimate=NO_COST,
        compiler_params=params(32),
        name="enter",
    )(weight, *arrays)


def gelu_parts(values):
    slope = math.sqrt(2.0 / math.pi)
    square = values * values
    tangent = jnp.tanh(slope * values * (1.0 + 0.044715 * square))
    half = 0.5 * (1.0 + tangent)
    grad = half + 0.5 * values * (1.0 - tangent * tangent) * slope * (1.0 + 3.0 * 0.044715 * square)
    return values * half, grad


def feed_kernel(pieces, where_ref, *refs):
    modes_refs, refs = refs[:pieces], refs[pieces:]
    (columns_ref, modes_table_ref, values_ref, cotangent_ref), refs = refs[:4], refs[4:]
    (gain_ref, shift_ref, up_ref, up_bias_ref, down_ref, down_bias_ref), refs = refs[:6], refs[6:]
    *grid_refs, output_ref, d_skipped_ref, sums_ref, flat_ref, total_ref = refs
    row, part = pl.program_id(0), pl.program_id(1)
    rows, parts = pl.num_programs(0), pl.num_programs(1)
    width = values_ref.shape[-1]
    cols = values_ref.shape[-2]
    hidden = up_ref.shape[-1]

    @pl.when((part == 0) & (row == 0))
    def _():
        load_modes(modes_refs, flat_ref)
        sums_ref[...] = jnp.zeros_like(sums_ref)

    spread = low(dot(columns_ref[0], flat_ref[row]))
    skipped = wide(values_ref[0, 0]) + wide(spread)
    normal, factor = normalise(skipped)
    normed = low(normal * gain_ref[...] + shift_ref[...])
    activated, slope = gelu_parts(dot(normed, up_ref[...]) + up_bias_ref[...])
    activated = low(activated)
    result = skipped + dot(activated, down_ref[...]) + down_bias_ref[...]
    output_ref[0, 0] = low(result)
    row_at = where_ref[4] + row
    column_at = where_ref[5] + part * cols + lax.broadcasted_iota(jnp.int32, (cols, 1), 0)
    inside = (column_at >= where_ref[2]) & (column_at < where_ref[3])
    inside = inside & (row_at >= where_ref[0]) & (row_at < where_ref[1])
    kept = jnp.where(inside, result, 0.0)

    cotangent = cotangent_ref[0, 0]
    d_preact = low(dot_along(cotangent, down_ref[...]) * slope)
    d_normed = dot_along(d_preact, up_ref[...])
    d_skipped = wide(cotangent) + normalise_back(normal, factor, d_normed * gain_ref[...])
    d_skipped_ref[0, 0] = d_skipped
    term = dot(modes_table_ref[0], low(d_skipped))

    @pl.when(part == 0)
    def _():
        total_ref[row] = term

    @pl.when(part > 0)
    def _():
        total_ref[row] += term

    @pl.when((part == parts - 1) & (row == rows - 1))
    def _():
        store_modes([total_ref[at] for at in range(total_ref.shape[0])], grid_refs)

    d_up = dot_across(normed, d_preact)
    for at in range(hidden // width):
        sums_ref[at * width : at * width + width] += d_up[:, at * width : at * width + width]
    sums_ref[hidden : 2 * hidden] += dot_across(activated, cotangent)
    at = 2 * hidden
    d_bias = column_sum(wide(d_preact))
    vectors = [d_bias[:, j * width : j * width + width] for j in range(hidden // width)] + [
        column_sum(wide(cotangent)),
        column_sum(d_normed * normal),
        column_sum(d_normed),
        column_sum(kept),
        column_sum(kept * kept),
    ]
    for j, vector in enumerate(vectors):
        sums_ref[at + j : at + j + 1] += vector


def feed(where, modes, columns, modes_table, values, cotangent, gain, shift, w_up, b_up, w_down, b_down):
    parts, rows, cols, width = values.shape
    hidden = w_up.shape[1]
    lanes = modes_table.shape[1]
    grid = (CHUNKS * modes[0].shape[0],) + modes[0].shape[1:]
    cells = pl.BlockSpec((1, 1, cols, width), lambda i, p: (p, i, 0, 0))
    by_part = lambda table: pl.BlockSpec((1,) + table.shape[1:], lambda i, p: (p, 0, 0))
    small = [gain[None], shift[None], w_up, b_up[None], w_down, b_down[None]]
    outs = [jax.ShapeDtypeStruct(grid, jnp.bfloat16)] * parts + [
        jax.ShapeDtypeStruct(values.shape, jnp.bfloat16),
        jax.ShapeDtypeStruct(values.shape, jnp.float32),
        jax.ShapeDtypeStruct(((2 * hidden + hidden // width + 5 + 63) // 64 * 64, width), jnp.float32),
    ]
    return pl.pallas_call(
        lambda *refs: feed_kernel(len(modes), *refs),
        grid=(rows, parts),
        out_shape=outs,
        in_specs=[pl.BlockSpec(memory_space=pltpu.SMEM)]
        + [whole_spec(m) for m in modes]
        + [by_part(columns), by_part(modes_table), cells, cells]
        + [whole_spec(v) for v in small],
        out_specs=[whole_spec(outs[0])] * parts + [cells, cells, whole_spec(outs[-1])],
        scratch_shapes=[pltpu.VMEM((rows, lanes, width), jnp.bfloat16), pltpu.VMEM((rows, lanes, width), jnp.float32)],
        cost_estimate=NO_COST,
        compiler_params=params(60),
        name="feed",
    )(where, *modes, columns, modes_table, values, cotangent, *small)


def leave_kernel(pieces, weight_ref, *refs):
    modes_refs, refs = refs[:pieces], refs[pieces:]
    columns_ref, values_ref, d_skipped_ref, gain_ref, out_ref, sums_ref, flat_ref = refs
    row, part = pl.program_id(0), pl.program_id(1)

    @pl.when((part == 0) & (row == 0))
    def _():
        load_modes(modes_refs, flat_ref)
        sums_ref[...] = jnp.zeros_like(sums_ref)

    d_normed = wide(low(dot(columns_ref[0], flat_ref[row]) * weight_ref[row]))
    normal, factor = normalise(wide(values_ref[0, 0]))
    out_ref[0, 0] = low(normalise_back(normal, factor, d_normed * gain_ref[...]) + d_skipped_ref[0, 0])
    sums_ref[0:1] += column_sum(d_normed * normal)
    sums_ref[1:2] += column_sum(d_normed)


def leave(weight, modes, columns, values, d_skipped, gain):
    parts, rows, cols, width = values.shape
    cells = pl.BlockSpec((1, 1, cols, width), lambda i, p: (p, i, 0, 0))
    return pl.pallas_call(
        lambda *refs: leave_kernel(len(modes), *refs),
        grid=(rows, parts),
        out_shape=[jax.ShapeDtypeStruct(values.shape, jnp.bfloat16), jax.ShapeDtypeStruct((8, width), jnp.float32)],
        in_specs=[pl.BlockSpec(memory_space=pltpu.SMEM)]
        + [whole_spec(m) for m in modes]
        + [
            pl.BlockSpec((1,) + columns.shape[1:], lambda i, p: (p, 0, 0)),
            cells,
            cells,
            pl.BlockSpec((1, width), lambda i, p: (0, 0)),
        ],
        out_specs=[cells, pl.BlockSpec((8, width), lambda i, p: (0, 0))],
        scratch_shapes=[pltpu.VMEM((rows, columns.shape[2], width), jnp.bfloat16)],
        cost_estimate=NO_COST,
        compiler_params=params(32),
        name="leave",
    )(weight, *modes, columns, values, d_skipped, gain[None])


def complex_weight(weight_ref):
    real, imag = weight_ref[0, 0], weight_ref[0, 1]
    return jnp.concatenate([jnp.concatenate([real, imag], 1), jnp.concatenate([-imag, real], 1)], 0)


class Core:
    def __init__(self, shard, slots, degrees, cut, rows, table, weights, back_table):
        self.slots, self.cut, self.degrees = slots, cut, degrees
        self.steps = shard[1] // PER_STEP
        ends = CHUNKS * self.steps
        self.first = ends if table is not None else 0
        self.last = ends if back_table is not None else 0
        self.grid = (self.first + cut + self.last,)
        self.modes = (degrees, CHUNKS * shard[1]) + shard[2:]
        self.per = degrees // cut
        block = (shard[0], PER_STEP) + shard[2:]
        place = lambda step, start, count: jnp.clip(step - start, 0, count - 1)
        self.middle = lambda s: place(s, self.first, cut)
        self.arrays, self.in_specs = [], []
        for chunk in range(CHUNKS if self.first else 0):
            spec = pl.BlockSpec(block, lambda s, chunk=chunk: (0, place(s, chunk * self.steps, self.steps), 0, 0))
            self.take([slot for sample in rows[chunk] for slot in sample], spec)
        if self.first:
            self.take([table], pl.BlockSpec((PER_STEP,) + table.shape[1:], lambda s: (place(s, 0, ends), 0, 0)))
        start = self.first + cut
        if self.last:
            spec = pl.BlockSpec((PER_STEP,) + back_table.shape[1:], lambda s: (place(s, start, ends), 0, 0))
            self.take([back_table], spec)
        self.take(weights, pl.BlockSpec((1,) + weights[0].shape[1:], lambda s: (self.middle(s), 0, 0, 0)))
        self.modes_spec = pl.BlockSpec((self.per,) + self.modes[1:], lambda s: (self.middle(s), 0, 0, 0))
        self.modes_shape = jax.ShapeDtypeStruct(self.modes, jnp.bfloat16)
        self.held = pltpu.VMEM(self.modes, jnp.bfloat16)
        self.out_specs, self.out_shape = [], []
        for chunk in range(CHUNKS if self.last else 0):
            at = lambda s, chunk=chunk: (0, 0, place(s, start + chunk * self.steps, self.steps), 0, 0)
            self.out_specs += [pl.BlockSpec((slots,) + block, at)] * 2
            self.out_shape += [jax.ShapeDtypeStruct((slots,) + shard, jnp.bfloat16)] * 2

    def take(self, arrays, spec):
        self.arrays += arrays
        self.in_specs += [spec] * len(arrays)

    def split(self, refs):
        at = CHUNKS * 2 * self.slots if self.first else 0
        shards, refs = refs[:at], refs[at:]
        table, refs = (refs[0], refs[1:]) if self.first else (None, refs)
        back_table, refs = (refs[0], refs[1:]) if self.last else (None, refs)
        count = len(self.arrays) - at - (table is not None) - (back_table is not None)
        return shards, table, back_table, refs[:count], refs[count:]

    def analyse(self, shard_refs, table_ref, held_ref):
        step = pl.program_id(0)
        for chunk in range(CHUNKS):
            refs = shard_refs[chunk * 2 * self.slots : (chunk + 1) * 2 * self.slots]

            @pl.when((step >= chunk * self.steps) & (step < (chunk + 1) * self.steps))
            def _(refs=refs):
                for at in range(PER_STEP):
                    samples = []
                    for sample in range(2):
                        rows = [flat_rows(ref[:, at]) for ref in refs[sample * self.slots : (sample + 1) * self.slots]]
                        total = dot(table_ref[at], jnp.concatenate(rows, 0))
                        samples.append(total.reshape(self.degrees, GROUP, -1))
                    held_ref[:, pl.ds(step * PER_STEP + at, 1)] = low(jnp.concatenate(samples, 1))[:, None]

    def synthesise(self, table_ref, held_ref, out_refs):
        step = pl.program_id(0) - self.first - self.cut
        for chunk in range(CHUNKS):
            refs = out_refs[2 * chunk : 2 * chunk + 2]

            @pl.when((step >= chunk * self.steps) & (step < (chunk + 1) * self.steps))
            def _(refs=refs):
                for at in range(PER_STEP):
                    modes = wide(held_ref[:, pl.ds(step * PER_STEP + at, 1)])
                    modes = modes.reshape(self.degrees, 2, GROUP, modes.shape[-1])
                    for sample, ref in enumerate(refs):
                        total = low(dot(table_ref[at], low(flat_rows(modes[:, sample]))))
                        ref[:, :, at] = total.reshape(ref.shape[:2] + ref.shape[3:])

    def in_middle(self):
        step = pl.program_id(0)
        return (step >= self.first) & (step < self.first + self.cut)

    def degree(self, at):
        return self.middle(pl.program_id(0)) * self.per + at

    def chunks(self, out):
        return [out[2 * chunk : 2 * chunk + 2] for chunk in range(CHUNKS)]


def flat_rows(modes):
    return modes.reshape(-1, modes.shape[-1])


def mix_forward(rows, table, back_table, weights, cut):
    shard = rows[0][0][0].shape
    core = Core(shard, len(rows[0][0]), len(weights) * cut, cut, rows, table, weights, back_table)

    def kernel(*refs):
        shards, table, back_table, weight_refs, (*out_refs, coeffs_ref, held_ref, mixed_ref) = core.split(refs)
        core.analyse(shards, table, held_ref)

        @pl.when(core.in_middle())
        def _():
            for at, weight_ref in enumerate(weight_refs):
                coeffs = held_ref[core.degree(at)]
                coeffs_ref[at] = coeffs
                mixed = low(dot(flat_rows(coeffs), complex_weight(weight_ref)))
                mixed_ref[core.degree(at)] = mixed.reshape(coeffs.shape)

        core.synthesise(back_table, mixed_ref, out_refs)

    out = pl.pallas_call(
        kernel,
        grid=core.grid,
        out_shape=core.out_shape + [core.modes_shape],
        in_specs=core.in_specs,
        out_specs=core.out_specs + [core.modes_spec],
        scratch_shapes=[core.held, core.held],
        cost_estimate=NO_COST,
        compiler_params=params(60),
        name="mix_forward",
    )(*core.arrays)
    return core.chunks(out), out[-1]


def mix_backward(rows, table, back_table, weights, cut, coeffs):
    shard = rows[0][0][0].shape
    core = Core(shard, len(rows[0][0]), len(weights) * cut, cut, rows, table, weights, back_table)
    weight = weights[0].shape
    grad = pl.BlockSpec((1,) + weight[1:], lambda s: (core.middle(s), 0, 0, 0))

    def kernel(*refs):
        shards, table, back_table, weight_refs, (coeffs_ref, *outs, held_ref, mixed_ref) = core.split(refs)
        core.analyse(shards, table, held_ref)

        @pl.when(core.in_middle())
        def _():
            for at, (weight_ref, target) in enumerate(zip(weight_refs, outs[-len(weights) :])):
                d_mixed = held_ref[core.degree(at)]
                d_coeffs = low(dot_along(flat_rows(d_mixed), complex_weight(weight_ref)))
                mixed_ref[core.degree(at)] = d_coeffs.reshape(d_mixed.shape)
                total = dot_across(flat_rows(coeffs_ref[at]), flat_rows(d_mixed))
                width = target.shape[-1]
                target[0, 0] = low(total[:width, :width] + total[width:, width:])
                target[0, 1] = low(total[:width, width:] - total[width:, :width])

        core.synthesise(back_table, mixed_ref, outs[: -len(weights)])

    out = pl.pallas_call(
        kernel,
        grid=core.grid,
        out_shape=core.out_shape + [jax.ShapeDtypeStruct(weight, jnp.bfloat16)] * len(weights),
        in_specs=core.in_specs + [core.modes_spec],
        out_specs=core.out_specs + [grad] * len(weights),
        scratch_shapes=[core.held, core.held],
        cost_estimate=NO_COST,
        compiler_params=params(60),
        name="mix_backward",
    )(*core.arrays, coeffs)
    return core.chunks(out), out[-len(weights) :]


def gather_rows(shards, gate):
    count = lax.axis_size("lat")
    own = [[shard] for shard in shards]
    for step in range(1, count):
        earlier = gate(step, own)
        sent = [rows[-1] for rows in own]
        if earlier is not None:
            sent = after(sent, earlier)
        own = [rows + [lax.ppermute(rows_sent, "lat", ring_pairs(count, 1))] for rows, rows_sent in zip(own, sent)]
    return [(rows, [swap_cores(slot) for slot in rows]) for rows in own]


def scatter_rows(own, other, gate=None):
    count = lax.axis_size("lat")
    other = swap_cores(other)
    arrived = None
    for slot in range(count - 1, -1, -1):
        total = wide(own[slot]) + wide(other[slot])
        if arrived is not None:
            total = total + wide(arrived)
        total = low(total)
        if slot == 1:
            midway = total
        if slot > 0:
            arrived = lax.ppermute(total, "lat", ring_pairs(count, -1))
            if slot == 3 and gate is not None:
                arrived = after(arrived, gate)
    return total, midway


def gather_weights(own):
    cut = own.shape[0] // 2
    first, last = own[:cut], own[cut:]
    return first, last, near(first), far(last)


def scatter_weights(grads):
    three = near(grads[3]), far(grads[7])
    one, two = after((grads[1], grads[6]), three)
    return three, (near(one), far(two))


def finish_weight_sum(grads, three, gate):
    from_near, from_far = after(three, gate)
    return far(low(wide(grads[2]) + wide(from_near))), near(low(wide(grads[5]) + wide(from_far)))


def sum_weights(grads, single, double):
    first = low(wide(grads[0]) + wide(single[0]) + wide(double[0]))
    last = low(wide(grads[4]) + wide(single[1]) + wide(double[1]))
    return first, last


class PartSum:
    def __init__(self, values):
        core = lax.axis_index("batch")
        half = values.shape[0] // 2
        self.mine = lax.dynamic_slice_in_dim(values, core * half, half, 0)
        self.other = swap_cores(lax.dynamic_slice_in_dim(values, (1 - core) * half, half, 0))

    def cores(self):
        return self.mine + self.other

    def chips(self, values):
        chip = lax.axis_index("lon")
        part = values.shape[0] // 4
        for_chip = lambda k: lax.dynamic_slice_in_dim(values, (chip ^ k) * part, part, 0)
        return sum(trade_pieces([for_chip(k) for k in range(4)]))

    def share(self, pieces):
        return jnp.concatenate(in_order(pieces, "lon"), 0)

    def finish(self, mine, other):
        core = lax.axis_index("batch")
        return jnp.concatenate([jnp.where(core == 0, mine, other), jnp.where(core == 0, other, mine)], 0)


def band_shards(
    inputs,
    gain_one,
    shift_one,
    spectral,
    gain_two,
    shift_two,
    w_up,
    b_up,
    w_down,
    b_down,
    crops,
    cotangent,
    run_mean,
    run_var,
    momentum,
):
    lat_count = lax.axis_size("lat")
    lon_count = lax.axis_size("lon")
    plane = lax.axis_index("lat")
    chip = lax.axis_index("lon")
    core = lax.axis_index("batch")
    rows_dev = inputs.shape[1]
    cols_dev = inputs.shape[2]
    width = inputs.shape[3]
    rows_chip = rows_dev // lon_count
    lat_rows = rows_dev * lat_count
    lon_cols = cols_dev * lon_count
    modes_dev = M // lon_count
    slots = (modes_dev + CHUNKS * PER_STEP * GROUP - 1) // (CHUNKS * PER_STEP * GROUP) * PER_STEP * GROUP
    groups = slots // GROUP
    owned = spectral.shape[0]
    cut = (owned + 3) // 4
    half = 2 * cut
    first_degree = core * (owned - half)
    skip = core * (2 * half - owned)
    by_row = (lon_count, rows_chip, cols_dev, width)

    first_hop = gather_weights(lax.dynamic_slice_in_dim(spectral, first_degree, half, 0))
    values = trade(inputs.reshape(by_row))

    across = chip ^ jnp.arange(lon_count, dtype=jnp.int32)
    in_chip = jnp.arange(CHUNKS * slots, dtype=jnp.int32)
    first_order = across[:, None] * modes_dev + in_chip[None, :]
    valid = jnp.broadcast_to(in_chip[None, :] < modes_dev, first_order.shape)
    order = jnp.where(valid, first_order, 0)
    to_modes, to_modes_back = dft_tables(lon_cols, lon_count, order.reshape(-1), valid.reshape(-1), 1)
    to_columns_back, to_columns = dft_tables(lon_cols, lon_count, order.reshape(-1), valid.reshape(-1), 2)
    first_row = (GRID_ROWS - lat_rows) // 2
    slot_plane = (plane - jnp.arange(lat_count, dtype=jnp.int32)) % lat_count
    row = across[:, None] * rows_chip + jnp.arange(rows_chip, dtype=jnp.int32)[None, :]
    row = (slot_plane[:, None] * rows_dev + row.reshape(1, -1)).reshape(-1)
    colatitude = (row.astype(jnp.float32) + (first_row + 0.5)) * (math.pi / GRID_ROWS)
    lane = jnp.arange(128, dtype=jnp.int32)
    orders = (chip * modes_dev + jnp.minimum(lane, modes_dev - 1)).astype(jnp.float32)
    owners = plane * lon_count + across
    poly = legendre(
        owners * owned + first_degree,
        skip,
        orders,
        lane < modes_dev,
        jnp.cos(colatitude),
        jnp.sin(colatitude),
        owned * lat_count * lon_count,
        cut,
    )
    analysis, synthesis = block_tables(poly, CHUNKS * slots)
    own_row = plane * rows_dev + chip * rows_chip
    angle = (own_row + jnp.arange(rows_chip, dtype=jnp.int32)).astype(jnp.float32) + (first_row + 0.5)
    quadrature = jnp.sin(angle * (math.pi / GRID_ROWS)) * ((math.pi / GRID_ROWS) * (2.0 * math.pi / math.sqrt(lon_cols)))

    def by_plane(pieces):
        return [
            jnp.stack([piece[chunk * groups : (chunk + 1) * groups] for piece in pieces], 0) for chunk in range(CHUNKS)
        ]

    def by_chip(chunks):
        traded = [trade_pieces([chunk[k] for k in range(lon_count)]) for chunk in chunks]
        return [traded[chunk][k] for k in range(lon_count) for chunk in range(CHUNKS)]

    values = after(values, (poly, analysis))
    pieces = trade_pieces(enter(quadrature, to_modes, values, gain_one, shift_one, CHUNKS * groups))
    shards_in = by_plane(pieces)
    first, last, near_first, far_last = after(first_hop, pieces[1])
    second_hop = (near(last), far(first))
    third_hop = (far(near_first), near(far_last))
    late = {2: synthesis, 3: (second_hop, to_columns, to_modes_back, to_columns_back)}
    rows_in = gather_rows(shards_in, lambda step, own: late.get(step))
    weights = [first, near_first, second_hop[1], third_hop[0], last, second_hop[0], far_last, third_hop[1]]
    partial, coeffs = mix_forward(rows_in, analysis, synthesis, weights, cut)
    grads = trade(after(cotangent, (rows_in, weights)).reshape(by_row))
    grid = by_chip([scatter_rows(*chunk, gate=grads)[0] for chunk in partial])

    where = jnp.concatenate([crops[0], own_row[None], jnp.zeros((1,), jnp.int32)])
    *d_grid, output, d_skipped, sums = feed(
        where, grid, to_columns, to_modes_back, values, grads, gain_two, shift_two, w_up, b_up, w_down, b_down
    )
    bounds = crops[0]
    count_rows = jnp.minimum(bounds[1], own_row + rows_chip) - jnp.maximum(bounds[0], own_row)
    count_cols = jnp.minimum(bounds[3], lon_cols) - jnp.maximum(bounds[2], 0)
    valid_count = (jnp.maximum(count_rows, 0) * jnp.maximum(count_cols, 0)).astype(jnp.float32)
    count_row = sums.shape[0] - 1
    sums = sums + jnp.where(jnp.arange(sums.shape[0]) == count_row, valid_count, 0.0)[:, None]

    shards_back = by_plane(trade_pieces(d_grid))
    traded = []

    def gate(step, own):
        if step == 1:
            traded.append(trade(after(output, shards_back)))
        return traded[0] if step == 2 else None

    rows_back = gather_rows(shards_back, gate)
    output = traded[0].reshape(inputs.shape)
    level = PartSum(after(sums, shards_back))
    sums = level.chips(level.cores())
    rows_back[1] = after(rows_back[1], sums)
    d_partial, d_weights = mix_backward(rows_back, analysis, synthesis, weights, cut, coeffs)
    three, single = scatter_weights(d_weights)
    d_modes, midway = zip(*[scatter_rows(*chunk) for chunk in d_partial])
    plane_pieces = after(gathered(after(sums, midway), "lat"), d_modes)
    sum_pieces = gathered(sum(in_order(plane_pieces, "lat")), "lon")
    traded = by_chip(after(d_modes, single))
    double = finish_weight_sum(d_weights, three, (traded, sum_pieces))
    sums = level.share(sum_pieces)
    other_sums = swap_cores(sums)
    d_inputs, d_norm = leave(
        quadrature, traded, to_columns_back, values, after(d_skipped, other_sums), gain_one
    )
    sums = level.finish(sums, other_sums)
    d_norm = sum_over_planes(d_norm + swap_cores(d_norm))
    norm_pieces = gathered(d_norm, "lon")
    d_inputs = wide(trade(d_inputs)).reshape(inputs.shape)
    d_norm = sum(in_order(norm_pieces, "lon"))
    halves = sum_weights(d_weights, single, after(double, norm_pieces))
    others = [swap_cores(part) for part in halves]
    own_first = [jnp.where(core == 0, mine, other) for mine, other in zip(halves, others)]
    own_last = [jnp.where(core == 0, other, mine) for mine, other in zip(halves, others)]
    own_last[0] = own_last[0][2 * half - owned :]
    d_spectral = jnp.concatenate([wide(part) for part in own_first + own_last], 0)

    hidden = w_up.shape[1]
    d_up = jnp.concatenate([sums[j * width : j * width + width] for j in range(hidden // width)], 1)
    d_down = sums[hidden : 2 * hidden]
    vectors = sums[2 * hidden :]
    pieces = hidden // width
    d_up_bias = vectors[:pieces].reshape(-1)
    d_down_bias, d_gain_two, d_shift_two, first_moment, second_moment = [vectors[pieces + j] for j in range(5)]
    count = sums[count_row, 0]
    batch_mean = first_moment / count
    batch_var = second_moment / count - batch_mean * batch_mean
    new_mean = (1.0 - momentum) * run_mean + momentum * batch_mean
    new_var = (1.0 - momentum) * run_var + momentum * batch_var
    return (
        output,
        d_inputs,
        d_norm[0],
        d_norm[1],
        d_spectral,
        d_gain_two,
        d_shift_two,
        d_up,
        d_up_bias,
        d_down,
        d_down_bias,
        new_mean,
        new_var,
    )


def fourier_tables(points, modes):
    column = jnp.arange(points, dtype=jnp.int32)
    order = jnp.arange(modes, dtype=jnp.int32)
    phase = column[:, None] * order[None, :] % points
    angle = phase.astype(jnp.float32) * (2.0 * math.pi / points)
    cosine = jnp.cos(angle)
    sine = jnp.sin(angle)
    scale = 1.0 / math.sqrt(points)
    forward_tab = jnp.stack([cosine * scale, -sine * scale], 1)
    factor = jnp.where(order == 0, 1.0, 2.0).astype(jnp.float32)
    inverse_tab = jnp.stack([(cosine * factor[None, :]).T, (-sine * factor[None, :]).T], 0)
    return (forward_tab.astype(jnp.bfloat16), inverse_tab.astype(jnp.bfloat16))


def grid_angles(rows_total):
    first_row = (GRID_ROWS - rows_total) // 2
    colatitude = (jnp.arange(rows_total, dtype=jnp.float32) + (first_row + 0.5)) * (
        math.pi / GRID_ROWS
    )
    return (jnp.cos(colatitude), jnp.sin(colatitude))


def legendre_scan(orders, cosines, sine_vals, degrees):
    order_col = orders[:, None]
    cos_row = cosines[None, :]
    log_start = 0.5 * (
        jnp.log((2.0 * order_col + 1.0) / (4.0 * math.pi))
        + lax.lgamma(order_col + 0.5)
        - lax.lgamma(order_col + 1.0)
        - 0.5 * math.log(math.pi)
    ) + order_col * jnp.log(sine_vals[None, :])
    diagonal_start = jnp.exp(log_start)
    second_start = cos_row * jnp.sqrt(2.0 * order_col + 3.0) * diagonal_start
    zeros_grid = jnp.zeros_like(diagonal_start)

    def advance(state, degree):
        before, latest = state
        upper_ratio = jnp.sqrt(
            (4.0 * degree * degree - 1.0)
            / jnp.maximum(degree * degree - order_col * order_col, 1.0)
        )
        lower_ratio = jnp.sqrt(
            jnp.maximum((degree - 1.0) * (degree - 1.0) - order_col * order_col, 0.0)
            / jnp.maximum(4.0 * (degree - 1.0) * (degree - 1.0) - 1.0, 1.0)
        )
        general = upper_ratio * (cos_row * latest - lower_ratio * before)
        current = jnp.where(
            degree < order_col,
            0.0,
            jnp.where(
                degree == order_col,
                diagonal_start,
                jnp.where(degree == order_col + 1.0, second_start, general),
            ),
        )
        return ((latest, current), current)

    ignored, stacked = lax.scan(
        advance, (zeros_grid, zeros_grid), jnp.arange(degrees).astype(cosines.dtype)
    )
    stacked = jnp.transpose(stacked, (1, 0, 2))
    degree_index = jnp.arange(degrees).astype(cosines.dtype)
    keep = (orders[:, None, None] < M) & (degree_index[None, :, None] < L)
    return jnp.where(keep, stacked, 0.0)


def mix_modes(coeffs, spectral):
    product = jnp.einsum("bmlrc,lscd->bmlrsd", coeffs, spectral, preferred_element_type=jnp.float32)
    real_part = product[:, :, :, 0, 0] - product[:, :, :, 1, 1]
    imag_part = product[:, :, :, 0, 1] + product[:, :, :, 1, 0]
    return jnp.stack([real_part, imag_part], 3).astype(jnp.bfloat16)


def coeff_back(d_mixed, spectral):
    returned = jnp.einsum(
        "bmlsd,lrcd->bmlsrc", d_mixed, spectral, preferred_element_type=jnp.float32
    )
    d_real = returned[:, :, :, 0, 0] + returned[:, :, :, 1, 1]
    d_imag = returned[:, :, :, 1, 0] - returned[:, :, :, 0, 1]
    return jnp.stack([d_real, d_imag], 3).astype(jnp.bfloat16)


def weight_back(coeffs, d_mixed):
    outer_sum = jnp.einsum(
        "bmlrc,bmlsd->lrscd", coeffs, d_mixed, preferred_element_type=jnp.float32
    )
    d_weight_real = outer_sum[:, 0, 0] + outer_sum[:, 1, 1]
    d_weight_imag = outer_sum[:, 0, 1] - outer_sum[:, 1, 0]
    return jnp.stack([d_weight_real, d_weight_imag], 1)


def degree_shards(
    inputs,
    gain_one,
    shift_one,
    spectral,
    gain_two,
    shift_two,
    w_up,
    b_up,
    w_down,
    b_down,
    crops,
    cotangent,
    run_mean,
    run_var,
    momentum,
):
    lat_count = lax.axis_size("lat")
    lon_count = lax.axis_size("lon")
    rows_dev = inputs.shape[1]
    cols_dev = inputs.shape[2]
    width = inputs.shape[3]
    lat_rows = rows_dev * lat_count
    lon_cols = cols_dev * lon_count
    modes_dev = (M + lat_count - 1) // lat_count
    modes_all = modes_dev * lat_count
    quarter = width // lon_count
    owned = spectral.shape[0]
    degrees_all = owned * lat_count * lon_count
    forward_tab, inverse_tab = fourier_tables(lon_cols, modes_all)
    cosines, sine_vals = grid_angles(lat_rows)
    orders = (lax.axis_index("lat") * modes_dev + jnp.arange(modes_dev, dtype=jnp.int32)).astype(
        jnp.float32
    )
    poly = legendre_scan(orders, cosines, sine_vals, degrees_all)
    quadrature = sine_vals * (math.pi / GRID_ROWS) * (2.0 * math.pi / math.sqrt(lon_cols))
    analysis = (poly * quadrature[None, None, :]).astype(jnp.bfloat16)
    synthesis = (
        poly.astype(jnp.bfloat16)
        .reshape(modes_dev, lat_count, lon_count, owned, lat_rows)
        .transpose(0, 2, 1, 3, 4)
    )
    input_wide = inputs.astype(jnp.float32)
    normed_one, norm_one_back = jax.vjp(layer_norm, input_wide, gain_one, shift_one)
    normed_low = normed_one.astype(jnp.bfloat16)
    fourier = jnp.einsum(
        "bijc,jrm->birmc",
        lax.all_to_all(normed_low, "lon", split_axis=3, concat_axis=2, tiled=True),
        forward_tab,
        preferred_element_type=jnp.float32,
    ).astype(jnp.bfloat16)
    portion = lax.all_to_all(fourier, "lat", split_axis=3, concat_axis=1, tiled=True)
    coeffs = jnp.einsum(
        "mli,birmc->bmlrc", analysis, portion, preferred_element_type=jnp.float32
    ).astype(jnp.bfloat16)
    coeffs = coeffs.reshape(1, modes_dev, lat_count, lon_count, owned, 2, portion.shape[4])
    owned_coeffs = lax.all_to_all(
        lax.all_to_all(coeffs, "lat", split_axis=2, concat_axis=1, tiled=True),
        "lon",
        split_axis=3,
        concat_axis=6,
        tiled=True,
    )
    coeffs_owned = owned_coeffs.reshape(1, modes_all, owned, 2, width)
    mixed_modes = mix_modes(coeffs_owned, spectral).reshape(1, modes_all, 1, 1, owned, 2, width)
    returned = lax.all_to_all(
        lax.all_to_all(mixed_modes, "lat", split_axis=1, concat_axis=3, tiled=True),
        "lon",
        split_axis=6,
        concat_axis=2,
        tiled=True,
    )
    grid_modes = jnp.einsum(
        "mjkqi,bmjkqrc->birmc", synthesis, returned, preferred_element_type=jnp.float32
    ).astype(jnp.bfloat16)
    spread = jnp.einsum(
        "birmc,rmj->bijc",
        lax.all_to_all(grid_modes, "lat", split_axis=1, concat_axis=3, tiled=True),
        inverse_tab,
        preferred_element_type=jnp.float32,
    ).astype(jnp.bfloat16)
    spectral_out = lax.all_to_all(spread, "lon", split_axis=2, concat_axis=3, tiled=True)
    skipped = input_wide + spectral_out.astype(jnp.float32)
    normed_two, norm_two_back = jax.vjp(layer_norm, skipped, gain_two, shift_two)
    normed_two_low = normed_two.astype(jnp.bfloat16)
    preact = (
        jnp.einsum("bijc,ch->bijh", normed_two_low, w_up, preferred_element_type=jnp.float32) + b_up
    )
    activated, gelu_back = jax.vjp(jax.nn.gelu, preact)
    activated_low = activated.astype(jnp.bfloat16)
    result = (
        skipped
        + jnp.einsum("bijh,hc->bijc", activated_low, w_down, preferred_element_type=jnp.float32)
        + b_down
    )
    output = result.astype(jnp.bfloat16)
    bounds = crops[0]
    row_global = lax.axis_index("lat") * rows_dev + jnp.arange(rows_dev, dtype=jnp.int32)
    col_global = lax.axis_index("lon") * cols_dev + jnp.arange(cols_dev, dtype=jnp.int32)
    inside_rows = (row_global >= bounds[0]) & (row_global < bounds[1])
    inside_cols = (col_global >= bounds[2]) & (col_global < bounds[3])
    mask_grid = (inside_rows[:, None] & inside_cols[None, :]).astype(jnp.float32)[None, :, :, None]
    valid_count = jnp.sum(mask_grid)
    first_moment = jnp.sum(mask_grid * result, (0, 1, 2))
    second_moment = jnp.sum(mask_grid * result * result, (0, 1, 2))
    grad_wide = cotangent.astype(jnp.float32)
    d_down = jnp.einsum(
        "bijh,bijc->hc", activated_low, cotangent, preferred_element_type=jnp.float32
    )
    d_down_bias = jnp.sum(grad_wide, (0, 1, 2))
    d_activated = jnp.einsum("bijc,hc->bijh", cotangent, w_down, preferred_element_type=jnp.float32)
    d_preact = gelu_back(d_activated)[0].astype(jnp.bfloat16)
    d_up = jnp.einsum("bijc,bijh->ch", normed_two_low, d_preact, preferred_element_type=jnp.float32)
    d_up_bias = jnp.sum(d_preact.astype(jnp.float32), (0, 1, 2))
    d_normed_two = jnp.einsum("bijh,ch->bijc", d_preact, w_up, preferred_element_type=jnp.float32)
    d_skipped, d_gain_two, d_shift_two = norm_two_back(d_normed_two)
    d_skipped = d_skipped + grad_wide
    d_spread = d_skipped.astype(jnp.bfloat16)
    d_grid = jnp.einsum(
        "bijc,rmj->birmc",
        lax.all_to_all(d_spread, "lon", split_axis=3, concat_axis=2, tiled=True),
        inverse_tab,
        preferred_element_type=jnp.float32,
    ).astype(jnp.bfloat16)
    d_returned = jnp.einsum(
        "mjkqi,birmc->bmjkqrc",
        synthesis,
        lax.all_to_all(d_grid, "lat", split_axis=3, concat_axis=1, tiled=True),
        preferred_element_type=jnp.float32,
    ).astype(jnp.bfloat16)
    d_mixed = lax.all_to_all(
        lax.all_to_all(d_returned, "lat", split_axis=3, concat_axis=1, tiled=True),
        "lon",
        split_axis=2,
        concat_axis=6,
        tiled=True,
    ).reshape(1, modes_all, owned, 2, width)
    d_coeffs = coeff_back(d_mixed, spectral)
    d_spectral = lax.psum(weight_back(coeffs_owned, d_mixed).astype(jnp.bfloat16), "batch").astype(
        jnp.float32
    )
    d_coeffs_wide = d_coeffs.reshape(1, modes_all, 1, 1, owned, 2, width)
    d_modes = lax.all_to_all(
        lax.all_to_all(d_coeffs_wide, "lat", split_axis=1, concat_axis=2, tiled=True),
        "lon",
        split_axis=6,
        concat_axis=3,
        tiled=True,
    ).reshape(1, modes_dev, degrees_all, 2, quarter)
    d_fourier = jnp.einsum(
        "mli,bmlrc->birmc", analysis, d_modes, preferred_element_type=jnp.float32
    ).astype(jnp.bfloat16)
    d_columns = jnp.einsum(
        "birmc,jrm->bijc",
        lax.all_to_all(d_fourier, "lat", split_axis=1, concat_axis=3, tiled=True),
        forward_tab,
        preferred_element_type=jnp.float32,
    ).astype(jnp.bfloat16)
    d_normed_one = lax.all_to_all(d_columns, "lon", split_axis=2, concat_axis=3, tiled=True).astype(
        jnp.float32
    )
    d_input_norm, d_gain_one, d_shift_one = norm_one_back(d_normed_one)
    d_inputs = d_input_norm + d_skipped
    summed = lax.psum(
        (
            d_up,
            d_down,
            d_up_bias,
            d_down_bias,
            d_gain_one,
            d_shift_one,
            d_gain_two,
            d_shift_two,
            valid_count,
            first_moment,
            second_moment,
        ),
        ("lat", "lon", "batch"),
    )
    batch_mean = summed[9] / summed[8]
    batch_var = summed[10] / summed[8] - batch_mean * batch_mean
    new_mean = (1.0 - momentum) * run_mean + momentum * batch_mean
    new_var = (1.0 - momentum) * run_var + momentum * batch_var
    return (
        output,
        d_inputs,
        summed[4],
        summed[5],
        d_spectral,
        summed[6],
        summed[7],
        summed[0],
        summed[2],
        summed[1],
        summed[3],
        new_mean,
        new_var,
    )


def shards(inputs, *rest):
    rows_dev = inputs.shape[1]
    lon_count = lax.axis_size("lon")
    banded = (
        lon_count == 4
        and lax.axis_size("batch") == 2
        and rows_dev == 2 * lon_count
        and M % lon_count == 0
        and M // lon_count <= 128
        and rest[2].shape[0] % 4 in (0, 3)
        and rows_dev * lax.axis_size("lat") <= 32
    )
    return (band_shards if banded else degree_shards)(inputs, *rest)


def solution(mesh):
    return jax.shard_map(
        shards,
        mesh=mesh,
        in_specs=(
            P("batch", "lat", "lon", None),
            P(),
            P(),
            P(("lat", "lon"), None, None, None),
            P(),
            P(),
            P(),
            P(),
            P(),
            P(),
            P("batch", None),
            P("batch", "lat", "lon", None),
            P(),
            P(),
            P(),
        ),
        out_specs=(
            P("batch", "lat", "lon", None),
            P("batch", "lat", "lon", None),
            P(),
            P(),
            P(("lat", "lon"), None, None, None),
            P(),
            P(),
            P(),
            P(),
            P(),
            P(),
            P(),
            P(),
        ),
        check_vma=False,
    )
```

```python
import math

import jax
import jax.numpy as jnp
from jax import lax
from jax.experimental import pallas as pl
from jax.experimental.pallas import tpu as pltpu
from jax.sharding import PartitionSpec as P

GRID_ROWS = 360
M = 360
L = 360


epsilon = 1e-05
GROUP = 8
CHUNKS = 2
PER_STEP = 6


def layer_norm(values, gain, shift):
    centre = values - jnp.mean(values, -1, keepdims=True)
    spread = jnp.mean(centre * centre, -1, keepdims=True)
    return centre * lax.rsqrt(spread + epsilon) * gain + shift


def xor_pairs(count, bit):
    return [(i, i ^ bit) for i in range(count)]


def ring_pairs(count, step):
    return [(i, (i + step) % count) for i in range(count)]


def swap_cores(values):
    return lax.ppermute(values, "batch", xor_pairs(2, 1))


def near(values):
    return lax.ppermute(values, "lon", xor_pairs(4, 1))


def far(values):
    return lax.ppermute(values, "lon", xor_pairs(4, 2))


def after(values, earlier):
    return lax.optimization_barrier((values, earlier))[0]


def trade(values):
    return lax.all_to_all(values, "lon", split_axis=0, concat_axis=0, tiled=True)


def cross(values, k):
    return lax.ppermute(values, "lon", xor_pairs(4, k))


def trade_pieces(pieces):
    return [pieces[0]] + [cross(pieces[k], k) for k in (1, 2, 3)]


def gathered(values, name):
    count = lax.axis_size(name)
    pairs = xor_pairs if name == "lon" else ring_pairs
    return [values] + [lax.ppermute(values, name, pairs(count, k)) for k in range(1, count)]


def in_order(pieces, name):
    at, count = lax.axis_index(name), len(pieces)
    pieces = jnp.stack(pieces, 0)
    where = lambda place: at ^ place if name == "lon" else (at - place) % count
    return [lax.dynamic_index_in_dim(pieces, where(place), 0, keepdims=False) for place in range(count)]


def sum_over_planes(values):
    return sum(in_order(gathered(values, "lat"), "lat"))


def dot(a, b):
    return jnp.dot(a, b, preferred_element_type=jnp.float32)


def dot_along(a, b):
    return lax.dot_general(a, b, (((1,), (1,)), ((), ())), preferred_element_type=jnp.float32)


def dot_across(a, b):
    return lax.dot_general(a, b, (((0,), (0,)), ((), ())), preferred_element_type=jnp.float32)


def low(values):
    return values.astype(jnp.bfloat16)


def wide(values):
    return values.astype(jnp.float32)


NO_COST = pl.CostEstimate(flops=0, transcendentals=0, bytes_accessed=0)


def params(megabytes):
    return pltpu.CompilerParams(vmem_limit_bytes=megabytes * 2**20)


def turned(cosine, sine, quarter_turns):
    turns = quarter_turns % 4
    real = jnp.where(turns == 0, cosine, jnp.where(turns == 1, -sine, jnp.where(turns == 2, -cosine, sine)))
    imag = jnp.where(turns == 0, -sine, jnp.where(turns == 1, -cosine, jnp.where(turns == 2, sine, cosine)))
    return real, imag


def dft_tables(points, parts, order, valid, axis):
    cols = points // parts
    column = jnp.arange(cols, dtype=jnp.int32)
    if axis == 1:
        order, valid, column = order[:, None], valid[:, None], column[None, :]
    else:
        order, valid, column = order[None, :], valid[None, :], column[:, None]
    angle = (order * column % points).astype(jnp.float32) * (2.0 * math.pi / points)
    cosine = jnp.where(valid, jnp.cos(angle), 0.0)
    sine = jnp.where(valid, jnp.sin(angle), 0.0)
    cosine, sine = lax.optimization_barrier((cosine, sine))
    part = jnp.arange(parts, dtype=jnp.int32)[:, None, None]
    real, imag = turned(cosine[None], sine[None], part * order[None])
    scales = (1.0 / math.sqrt(points), jnp.where(order == 0, 1.0, 2.0)[None])
    return [jnp.concatenate([low(real * scale), low(imag * scale)], axis) for scale in scales]


def legendre_kernel(cut, starts_ref, upper_ref, lower_ref, order_ref, cos_ref, diag_ref, second_ref, out_ref, all_ref):
    degrees = all_ref.shape[0]
    cosines = cos_ref[...]
    diagonal = diag_ref[...]
    second = second_ref[...]
    order = order_ref[...]

    def advance(degree, state):
        before, latest = state
        level = degree.astype(jnp.float32)
        upper = upper_ref[pl.ds(degree, 1), :]
        lower = lower_ref[pl.ds(degree, 1), :]
        general = upper * (cosines * latest - lower * before)
        current = jnp.where(
            level < order,
            0.0,
            jnp.where(level == order, diagonal, jnp.where(level == order + 1.0, second, general)),
        )
        all_ref[pl.ds(degree, 1)] = current[None]
        return latest, current

    unroll = 8 if degrees % 8 == 0 else 1

    def several(step, state):
        for at in range(unroll):
            state = advance(step * unroll + at, state)
        return state

    zeros = cosines * 0.0
    lax.fori_loop(0, degrees // unroll, several, (zeros, zeros))
    blocks = out_ref.shape[0] // (2 * cut)
    for block in range(blocks):
        for half in range(2):

            def copy(at, carry, block=block, half=half):
                degree = starts_ref[block] + half * cut + at
                value = all_ref[pl.ds(degree, 1)]
                keep = (degree < L) & (half * cut + at >= starts_ref[blocks])
                out_ref[pl.ds((at * 2 + half) * blocks + block, 1)] = jnp.where(keep, value, 0.0)
                return carry

            lax.fori_loop(0, cut, copy, 0)


def legendre(starts, skip, orders, valid, cosines, sine_vals, degrees, cut):
    order_row = orders[None, :]
    sine_col = sine_vals[:, None]
    log_start = 0.5 * (
        jnp.log((2.0 * order_row + 1.0) / (4.0 * math.pi))
        + lax.lgamma(order_row + 0.5)
        - lax.lgamma(order_row + 1.0)
        - 0.5 * math.log(math.pi)
    ) + order_row * jnp.log(sine_col)
    diagonal = jnp.where(valid[None, :], jnp.exp(log_start), 0.0)
    second = cosines[:, None] * jnp.sqrt(2.0 * order_row + 3.0) * diagonal
    degree = jnp.arange(degrees, dtype=jnp.float32)[:, None]
    upper = jnp.sqrt((4.0 * degree * degree - 1.0) / jnp.maximum(degree * degree - order_row * order_row, 1.0))
    lower = jnp.sqrt(
        jnp.maximum((degree - 1.0) * (degree - 1.0) - order_row * order_row, 0.0)
        / jnp.maximum(4.0 * (degree - 1.0) * (degree - 1.0) - 1.0, 1.0)
    )
    shape = diagonal.shape
    return pl.pallas_call(
        lambda *refs: legendre_kernel(cut, *refs),
        out_shape=jax.ShapeDtypeStruct((starts.shape[0] * 2 * cut,) + shape, jnp.float32),
        in_specs=[pl.BlockSpec(memory_space=pltpu.SMEM)] + [pl.BlockSpec(memory_space=pltpu.VMEM)] * 6,
        out_specs=pl.BlockSpec(memory_space=pltpu.VMEM),
        scratch_shapes=[pltpu.VMEM((degrees,) + shape, jnp.float32)],
        cost_estimate=NO_COST,
        compiler_params=params(24),
        name="legendre",
    )(
        jnp.concatenate([starts, skip[None]]).astype(jnp.int32),
        upper,
        lower,
        jnp.broadcast_to(order_row, shape),
        jnp.broadcast_to(cosines[:, None], shape),
        diagonal,
        second,
    )


def block_tables(poly, slots):
    degrees, rows, _ = poly.shape
    groups = slots // GROUP
    values = low(poly[:, :, :slots]).reshape(degrees, rows, groups, GROUP)

    def expand(table, depth):
        lanes = depth * GROUP
        lane = jnp.arange(lanes, dtype=jnp.int32)
        repeat = low(jnp.arange(depth, dtype=jnp.int32)[:, None] == lane[None, :] // GROUP)
        flat = table.reshape(-1, depth)
        row = jnp.arange(flat.shape[0], dtype=jnp.int32)
        same = row[:, None] % GROUP == lane[None, :] % GROUP
        return low(jnp.where(same, dot(flat, repeat), 0.0)).reshape(groups, -1, lanes)

    return expand(values.transpose(2, 0, 3, 1), rows), expand(values.transpose(2, 1, 3, 0), degrees)


def normalise(values):
    centre = values - jnp.mean(values, -1, keepdims=True)
    factor = lax.rsqrt(jnp.mean(centre * centre, -1, keepdims=True) + epsilon)
    return centre * factor, factor


def normalise_back(normal, factor, grad):
    return factor * (
        grad - jnp.mean(grad, -1, keepdims=True) - normal * jnp.mean(grad * normal, -1, keepdims=True)
    )


def column_sum(values):
    return jnp.sum(values, 0, keepdims=True)


def store_modes(totals, refs):
    groups, _, double = refs[0].shape
    width = double // 2
    slots = groups * GROUP
    for part in range(2):
        for owner, ref in enumerate(refs):
            at = (part * len(refs) + owner) * slots
            rows = [total[at : at + slots].reshape(groups, GROUP, width) for total in totals]
            ref[:, :, part * width : part * width + width] = low(jnp.concatenate(rows, 1))


def load_modes(refs, flat_ref):
    groups, _, double = refs[0].shape
    width = double // 2
    slots = groups * GROUP
    rows = flat_ref.shape[0]
    half = flat_ref.shape[1] // 2
    for piece, ref in enumerate(refs):
        owner, chunk = piece // CHUNKS, piece % CHUNKS
        at = (owner * CHUNKS + chunk) * slots
        modes = wide(ref[...]).reshape(groups, rows, GROUP, double)
        for row in range(rows):
            flat = low(modes[:, row].reshape(slots, double))
            flat_ref[row, at : at + slots] = flat[:, :width]
            flat_ref[row, half + at : half + at + slots] = flat[:, width:]


def whole_spec(array):
    return pl.BlockSpec(array.shape, lambda *at: (0,) * len(array.shape))


def enter_kernel(weight_ref, table_ref, values_ref, gain_ref, shift_ref, *out_refs):
    totals = []
    for row in range(values_ref.shape[1]):
        total = 0.0
        for part in range(table_ref.shape[0]):
            normal, _ = normalise(wide(values_ref[part, row]))
            total += dot(table_ref[part], low(normal * gain_ref[...] + shift_ref[...]))
        totals.append(total * weight_ref[row])
    store_modes(totals, out_refs)


def enter(weight, table, values, gain, shift, groups):
    parts, rows, cols, width = values.shape
    arrays = [table, values, gain[None], shift[None]]
    return pl.pallas_call(
        enter_kernel,
        out_shape=[jax.ShapeDtypeStruct((groups, rows * GROUP, 2 * width), jnp.bfloat16)] * parts,
        in_specs=[pl.BlockSpec(memory_space=pltpu.SMEM)] + [pl.BlockSpec(memory_space=pltpu.VMEM)] * 4,
        out_specs=[pl.BlockSpec(memory_space=pltpu.VMEM)] * parts,
        cost_estimate=NO_COST,
        compiler_params=params(32),
        name="enter",
    )(weight, *arrays)


def gelu_parts(values):
    slope = math.sqrt(2.0 / math.pi)
    square = values * values
    tangent = jnp.tanh(slope * values * (1.0 + 0.044715 * square))
    half = 0.5 * (1.0 + tangent)
    grad = half + 0.5 * values * (1.0 - tangent * tangent) * slope * (1.0 + 3.0 * 0.044715 * square)
    return values * half, grad


def feed_kernel(pieces, where_ref, *refs):
    modes_refs, refs = refs[:pieces], refs[pieces:]
    (columns_ref, modes_table_ref, values_ref, cotangent_ref), refs = refs[:4], refs[4:]
    (gain_ref, shift_ref, up_ref, up_bias_ref, down_ref, down_bias_ref), refs = refs[:6], refs[6:]
    *grid_refs, output_ref, d_skipped_ref, sums_ref, flat_ref, total_ref = refs
    row, part = pl.program_id(0), pl.program_id(1)
    rows, parts = pl.num_programs(0), pl.num_programs(1)
    width = values_ref.shape[-1]
    cols = values_ref.shape[-2]
    hidden = up_ref.shape[-1]

    @pl.when((part == 0) & (row == 0))
    def _():
        load_modes(modes_refs, flat_ref)
        sums_ref[...] = jnp.zeros_like(sums_ref)

    spread = low(dot(columns_ref[0], flat_ref[row]))
    skipped = wide(values_ref[0, 0]) + wide(spread)
    normal, factor = normalise(skipped)
    normed = low(normal * gain_ref[...] + shift_ref[...])
    activated, slope = gelu_parts(dot(normed, up_ref[...]) + up_bias_ref[...])
    activated = low(activated)
    result = skipped + dot(activated, down_ref[...]) + down_bias_ref[...]
    output_ref[0, 0] = low(result)
    row_at = where_ref[4] + row
    column_at = where_ref[5] + part * cols + lax.broadcasted_iota(jnp.int32, (cols, 1), 0)
    inside = (column_at >= where_ref[2]) & (column_at < where_ref[3])
    inside = inside & (row_at >= where_ref[0]) & (row_at < where_ref[1])
    kept = jnp.where(inside, result, 0.0)

    cotangent = cotangent_ref[0, 0]
    d_preact = low(dot_along(cotangent, down_ref[...]) * slope)
    d_normed = dot_along(d_preact, up_ref[...])
    d_skipped = wide(cotangent) + normalise_back(normal, factor, d_normed * gain_ref[...])
    d_skipped_ref[0, 0] = d_skipped
    term = dot(modes_table_ref[0], low(d_skipped))

    @pl.when(part == 0)
    def _():
        total_ref[row] = term

    @pl.when(part > 0)
    def _():
        total_ref[row] += term

    @pl.when((part == parts - 1) & (row == rows - 1))
    def _():
        store_modes([total_ref[at] for at in range(total_ref.shape[0])], grid_refs)

    d_up = dot_across(normed, d_preact)
    for at in range(hidden // width):
        sums_ref[at * width : at * width + width] += d_up[:, at * width : at * width + width]
    sums_ref[hidden : 2 * hidden] += dot_across(activated, cotangent)
    at = 2 * hidden
    d_bias = column_sum(wide(d_preact))
    vectors = [d_bias[:, j * width : j * width + width] for j in range(hidden // width)] + [
        column_sum(wide(cotangent)),
        column_sum(d_normed * normal),
        column_sum(d_normed),
        column_sum(kept),
        column_sum(kept * kept),
    ]
    for j, vector in enumerate(vectors):
        sums_ref[at + j : at + j + 1] += vector


def feed(where, modes, columns, modes_table, values, cotangent, gain, shift, w_up, b_up, w_down, b_down):
    parts, rows, cols, width = values.shape
    hidden = w_up.shape[1]
    lanes = modes_table.shape[1]
    grid = (CHUNKS * modes[0].shape[0],) + modes[0].shape[1:]
    cells = pl.BlockSpec((1, 1, cols, width), lambda i, p: (p, i, 0, 0))
    by_part = lambda table: pl.BlockSpec((1,) + table.shape[1:], lambda i, p: (p, 0, 0))
    small = [gain[None], shift[None], w_up, b_up[None], w_down, b_down[None]]
    outs = [jax.ShapeDtypeStruct(grid, jnp.bfloat16)] * parts + [
        jax.ShapeDtypeStruct(values.shape, jnp.bfloat16),
        jax.ShapeDtypeStruct(values.shape, jnp.float32),
        jax.ShapeDtypeStruct(((2 * hidden + hidden // width + 5 + 63) // 64 * 64, width), jnp.float32),
    ]
    return pl.pallas_call(
        lambda *refs: feed_kernel(len(modes), *refs),
        grid=(rows, parts),
        out_shape=outs,
        in_specs=[pl.BlockSpec(memory_space=pltpu.SMEM)]
        + [whole_spec(m) for m in modes]
        + [by_part(columns), by_part(modes_table), cells, cells]
        + [whole_spec(v) for v in small],
        out_specs=[whole_spec(outs[0])] * parts + [cells, cells, whole_spec(outs[-1])],
        scratch_shapes=[pltpu.VMEM((rows, lanes, width), jnp.bfloat16), pltpu.VMEM((rows, lanes, width), jnp.float32)],
        cost_estimate=NO_COST,
        compiler_params=params(60),
        name="feed",
    )(where, *modes, columns, modes_table, values, cotangent, *small)


def leave_kernel(pieces, weight_ref, *refs):
    modes_refs, refs = refs[:pieces], refs[pieces:]
    columns_ref, values_ref, d_skipped_ref, gain_ref, out_ref, sums_ref, flat_ref = refs
    row, part = pl.program_id(0), pl.program_id(1)

    @pl.when((part == 0) & (row == 0))
    def _():
        load_modes(modes_refs, flat_ref)
        sums_ref[...] = jnp.zeros_like(sums_ref)

    d_normed = wide(low(dot(columns_ref[0], flat_ref[row]) * weight_ref[row]))
    normal, factor = normalise(wide(values_ref[0, 0]))
    out_ref[0, 0] = low(normalise_back(normal, factor, d_normed * gain_ref[...]) + d_skipped_ref[0, 0])
    sums_ref[0:1] += column_sum(d_normed * normal)
    sums_ref[1:2] += column_sum(d_normed)


def leave(weight, modes, columns, values, d_skipped, gain):
    parts, rows, cols, width = values.shape
    cells = pl.BlockSpec((1, 1, cols, width), lambda i, p: (p, i, 0, 0))
    return pl.pallas_call(
        lambda *refs: leave_kernel(len(modes), *refs),
        grid=(rows, parts),
        out_shape=[jax.ShapeDtypeStruct(values.shape, jnp.bfloat16), jax.ShapeDtypeStruct((8, width), jnp.float32)],
        in_specs=[pl.BlockSpec(memory_space=pltpu.SMEM)]
        + [whole_spec(m) for m in modes]
        + [
            pl.BlockSpec((1,) + columns.shape[1:], lambda i, p: (p, 0, 0)),
            cells,
            cells,
            pl.BlockSpec((1, width), lambda i, p: (0, 0)),
        ],
        out_specs=[cells, pl.BlockSpec((8, width), lambda i, p: (0, 0))],
        scratch_shapes=[pltpu.VMEM((rows, columns.shape[2], width), jnp.bfloat16)],
        cost_estimate=NO_COST,
        compiler_params=params(32),
        name="leave",
    )(weight, *modes, columns, values, d_skipped, gain[None])


def complex_weight(weight_ref):
    real, imag = weight_ref[0, 0], weight_ref[0, 1]
    return jnp.concatenate([jnp.concatenate([real, imag], 1), jnp.concatenate([-imag, real], 1)], 0)


class Core:
    def __init__(self, shard, slots, degrees, cut, rows, table, weights, back_table):
        self.slots, self.cut, self.degrees = slots, cut, degrees
        self.steps = shard[1] // PER_STEP
        ends = CHUNKS * self.steps
        self.first = ends if table is not None else 0
        self.last = ends if back_table is not None else 0
        self.grid = (self.first + cut + self.last,)
        self.modes = (degrees, CHUNKS * shard[1]) + shard[2:]
        self.per = degrees // cut
        block = (shard[0], PER_STEP) + shard[2:]
        place = lambda step, start, count: jnp.clip(step - start, 0, count - 1)
        self.middle = lambda s: place(s, self.first, cut)
        self.arrays, self.in_specs = [], []
        for chunk in range(CHUNKS if self.first else 0):
            spec = pl.BlockSpec(block, lambda s, chunk=chunk: (0, place(s, chunk * self.steps, self.steps), 0, 0))
            self.take([slot for sample in rows[chunk] for slot in sample], spec)
        if self.first:
            self.take([table], pl.BlockSpec((PER_STEP,) + table.shape[1:], lambda s: (place(s, 0, ends), 0, 0)))
        start = self.first + cut
        if self.last:
            spec = pl.BlockSpec((PER_STEP,) + back_table.shape[1:], lambda s: (place(s, start, ends), 0, 0))
            self.take([back_table], spec)
        self.take(weights, pl.BlockSpec((1,) + weights[0].shape[1:], lambda s: (self.middle(s), 0, 0, 0)))
        self.modes_spec = pl.BlockSpec((self.per,) + self.modes[1:], lambda s: (self.middle(s), 0, 0, 0))
        self.modes_shape = jax.ShapeDtypeStruct(self.modes, jnp.bfloat16)
        self.held = pltpu.VMEM(self.modes, jnp.bfloat16)
        self.out_specs, self.out_shape = [], []
        for chunk in range(CHUNKS if self.last else 0):
            at = lambda s, chunk=chunk: (0, 0, place(s, start + chunk * self.steps, self.steps), 0, 0)
            self.out_specs += [pl.BlockSpec((slots,) + block, at)] * 2
            self.out_shape += [jax.ShapeDtypeStruct((slots,) + shard, jnp.bfloat16)] * 2

    def take(self, arrays, spec):
        self.arrays += arrays
        self.in_specs += [spec] * len(arrays)

    def split(self, refs):
        at = CHUNKS * 2 * self.slots if self.first else 0
        shards, refs = refs[:at], refs[at:]
        table, refs = (refs[0], refs[1:]) if self.first else (None, refs)
        back_table, refs = (refs[0], refs[1:]) if self.last else (None, refs)
        count = len(self.arrays) - at - (table is not None) - (back_table is not None)
        return shards, table, back_table, refs[:count], refs[count:]

    def analyse(self, shard_refs, table_ref, held_ref):
        step = pl.program_id(0)
        for chunk in range(CHUNKS):
            refs = shard_refs[chunk * 2 * self.slots : (chunk + 1) * 2 * self.slots]

            @pl.when((step >= chunk * self.steps) & (step < (chunk + 1) * self.steps))
            def _(refs=refs):
                for at in range(PER_STEP):
                    samples = []
                    for sample in range(2):
                        rows = [flat_rows(ref[:, at]) for ref in refs[sample * self.slots : (sample + 1) * self.slots]]
                        total = dot(table_ref[at], jnp.concatenate(rows, 0))
                        samples.append(total.reshape(self.degrees, GROUP, -1))
                    held_ref[:, pl.ds(step * PER_STEP + at, 1)] = low(jnp.concatenate(samples, 1))[:, None]

    def synthesise(self, table_ref, held_ref, out_refs):
        step = pl.program_id(0) - self.first - self.cut
        for chunk in range(CHUNKS):
            refs = out_refs[2 * chunk : 2 * chunk + 2]

            @pl.when((step >= chunk * self.steps) & (step < (chunk + 1) * self.steps))
            def _(refs=refs):
                for at in range(PER_STEP):
                    modes = wide(held_ref[:, pl.ds(step * PER_STEP + at, 1)])
                    modes = modes.reshape(self.degrees, 2, GROUP, modes.shape[-1])
                    for sample, ref in enumerate(refs):
                        total = low(dot(table_ref[at], low(flat_rows(modes[:, sample]))))
                        ref[:, :, at] = total.reshape(ref.shape[:2] + ref.shape[3:])

    def in_middle(self):
        step = pl.program_id(0)
        return (step >= self.first) & (step < self.first + self.cut)

    def degree(self, at):
        return self.middle(pl.program_id(0)) * self.per + at

    def chunks(self, out):
        return [out[2 * chunk : 2 * chunk + 2] for chunk in range(CHUNKS)]


def flat_rows(modes):
    return modes.reshape(-1, modes.shape[-1])


def mix_forward(rows, table, back_table, weights, cut):
    shard = rows[0][0][0].shape
    core = Core(shard, len(rows[0][0]), len(weights) * cut, cut, rows, table, weights, back_table)

    def kernel(*refs):
        shards, table, back_table, weight_refs, (*out_refs, coeffs_ref, held_ref, mixed_ref) = core.split(refs)
        core.analyse(shards, table, held_ref)

        @pl.when(core.in_middle())
        def _():
            for at, weight_ref in enumerate(weight_refs):
                coeffs = held_ref[core.degree(at)]
                coeffs_ref[at] = coeffs
                mixed = low(dot(flat_rows(coeffs), complex_weight(weight_ref)))
                mixed_ref[core.degree(at)] = mixed.reshape(coeffs.shape)

        core.synthesise(back_table, mixed_ref, out_refs)

    out = pl.pallas_call(
        kernel,
        grid=core.grid,
        out_shape=core.out_shape + [core.modes_shape],
        in_specs=core.in_specs,
        out_specs=core.out_specs + [core.modes_spec],
        scratch_shapes=[core.held, core.held],
        cost_estimate=NO_COST,
        compiler_params=params(60),
        name="mix_forward",
    )(*core.arrays)
    return core.chunks(out), out[-1]


def mix_backward(rows, table, back_table, weights, cut, coeffs):
    shard = rows[0][0][0].shape
    core = Core(shard, len(rows[0][0]), len(weights) * cut, cut, rows, table, weights, back_table)
    weight = weights[0].shape
    grad = pl.BlockSpec((1,) + weight[1:], lambda s: (core.middle(s), 0, 0, 0))

    def kernel(*refs):
        shards, table, back_table, weight_refs, (coeffs_ref, *outs, held_ref, mixed_ref) = core.split(refs)
        core.analyse(shards, table, held_ref)

        @pl.when(core.in_middle())
        def _():
            for at, (weight_ref, target) in enumerate(zip(weight_refs, outs[-len(weights) :])):
                d_mixed = held_ref[core.degree(at)]
                d_coeffs = low(dot_along(flat_rows(d_mixed), complex_weight(weight_ref)))
                mixed_ref[core.degree(at)] = d_coeffs.reshape(d_mixed.shape)
                width = target.shape[-1]
                left, right = flat_rows(coeffs_ref[at]), flat_rows(d_mixed)
                turned_right = jnp.concatenate([right[:, width:], -right[:, :width]], 1)
                total = dot_across(
                    jnp.concatenate([left[:, :width], left[:, width:]], 0), jnp.concatenate([right, turned_right], 0)
                )
                target[0, 0] = low(total[:, :width])
                target[0, 1] = low(total[:, width:])

        core.synthesise(back_table, mixed_ref, outs[: -len(weights)])

    out = pl.pallas_call(
        kernel,
        grid=core.grid,
        out_shape=core.out_shape + [jax.ShapeDtypeStruct(weight, jnp.bfloat16)] * len(weights),
        in_specs=core.in_specs + [core.modes_spec],
        out_specs=core.out_specs + [grad] * len(weights),
        scratch_shapes=[core.held, core.held],
        cost_estimate=NO_COST,
        compiler_params=params(60),
        name="mix_backward",
    )(*core.arrays, coeffs)
    return core.chunks(out), out[-len(weights) :]


def gather_rows(shards, gate):
    count = lax.axis_size("lat")
    own = [[shard] for shard in shards]
    for step in range(1, count):
        earlier = gate(step, own)
        sent = [rows[-1] for rows in own]
        if earlier is not None:
            sent[-1] = after(sent[-1], earlier)
        own = [rows + [lax.ppermute(rows_sent, "lat", ring_pairs(count, 1))] for rows, rows_sent in zip(own, sent)]
    return [(rows, [swap_cores(slot) for slot in rows]) for rows in own]


def scatter_rows(own, other, gate=None, sent=None):
    count = lax.axis_size("lat")
    other = swap_cores(other)
    arrived = None
    for slot in range(count - 1, -1, -1):
        total = wide(own[slot]) + wide(other[slot])
        if arrived is not None:
            total = total + wide(arrived)
        total = low(total)
        if slot == 1:
            midway = total
        if slot == count - 1 and sent is not None:
            sent.append(total)
        if slot > 0:
            arrived = lax.ppermute(total, "lat", ring_pairs(count, -1))
            if slot == 2 and gate is not None:
                arrived = after(arrived, gate)
    return total, midway


def gather_weights(own):
    cut = own.shape[0] // 2
    first, last = own[:cut], own[cut:]
    return first, last, near(first), far(last)


def scatter_weights(grads):
    three = near(grads[3]), far(grads[7])
    one, two = after((grads[1], grads[6]), three)
    return three, (near(one), far(two))


def finish_weight_sum(grads, three, gate):
    from_near, from_far = after(three, gate)
    return far(low(wide(grads[2]) + wide(from_near))), near(low(wide(grads[5]) + wide(from_far)))


def sum_weights(grads, single, double):
    first = low(wide(grads[0]) + wide(single[0]) + wide(double[0]))
    last = low(wide(grads[4]) + wide(single[1]) + wide(double[1]))
    return first, last


class PartSum:
    def __init__(self, values):
        core = lax.axis_index("batch")
        half = values.shape[0] // 2
        self.mine = lax.dynamic_slice_in_dim(values, core * half, half, 0)
        self.other = swap_cores(lax.dynamic_slice_in_dim(values, (1 - core) * half, half, 0))

    def cores(self):
        return self.mine + self.other

    def chips(self, values):
        chip = lax.axis_index("lon")
        part = values.shape[0] // 4
        for_chip = lambda k: lax.dynamic_slice_in_dim(values, (chip ^ k) * part, part, 0)
        return sum(trade_pieces([for_chip(k) for k in range(4)]))

    def share(self, pieces):
        return jnp.concatenate(in_order(pieces, "lon"), 0)

    def finish(self, mine, other):
        core = lax.axis_index("batch")
        return jnp.concatenate([jnp.where(core == 0, mine, other), jnp.where(core == 0, other, mine)], 0)


def band_shards(
    inputs,
    gain_one,
    shift_one,
    spectral,
    gain_two,
    shift_two,
    w_up,
    b_up,
    w_down,
    b_down,
    crops,
    cotangent,
    run_mean,
    run_var,
    momentum,
):
    lat_count = lax.axis_size("lat")
    lon_count = lax.axis_size("lon")
    plane = lax.axis_index("lat")
    chip = lax.axis_index("lon")
    core = lax.axis_index("batch")
    rows_dev = inputs.shape[1]
    cols_dev = inputs.shape[2]
    width = inputs.shape[3]
    rows_chip = rows_dev // lon_count
    lat_rows = rows_dev * lat_count
    lon_cols = cols_dev * lon_count
    modes_dev = M // lon_count
    slots = (modes_dev + CHUNKS * PER_STEP * GROUP - 1) // (CHUNKS * PER_STEP * GROUP) * PER_STEP * GROUP
    groups = slots // GROUP
    owned = spectral.shape[0]
    cut = (owned + 3) // 4
    half = 2 * cut
    first_degree = core * (owned - half)
    skip = core * (2 * half - owned)
    by_row = (lon_count, rows_chip, cols_dev, width)

    first_hop = gather_weights(lax.dynamic_slice_in_dim(spectral, first_degree, half, 0))
    values = trade(inputs.reshape(by_row))

    across = chip ^ jnp.arange(lon_count, dtype=jnp.int32)
    in_chip = jnp.arange(CHUNKS * slots, dtype=jnp.int32)
    first_order = across[:, None] * modes_dev + in_chip[None, :]
    valid = jnp.broadcast_to(in_chip[None, :] < modes_dev, first_order.shape)
    order = jnp.where(valid, first_order, 0)
    to_modes, to_modes_back = dft_tables(lon_cols, lon_count, order.reshape(-1), valid.reshape(-1), 1)
    to_columns_back, to_columns = dft_tables(lon_cols, lon_count, order.reshape(-1), valid.reshape(-1), 2)
    first_row = (GRID_ROWS - lat_rows) // 2
    slot_plane = (plane - jnp.arange(lat_count, dtype=jnp.int32)) % lat_count
    row = across[:, None] * rows_chip + jnp.arange(rows_chip, dtype=jnp.int32)[None, :]
    row = (slot_plane[:, None] * rows_dev + row.reshape(1, -1)).reshape(-1)
    colatitude = (row.astype(jnp.float32) + (first_row + 0.5)) * (math.pi / GRID_ROWS)
    lane = jnp.arange(128, dtype=jnp.int32)
    orders = (chip * modes_dev + jnp.minimum(lane, modes_dev - 1)).astype(jnp.float32)
    owners = plane * lon_count + across
    poly = legendre(
        owners * owned + first_degree,
        skip,
        orders,
        lane < modes_dev,
        jnp.cos(colatitude),
        jnp.sin(colatitude),
        owned * lat_count * lon_count,
        cut,
    )
    analysis, synthesis = block_tables(poly, CHUNKS * slots)
    own_row = plane * rows_dev + chip * rows_chip
    angle = (own_row + jnp.arange(rows_chip, dtype=jnp.int32)).astype(jnp.float32) + (first_row + 0.5)
    quadrature = jnp.sin(angle * (math.pi / GRID_ROWS)) * ((math.pi / GRID_ROWS) * (2.0 * math.pi / math.sqrt(lon_cols)))

    def by_plane(pieces):
        return [
            jnp.stack([piece[chunk * groups : (chunk + 1) * groups] for piece in pieces], 0) for chunk in range(CHUNKS)
        ]

    def by_chip(chunks):
        traded = [trade_pieces([chunk[k] for k in range(lon_count)]) for chunk in chunks]
        return [traded[chunk][k] for k in range(lon_count) for chunk in range(CHUNKS)]

    values = after(values, (poly, analysis))
    pieces = trade_pieces(enter(quadrature, to_modes, values, gain_one, shift_one, CHUNKS * groups))
    shards_in = by_plane(pieces)
    first, last, near_first, far_last = after(first_hop, pieces[1])
    second_hop = (near(last), far(first))
    third_hop = (far(near_first), near(far_last))
    late = {2: synthesis, 3: (second_hop, to_columns, to_modes_back, to_columns_back)}
    rows_in = gather_rows(shards_in, lambda step, own: late.get(step))
    weights = [first, near_first, second_hop[1], third_hop[0], last, second_hop[0], far_last, third_hop[1]]
    partial, coeffs = mix_forward(rows_in, analysis, synthesis, weights, cut)
    sent = []
    grid = [scatter_rows(*partial[0], sent=sent)[0]]
    grads = trade(after(cotangent, sent).reshape(by_row))
    grid = by_chip(grid + [scatter_rows(*chunk, gate=grads)[0] for chunk in partial[1:]])

    where = jnp.concatenate([crops[0], own_row[None], jnp.zeros((1,), jnp.int32)])
    *d_grid, output, d_skipped, sums = feed(
        where, grid, to_columns, to_modes_back, values, grads, gain_two, shift_two, w_up, b_up, w_down, b_down
    )
    bounds = crops[0]
    count_rows = jnp.minimum(bounds[1], own_row + rows_chip) - jnp.maximum(bounds[0], own_row)
    count_cols = jnp.minimum(bounds[3], lon_cols) - jnp.maximum(bounds[2], 0)
    valid_count = (jnp.maximum(count_rows, 0) * jnp.maximum(count_cols, 0)).astype(jnp.float32)
    count_row = sums.shape[0] - 1
    sums = sums + jnp.where(jnp.arange(sums.shape[0]) == count_row, valid_count, 0.0)[:, None]

    shards_back = by_plane(trade_pieces(d_grid))
    traded = []

    def gate(step, own):
        if step == 1:
            traded.append(trade(after(output, shards_back)))
        return traded[0] if step == 2 else None

    rows_back = gather_rows(shards_back, gate)
    output = traded[0].reshape(inputs.shape)
    level = PartSum(after(sums, shards_back))
    sums = level.chips(level.cores())
    rows_back[1] = after(rows_back[1], sums)
    d_partial, d_weights = mix_backward(rows_back, analysis, synthesis, weights, cut, coeffs)
    three, single = scatter_weights(d_weights)
    d_modes, midway = zip(*[scatter_rows(*chunk) for chunk in d_partial])
    plane_pieces = after(gathered(after(sums, midway), "lat"), d_modes)
    sum_pieces = gathered(sum(in_order(plane_pieces, "lat")), "lon")
    traded = by_chip(after(d_modes, single))
    double = finish_weight_sum(d_weights, three, (traded, sum_pieces))
    sums = level.share(sum_pieces)
    other_sums = swap_cores(sums)
    d_inputs, d_norm = leave(
        quadrature, traded, to_columns_back, values, after(d_skipped, other_sums), gain_one
    )
    sums = level.finish(sums, other_sums)
    d_norm = sum_over_planes(d_norm + swap_cores(d_norm))
    norm_pieces = gathered(d_norm, "lon")
    d_inputs = wide(trade(d_inputs)).reshape(inputs.shape)
    d_norm = sum(in_order(norm_pieces, "lon"))
    halves = sum_weights(d_weights, single, after(double, norm_pieces))
    others = [swap_cores(part) for part in halves]
    own_first = [jnp.where(core == 0, mine, other) for mine, other in zip(halves, others)]
    own_last = [jnp.where(core == 0, other, mine) for mine, other in zip(halves, others)]
    own_last[0] = own_last[0][2 * half - owned :]
    d_spectral = jnp.concatenate([wide(part) for part in own_first + own_last], 0)

    hidden = w_up.shape[1]
    d_up = jnp.concatenate([sums[j * width : j * width + width] for j in range(hidden // width)], 1)
    d_down = sums[hidden : 2 * hidden]
    vectors = sums[2 * hidden :]
    pieces = hidden // width
    d_up_bias = vectors[:pieces].reshape(-1)
    d_down_bias, d_gain_two, d_shift_two, first_moment, second_moment = [vectors[pieces + j] for j in range(5)]
    count = sums[count_row, 0]
    batch_mean = first_moment / count
    batch_var = second_moment / count - batch_mean * batch_mean
    new_mean = (1.0 - momentum) * run_mean + momentum * batch_mean
    new_var = (1.0 - momentum) * run_var + momentum * batch_var
    return (
        output,
        d_inputs,
        d_norm[0],
        d_norm[1],
        d_spectral,
        d_gain_two,
        d_shift_two,
        d_up,
        d_up_bias,
        d_down,
        d_down_bias,
        new_mean,
        new_var,
    )


def fourier_tables(points, modes):
    column = jnp.arange(points, dtype=jnp.int32)
    order = jnp.arange(modes, dtype=jnp.int32)
    phase = column[:, None] * order[None, :] % points
    angle = phase.astype(jnp.float32) * (2.0 * math.pi / points)
    cosine = jnp.cos(angle)
    sine = jnp.sin(angle)
    scale = 1.0 / math.sqrt(points)
    forward_tab = jnp.stack([cosine * scale, -sine * scale], 1)
    factor = jnp.where(order == 0, 1.0, 2.0).astype(jnp.float32)
    inverse_tab = jnp.stack([(cosine * factor[None, :]).T, (-sine * factor[None, :]).T], 0)
    return (forward_tab.astype(jnp.bfloat16), inverse_tab.astype(jnp.bfloat16))


def grid_angles(rows_total):
    first_row = (GRID_ROWS - rows_total) // 2
    colatitude = (jnp.arange(rows_total, dtype=jnp.float32) + (first_row + 0.5)) * (
        math.pi / GRID_ROWS
    )
    return (jnp.cos(colatitude), jnp.sin(colatitude))


def legendre_scan(orders, cosines, sine_vals, degrees):
    order_col = orders[:, None]
    cos_row = cosines[None, :]
    log_start = 0.5 * (
        jnp.log((2.0 * order_col + 1.0) / (4.0 * math.pi))
        + lax.lgamma(order_col + 0.5)
        - lax.lgamma(order_col + 1.0)
        - 0.5 * math.log(math.pi)
    ) + order_col * jnp.log(sine_vals[None, :])
    diagonal_start = jnp.exp(log_start)
    second_start = cos_row * jnp.sqrt(2.0 * order_col + 3.0) * diagonal_start
    zeros_grid = jnp.zeros_like(diagonal_start)

    def advance(state, degree):
        before, latest = state
        upper_ratio = jnp.sqrt(
            (4.0 * degree * degree - 1.0)
            / jnp.maximum(degree * degree - order_col * order_col, 1.0)
        )
        lower_ratio = jnp.sqrt(
            jnp.maximum((degree - 1.0) * (degree - 1.0) - order_col * order_col, 0.0)
            / jnp.maximum(4.0 * (degree - 1.0) * (degree - 1.0) - 1.0, 1.0)
        )
        general = upper_ratio * (cos_row * latest - lower_ratio * before)
        current = jnp.where(
            degree < order_col,
            0.0,
            jnp.where(
                degree == order_col,
                diagonal_start,
                jnp.where(degree == order_col + 1.0, second_start, general),
            ),
        )
        return ((latest, current), current)

    ignored, stacked = lax.scan(
        advance, (zeros_grid, zeros_grid), jnp.arange(degrees).astype(cosines.dtype)
    )
    stacked = jnp.transpose(stacked, (1, 0, 2))
    degree_index = jnp.arange(degrees).astype(cosines.dtype)
    keep = (orders[:, None, None] < M) & (degree_index[None, :, None] < L)
    return jnp.where(keep, stacked, 0.0)


def mix_modes(coeffs, spectral):
    product = jnp.einsum("bmlrc,lscd->bmlrsd", coeffs, spectral, preferred_element_type=jnp.float32)
    real_part = product[:, :, :, 0, 0] - product[:, :, :, 1, 1]
    imag_part = product[:, :, :, 0, 1] + product[:, :, :, 1, 0]
    return jnp.stack([real_part, imag_part], 3).astype(jnp.bfloat16)


def coeff_back(d_mixed, spectral):
    returned = jnp.einsum(
        "bmlsd,lrcd->bmlsrc", d_mixed, spectral, preferred_element_type=jnp.float32
    )
    d_real = returned[:, :, :, 0, 0] + returned[:, :, :, 1, 1]
    d_imag = returned[:, :, :, 1, 0] - returned[:, :, :, 0, 1]
    return jnp.stack([d_real, d_imag], 3).astype(jnp.bfloat16)


def weight_back(coeffs, d_mixed):
    outer_sum = jnp.einsum(
        "bmlrc,bmlsd->lrscd", coeffs, d_mixed, preferred_element_type=jnp.float32
    )
    d_weight_real = outer_sum[:, 0, 0] + outer_sum[:, 1, 1]
    d_weight_imag = outer_sum[:, 0, 1] - outer_sum[:, 1, 0]
    return jnp.stack([d_weight_real, d_weight_imag], 1)


def degree_shards(
    inputs,
    gain_one,
    shift_one,
    spectral,
    gain_two,
    shift_two,
    w_up,
    b_up,
    w_down,
    b_down,
    crops,
    cotangent,
    run_mean,
    run_var,
    momentum,
):
    lat_count = lax.axis_size("lat")
    lon_count = lax.axis_size("lon")
    rows_dev = inputs.shape[1]
    cols_dev = inputs.shape[2]
    width = inputs.shape[3]
    lat_rows = rows_dev * lat_count
    lon_cols = cols_dev * lon_count
    modes_dev = (M + lat_count - 1) // lat_count
    modes_all = modes_dev * lat_count
    quarter = width // lon_count
    owned = spectral.shape[0]
    degrees_all = owned * lat_count * lon_count
    forward_tab, inverse_tab = fourier_tables(lon_cols, modes_all)
    cosines, sine_vals = grid_angles(lat_rows)
    orders = (lax.axis_index("lat") * modes_dev + jnp.arange(modes_dev, dtype=jnp.int32)).astype(
        jnp.float32
    )
    poly = legendre_scan(orders, cosines, sine_vals, degrees_all)
    quadrature = sine_vals * (math.pi / GRID_ROWS) * (2.0 * math.pi / math.sqrt(lon_cols))
    analysis = (poly * quadrature[None, None, :]).astype(jnp.bfloat16)
    synthesis = (
        poly.astype(jnp.bfloat16)
        .reshape(modes_dev, lat_count, lon_count, owned, lat_rows)
        .transpose(0, 2, 1, 3, 4)
    )
    input_wide = inputs.astype(jnp.float32)
    normed_one, norm_one_back = jax.vjp(layer_norm, input_wide, gain_one, shift_one)
    normed_low = normed_one.astype(jnp.bfloat16)
    fourier = jnp.einsum(
        "bijc,jrm->birmc",
        lax.all_to_all(normed_low, "lon", split_axis=3, concat_axis=2, tiled=True),
        forward_tab,
        preferred_element_type=jnp.float32,
    ).astype(jnp.bfloat16)
    portion = lax.all_to_all(fourier, "lat", split_axis=3, concat_axis=1, tiled=True)
    coeffs = jnp.einsum(
        "mli,birmc->bmlrc", analysis, portion, preferred_element_type=jnp.float32
    ).astype(jnp.bfloat16)
    coeffs = coeffs.reshape(1, modes_dev, lat_count, lon_count, owned, 2, portion.shape[4])
    owned_coeffs = lax.all_to_all(
        lax.all_to_all(coeffs, "lat", split_axis=2, concat_axis=1, tiled=True),
        "lon",
        split_axis=3,
        concat_axis=6,
        tiled=True,
    )
    coeffs_owned = owned_coeffs.reshape(1, modes_all, owned, 2, width)
    mixed_modes = mix_modes(coeffs_owned, spectral).reshape(1, modes_all, 1, 1, owned, 2, width)
    returned = lax.all_to_all(
        lax.all_to_all(mixed_modes, "lat", split_axis=1, concat_axis=3, tiled=True),
        "lon",
        split_axis=6,
        concat_axis=2,
        tiled=True,
    )
    grid_modes = jnp.einsum(
        "mjkqi,bmjkqrc->birmc", synthesis, returned, preferred_element_type=jnp.float32
    ).astype(jnp.bfloat16)
    spread = jnp.einsum(
        "birmc,rmj->bijc",
        lax.all_to_all(grid_modes, "lat", split_axis=1, concat_axis=3, tiled=True),
        inverse_tab,
        preferred_element_type=jnp.float32,
    ).astype(jnp.bfloat16)
    spectral_out = lax.all_to_all(spread, "lon", split_axis=2, concat_axis=3, tiled=True)
    skipped = input_wide + spectral_out.astype(jnp.float32)
    normed_two, norm_two_back = jax.vjp(layer_norm, skipped, gain_two, shift_two)
    normed_two_low = normed_two.astype(jnp.bfloat16)
    preact = (
        jnp.einsum("bijc,ch->bijh", normed_two_low, w_up, preferred_element_type=jnp.float32) + b_up
    )
    activated, gelu_back = jax.vjp(jax.nn.gelu, preact)
    activated_low = activated.astype(jnp.bfloat16)
    result = (
        skipped
        + jnp.einsum("bijh,hc->bijc", activated_low, w_down, preferred_element_type=jnp.float32)
        + b_down
    )
    output = result.astype(jnp.bfloat16)
    bounds = crops[0]
    row_global = lax.axis_index("lat") * rows_dev + jnp.arange(rows_dev, dtype=jnp.int32)
    col_global = lax.axis_index("lon") * cols_dev + jnp.arange(cols_dev, dtype=jnp.int32)
    inside_rows = (row_global >= bounds[0]) & (row_global < bounds[1])
    inside_cols = (col_global >= bounds[2]) & (col_global < bounds[3])
    mask_grid = (inside_rows[:, None] & inside_cols[None, :]).astype(jnp.float32)[None, :, :, None]
    valid_count = jnp.sum(mask_grid)
    first_moment = jnp.sum(mask_grid * result, (0, 1, 2))
    second_moment = jnp.sum(mask_grid * result * result, (0, 1, 2))
    grad_wide = cotangent.astype(jnp.float32)
    d_down = jnp.einsum(
        "bijh,bijc->hc", activated_low, cotangent, preferred_element_type=jnp.float32
    )
    d_down_bias = jnp.sum(grad_wide, (0, 1, 2))
    d_activated = jnp.einsum("bijc,hc->bijh", cotangent, w_down, preferred_element_type=jnp.float32)
    d_preact = gelu_back(d_activated)[0].astype(jnp.bfloat16)
    d_up = jnp.einsum("bijc,bijh->ch", normed_two_low, d_preact, preferred_element_type=jnp.float32)
    d_up_bias = jnp.sum(d_preact.astype(jnp.float32), (0, 1, 2))
    d_normed_two = jnp.einsum("bijh,ch->bijc", d_preact, w_up, preferred_element_type=jnp.float32)
    d_skipped, d_gain_two, d_shift_two = norm_two_back(d_normed_two)
    d_skipped = d_skipped + grad_wide
    d_spread = d_skipped.astype(jnp.bfloat16)
    d_grid = jnp.einsum(
        "bijc,rmj->birmc",
        lax.all_to_all(d_spread, "lon", split_axis=3, concat_axis=2, tiled=True),
        inverse_tab,
        preferred_element_type=jnp.float32,
    ).astype(jnp.bfloat16)
    d_returned = jnp.einsum(
        "mjkqi,birmc->bmjkqrc",
        synthesis,
        lax.all_to_all(d_grid, "lat", split_axis=3, concat_axis=1, tiled=True),
        preferred_element_type=jnp.float32,
    ).astype(jnp.bfloat16)
    d_mixed = lax.all_to_all(
        lax.all_to_all(d_returned, "lat", split_axis=3, concat_axis=1, tiled=True),
        "lon",
        split_axis=2,
        concat_axis=6,
        tiled=True,
    ).reshape(1, modes_all, owned, 2, width)
    d_coeffs = coeff_back(d_mixed, spectral)
    d_spectral = lax.psum(weight_back(coeffs_owned, d_mixed).astype(jnp.bfloat16), "batch").astype(
        jnp.float32
    )
    d_coeffs_wide = d_coeffs.reshape(1, modes_all, 1, 1, owned, 2, width)
    d_modes = lax.all_to_all(
        lax.all_to_all(d_coeffs_wide, "lat", split_axis=1, concat_axis=2, tiled=True),
        "lon",
        split_axis=6,
        concat_axis=3,
        tiled=True,
    ).reshape(1, modes_dev, degrees_all, 2, quarter)
    d_fourier = jnp.einsum(
        "mli,bmlrc->birmc", analysis, d_modes, preferred_element_type=jnp.float32
    ).astype(jnp.bfloat16)
    d_columns = jnp.einsum(
        "birmc,jrm->bijc",
        lax.all_to_all(d_fourier, "lat", split_axis=1, concat_axis=3, tiled=True),
        forward_tab,
        preferred_element_type=jnp.float32,
    ).astype(jnp.bfloat16)
    d_normed_one = lax.all_to_all(d_columns, "lon", split_axis=2, concat_axis=3, tiled=True).astype(
        jnp.float32
    )
    d_input_norm, d_gain_one, d_shift_one = norm_one_back(d_normed_one)
    d_inputs = d_input_norm + d_skipped
    summed = lax.psum(
        (
            d_up,
            d_down,
            d_up_bias,
            d_down_bias,
            d_gain_one,
            d_shift_one,
            d_gain_two,
            d_shift_two,
            valid_count,
            first_moment,
            second_moment,
        ),
        ("lat", "lon", "batch"),
    )
    batch_mean = summed[9] / summed[8]
    batch_var = summed[10] / summed[8] - batch_mean * batch_mean
    new_mean = (1.0 - momentum) * run_mean + momentum * batch_mean
    new_var = (1.0 - momentum) * run_var + momentum * batch_var
    return (
        output,
        d_inputs,
        summed[4],
        summed[5],
        d_spectral,
        summed[6],
        summed[7],
        summed[0],
        summed[2],
        summed[1],
        summed[3],
        new_mean,
        new_var,
    )


def shards(inputs, *rest):
    rows_dev = inputs.shape[1]
    lon_count = lax.axis_size("lon")
    banded = (
        lon_count == 4
        and lax.axis_size("batch") == 2
        and rows_dev == 2 * lon_count
        and M % lon_count == 0
        and M // lon_count <= 128
        and rest[2].shape[0] % 4 in (0, 3)
        and rows_dev * lax.axis_size("lat") <= 32
    )
    return (band_shards if banded else degree_shards)(inputs, *rest)


def solution(mesh):
    return jax.shard_map(
        shards,
        mesh=mesh,
        in_specs=(
            P("batch", "lat", "lon", None),
            P(),
            P(),
            P(("lat", "lon"), None, None, None),
            P(),
            P(),
            P(),
            P(),
            P(),
            P(),
            P("batch", None),
            P("batch", "lat", "lon", None),
            P(),
            P(),
            P(),
        ),
        out_specs=(
            P("batch", "lat", "lon", None),
            P("batch", "lat", "lon", None),
            P(),
            P(),
            P(("lat", "lon"), None, None, None),
            P(),
            P(),
            P(),
            P(),
            P(),
            P(),
            P(),
            P(),
        ),
        check_vma=False,
    )
```

```python
import math

import jax
import jax.numpy as jnp
from jax import lax
from jax.experimental import pallas as pl
from jax.experimental.pallas import tpu as pltpu
from jax.sharding import PartitionSpec as P

GRID_ROWS = 360
M = 360
L = 360


epsilon = 1e-05
GROUP = 8
CHUNKS = 2
PER_STEP = 6


def layer_norm(values, gain, shift):
    centre = values - jnp.mean(values, -1, keepdims=True)
    spread = jnp.mean(centre * centre, -1, keepdims=True)
    return centre * lax.rsqrt(spread + epsilon) * gain + shift


def xor_pairs(count, bit):
    return [(i, i ^ bit) for i in range(count)]


def ring_pairs(count, step):
    return [(i, (i + step) % count) for i in range(count)]


def swap_cores(values):
    return lax.ppermute(values, "batch", xor_pairs(2, 1))


def near(values):
    return lax.ppermute(values, "lon", xor_pairs(4, 1))


def far(values):
    return lax.ppermute(values, "lon", xor_pairs(4, 2))


def after(values, earlier):
    return lax.optimization_barrier((values, earlier))[0]


def trade(values):
    return lax.all_to_all(values, "lon", split_axis=0, concat_axis=0, tiled=True)


def cross(values, k):
    return lax.ppermute(values, "lon", xor_pairs(4, k))


def trade_pieces(pieces):
    return [pieces[0]] + [cross(pieces[k], k) for k in (1, 2, 3)]


def gathered(values, name):
    count = lax.axis_size(name)
    pairs = xor_pairs if name == "lon" else ring_pairs
    return [values] + [lax.ppermute(values, name, pairs(count, k)) for k in range(1, count)]


def in_order(pieces, name):
    at, count = lax.axis_index(name), len(pieces)
    pieces = jnp.stack(pieces, 0)
    where = lambda place: at ^ place if name == "lon" else (at - place) % count
    return [lax.dynamic_index_in_dim(pieces, where(place), 0, keepdims=False) for place in range(count)]


def sum_over_planes(values):
    return sum(in_order(gathered(values, "lat"), "lat"))


def dot(a, b):
    return jnp.dot(a, b, preferred_element_type=jnp.float32)


def dot_along(a, b):
    return lax.dot_general(a, b, (((1,), (1,)), ((), ())), preferred_element_type=jnp.float32)


def dot_across(a, b):
    return lax.dot_general(a, b, (((0,), (0,)), ((), ())), preferred_element_type=jnp.float32)


def low(values):
    return values.astype(jnp.bfloat16)


def wide(values):
    return values.astype(jnp.float32)


NO_COST = pl.CostEstimate(flops=0, transcendentals=0, bytes_accessed=0)


def params(megabytes):
    return pltpu.CompilerParams(vmem_limit_bytes=megabytes * 2**20)


def turned(cosine, sine, quarter_turns):
    turns = quarter_turns % 4
    real = jnp.where(turns == 0, cosine, jnp.where(turns == 1, -sine, jnp.where(turns == 2, -cosine, sine)))
    imag = jnp.where(turns == 0, -sine, jnp.where(turns == 1, -cosine, jnp.where(turns == 2, sine, cosine)))
    return real, imag


def dft_tables(points, parts, order, valid, axis):
    cols = points // parts
    column = jnp.arange(cols, dtype=jnp.int32)
    if axis == 1:
        order, valid, column = order[:, None], valid[:, None], column[None, :]
    else:
        order, valid, column = order[None, :], valid[None, :], column[:, None]
    angle = (order * column % points).astype(jnp.float32) * (2.0 * math.pi / points)
    cosine = jnp.where(valid, jnp.cos(angle), 0.0)
    sine = jnp.where(valid, jnp.sin(angle), 0.0)
    cosine, sine = lax.optimization_barrier((cosine, sine))
    part = jnp.arange(parts, dtype=jnp.int32)[:, None, None]
    real, imag = turned(cosine[None], sine[None], part * order[None])
    scales = (1.0 / math.sqrt(points), jnp.where(order == 0, 1.0, 2.0)[None])
    return [jnp.concatenate([low(real * scale), low(imag * scale)], axis) for scale in scales]


def legendre_kernel(cut, starts_ref, upper_ref, lower_ref, order_ref, cos_ref, diag_ref, second_ref, out_ref, all_ref):
    degrees = all_ref.shape[0]
    cosines = cos_ref[...]
    diagonal = diag_ref[...]
    second = second_ref[...]
    order = order_ref[...]

    def advance(degree, state):
        before, latest = state
        level = degree.astype(jnp.float32)
        upper = upper_ref[pl.ds(degree, 1), :]
        lower = lower_ref[pl.ds(degree, 1), :]
        general = upper * (cosines * latest - lower * before)
        current = jnp.where(
            level < order,
            0.0,
            jnp.where(level == order, diagonal, jnp.where(level == order + 1.0, second, general)),
        )
        all_ref[pl.ds(degree, 1)] = current[None]
        return latest, current

    unroll = 8 if degrees % 8 == 0 else 1

    def several(step, state):
        for at in range(unroll):
            state = advance(step * unroll + at, state)
        return state

    zeros = cosines * 0.0
    lax.fori_loop(0, degrees // unroll, several, (zeros, zeros))
    blocks = out_ref.shape[0] // (2 * cut)
    for block in range(blocks):
        for half in range(2):

            def copy(at, carry, block=block, half=half):
                degree = starts_ref[block] + half * cut + at
                value = all_ref[pl.ds(degree, 1)]
                keep = (degree < L) & (half * cut + at >= starts_ref[blocks])
                out_ref[pl.ds((at * 2 + half) * blocks + block, 1)] = jnp.where(keep, value, 0.0)
                return carry

            lax.fori_loop(0, cut, copy, 0)


def legendre(starts, skip, orders, valid, cosines, sine_vals, degrees, cut):
    order_row = orders[None, :]
    sine_col = sine_vals[:, None]
    log_start = 0.5 * (
        jnp.log((2.0 * order_row + 1.0) / (4.0 * math.pi))
        + lax.lgamma(order_row + 0.5)
        - lax.lgamma(order_row + 1.0)
        - 0.5 * math.log(math.pi)
    ) + order_row * jnp.log(sine_col)
    diagonal = jnp.where(valid[None, :], jnp.exp(log_start), 0.0)
    second = cosines[:, None] * jnp.sqrt(2.0 * order_row + 3.0) * diagonal
    degree = jnp.arange(degrees, dtype=jnp.float32)[:, None]
    upper = jnp.sqrt((4.0 * degree * degree - 1.0) / jnp.maximum(degree * degree - order_row * order_row, 1.0))
    lower = jnp.sqrt(
        jnp.maximum((degree - 1.0) * (degree - 1.0) - order_row * order_row, 0.0)
        / jnp.maximum(4.0 * (degree - 1.0) * (degree - 1.0) - 1.0, 1.0)
    )
    shape = diagonal.shape
    return pl.pallas_call(
        lambda *refs: legendre_kernel(cut, *refs),
        out_shape=jax.ShapeDtypeStruct((starts.shape[0] * 2 * cut,) + shape, jnp.float32),
        in_specs=[pl.BlockSpec(memory_space=pltpu.SMEM)] + [pl.BlockSpec(memory_space=pltpu.VMEM)] * 6,
        out_specs=pl.BlockSpec(memory_space=pltpu.VMEM),
        scratch_shapes=[pltpu.VMEM((degrees,) + shape, jnp.float32)],
        cost_estimate=NO_COST,
        compiler_params=params(24),
        name="legendre",
    )(
        jnp.concatenate([starts, skip[None]]).astype(jnp.int32),
        upper,
        lower,
        jnp.broadcast_to(order_row, shape),
        jnp.broadcast_to(cosines[:, None], shape),
        diagonal,
        second,
    )


def block_tables(poly, slots):
    degrees, rows, _ = poly.shape
    groups = slots // GROUP
    values = low(poly[:, :, :slots]).reshape(degrees, rows, groups, GROUP)

    def expand(table, depth):
        lanes = depth * GROUP
        lane = jnp.arange(lanes, dtype=jnp.int32)
        repeat = low(jnp.arange(depth, dtype=jnp.int32)[:, None] == lane[None, :] // GROUP)
        flat = table.reshape(-1, depth)
        row = jnp.arange(flat.shape[0], dtype=jnp.int32)
        same = row[:, None] % GROUP == lane[None, :] % GROUP
        return low(jnp.where(same, dot(flat, repeat), 0.0)).reshape(groups, -1, lanes)

    return expand(values.transpose(2, 0, 3, 1), rows), expand(values.transpose(2, 1, 3, 0), degrees)


def normalise(values):
    centre = values - jnp.mean(values, -1, keepdims=True)
    factor = lax.rsqrt(jnp.mean(centre * centre, -1, keepdims=True) + epsilon)
    return centre * factor, factor


def normalise_back(normal, factor, grad):
    return factor * (
        grad - jnp.mean(grad, -1, keepdims=True) - normal * jnp.mean(grad * normal, -1, keepdims=True)
    )


def column_sum(values):
    return jnp.sum(values, 0, keepdims=True)


def store_modes(totals, refs):
    groups, _, double = refs[0].shape
    width = double // 2
    slots = groups * GROUP
    for part in range(2):
        for owner, ref in enumerate(refs):
            at = (part * len(refs) + owner) * slots
            rows = [total[at : at + slots].reshape(groups, GROUP, width) for total in totals]
            ref[:, :, part * width : part * width + width] = low(jnp.concatenate(rows, 1))


def load_modes(refs, flat_ref):
    groups, _, double = refs[0].shape
    width = double // 2
    slots = groups * GROUP
    rows = flat_ref.shape[1] // width
    half = flat_ref.shape[0] // 2
    for piece, ref in enumerate(refs):
        owner, chunk = piece // CHUNKS, piece % CHUNKS
        at = (owner * CHUNKS + chunk) * slots
        modes = wide(ref[...]).reshape(groups, rows, GROUP, double)
        for row in range(rows):
            flat = low(modes[:, row].reshape(slots, double))
            lanes = slice(row * width, row * width + width)
            flat_ref[at : at + slots, lanes] = flat[:, :width]
            flat_ref[half + at : half + at + slots, lanes] = flat[:, width:]


def whole_spec(array):
    return pl.BlockSpec(array.shape, lambda *at: (0,) * len(array.shape))


def enter_kernel(weight_ref, table_ref, values_ref, gain_ref, shift_ref, *out_refs):
    totals = []
    for row in range(values_ref.shape[1]):
        total = 0.0
        for part in range(table_ref.shape[0]):
            normal, _ = normalise(wide(values_ref[part, row]))
            total += dot(table_ref[part], low(normal * gain_ref[...] + shift_ref[...]))
        totals.append(total * weight_ref[row])
    store_modes(totals, out_refs)


def enter(weight, table, values, gain, shift, groups):
    parts, rows, cols, width = values.shape
    arrays = [table, values, gain[None], shift[None]]
    return pl.pallas_call(
        enter_kernel,
        out_shape=[jax.ShapeDtypeStruct((groups, rows * GROUP, 2 * width), jnp.bfloat16)] * parts,
        in_specs=[pl.BlockSpec(memory_space=pltpu.SMEM)] + [pl.BlockSpec(memory_space=pltpu.VMEM)] * 4,
        out_specs=[pl.BlockSpec(memory_space=pltpu.VMEM)] * parts,
        cost_estimate=NO_COST,
        compiler_params=params(32),
        name="enter",
    )(weight, *arrays)


def gelu_parts(values):
    slope = math.sqrt(2.0 / math.pi)
    square = values * values
    tangent = jnp.tanh(slope * values * (1.0 + 0.044715 * square))
    half = 0.5 * (1.0 + tangent)
    grad = half + 0.5 * values * (1.0 - tangent * tangent) * slope * (1.0 + 3.0 * 0.044715 * square)
    return values * half, grad


def feed_kernel(pieces, where_ref, *refs):
    modes_refs, refs = refs[:pieces], refs[pieces:]
    (columns_ref, modes_table_ref, values_ref, cotangent_ref), refs = refs[:4], refs[4:]
    (gain_ref, shift_ref, up_ref, up_bias_ref, down_ref, down_bias_ref), refs = refs[:6], refs[6:]
    *grid_refs, output_ref, d_skipped_ref, sums_ref, flat_ref, total_ref = refs
    part, parts = pl.program_id(0), pl.num_programs(0)
    _, rows, cols, width = values_ref.shape
    hidden = up_ref.shape[-1]

    @pl.when(part == 0)
    def _():
        load_modes(modes_refs, flat_ref)
        sums_ref[...] = jnp.zeros_like(sums_ref)
        total_ref[...] = jnp.zeros_like(total_ref)

    spreads = low(dot(columns_ref[0], flat_ref[...]))
    column_at = where_ref[5] + part * cols + lax.broadcasted_iota(jnp.int32, (cols, 1), 0)
    inside_columns = (column_at >= where_ref[2]) & (column_at < where_ref[3])
    grads, sums = [], []
    for row in range(rows):
        skipped = wide(values_ref[0, row]) + wide(spreads[:, row * width : row * width + width])
        normal, factor = normalise(skipped)
        normed = low(normal * gain_ref[...] + shift_ref[...])
        activated, slope = gelu_parts(dot(normed, up_ref[...]) + up_bias_ref[...])
        activated = low(activated)
        result = skipped + dot(activated, down_ref[...]) + down_bias_ref[...]
        output_ref[0, row] = low(result)
        row_at = where_ref[4] + row
        kept = jnp.where(inside_columns & (row_at >= where_ref[0]) & (row_at < where_ref[1]), result, 0.0)

        cotangent = cotangent_ref[0, row]
        d_preact = low(dot_along(cotangent, down_ref[...]) * slope)
        d_normed = dot_along(d_preact, up_ref[...])
        d_skipped = wide(cotangent) + normalise_back(normal, factor, d_normed * gain_ref[...])
        d_skipped_ref[0, row] = d_skipped
        grads.append(low(d_skipped))
        d_bias = column_sum(wide(d_preact))
        vectors = [d_bias[:, j * width : j * width + width] for j in range(hidden // width)] + [
            column_sum(wide(cotangent)),
            column_sum(d_normed * normal),
            column_sum(d_normed),
            column_sum(kept),
            column_sum(kept * kept),
        ]
        sums.append([dot_across(normed, d_preact), dot_across(activated, cotangent)] + vectors)

    total_ref[...] += dot(modes_table_ref[0], jnp.concatenate(grads, 1))

    @pl.when(part == parts - 1)
    def _():
        store_modes([total_ref[:, row * width : row * width + width] for row in range(rows)], grid_refs)

    d_up, d_down, *vectors = [sum(terms) for terms in zip(*sums)]
    for at in range(hidden // width):
        sums_ref[at * width : at * width + width] += d_up[:, at * width : at * width + width]
    sums_ref[hidden : 2 * hidden] += d_down
    at = 2 * hidden
    for j, vector in enumerate(vectors):
        sums_ref[at + j : at + j + 1] += vector


def feed(where, modes, columns, modes_table, values, cotangent, gain, shift, w_up, b_up, w_down, b_down):
    parts, rows, cols, width = values.shape
    hidden = w_up.shape[1]
    lanes = modes_table.shape[1]
    grid = (CHUNKS * modes[0].shape[0],) + modes[0].shape[1:]
    cells = pl.BlockSpec((1, rows, cols, width), lambda p: (p, 0, 0, 0))
    by_part = lambda table: pl.BlockSpec((1,) + table.shape[1:], lambda p: (p, 0, 0))
    small = [gain[None], shift[None], w_up, b_up[None], w_down, b_down[None]]
    outs = [jax.ShapeDtypeStruct(grid, jnp.bfloat16)] * parts + [
        jax.ShapeDtypeStruct(values.shape, jnp.bfloat16),
        jax.ShapeDtypeStruct(values.shape, jnp.float32),
        jax.ShapeDtypeStruct(((2 * hidden + hidden // width + 5 + 63) // 64 * 64, width), jnp.float32),
    ]
    return pl.pallas_call(
        lambda *refs: feed_kernel(len(modes), *refs),
        grid=(parts,),
        out_shape=outs,
        in_specs=[pl.BlockSpec(memory_space=pltpu.SMEM)]
        + [whole_spec(m) for m in modes]
        + [by_part(columns), by_part(modes_table), cells, cells]
        + [whole_spec(v) for v in small],
        out_specs=[whole_spec(outs[0])] * parts + [cells, cells, whole_spec(outs[-1])],
        scratch_shapes=[pltpu.VMEM((lanes, rows * width), jnp.bfloat16), pltpu.VMEM((lanes, rows * width), jnp.float32)],
        cost_estimate=NO_COST,
        compiler_params=params(60),
        name="feed",
    )(where, *modes, columns, modes_table, values, cotangent, *small)


def leave_kernel(pieces, weight_ref, *refs):
    modes_refs, refs = refs[:pieces], refs[pieces:]
    columns_ref, values_ref, d_skipped_ref, gain_ref, out_ref, sums_ref, flat_ref = refs
    _, rows, _, width = values_ref.shape

    @pl.when(pl.program_id(0) == 0)
    def _():
        load_modes(modes_refs, flat_ref)
        sums_ref[...] = jnp.zeros_like(sums_ref)

    columns = dot(columns_ref[0], flat_ref[...])
    for row in range(rows):
        d_normed = wide(low(columns[:, row * width : row * width + width] * weight_ref[row]))
        normal, factor = normalise(wide(values_ref[0, row]))
        out_ref[0, row] = low(normalise_back(normal, factor, d_normed * gain_ref[...]) + d_skipped_ref[0, row])
        sums_ref[0:1] += column_sum(d_normed * normal)
        sums_ref[1:2] += column_sum(d_normed)


def leave(weight, modes, columns, values, d_skipped, gain):
    parts, rows, cols, width = values.shape
    cells = pl.BlockSpec((1, rows, cols, width), lambda p: (p, 0, 0, 0))
    return pl.pallas_call(
        lambda *refs: leave_kernel(len(modes), *refs),
        grid=(parts,),
        out_shape=[jax.ShapeDtypeStruct(values.shape, jnp.bfloat16), jax.ShapeDtypeStruct((8, width), jnp.float32)],
        in_specs=[pl.BlockSpec(memory_space=pltpu.SMEM)]
        + [whole_spec(m) for m in modes]
        + [
            pl.BlockSpec((1,) + columns.shape[1:], lambda p: (p, 0, 0)),
            cells,
            cells,
            pl.BlockSpec((1, width), lambda p: (0, 0)),
        ],
        out_specs=[cells, pl.BlockSpec((8, width), lambda p: (0, 0))],
        scratch_shapes=[pltpu.VMEM((columns.shape[2], rows * width), jnp.bfloat16)],
        cost_estimate=NO_COST,
        compiler_params=params(32),
        name="leave",
    )(weight, *modes, columns, values, d_skipped, gain[None])


def complex_weight(weight_ref):
    real, imag = weight_ref[0, 0], weight_ref[0, 1]
    return jnp.concatenate([jnp.concatenate([real, imag], 1), jnp.concatenate([-imag, real], 1)], 0)


class Core:
    def __init__(self, shard, slots, degrees, cut, rows, table, weights, back_table):
        self.slots, self.cut, self.degrees = slots, cut, degrees
        self.steps = shard[1] // PER_STEP
        ends = CHUNKS * self.steps
        self.first = ends if table is not None else 0
        self.last = ends if back_table is not None else 0
        self.grid = (self.first + cut + self.last,)
        self.modes = (degrees, CHUNKS * shard[1]) + shard[2:]
        self.per = degrees // cut
        block = (shard[0], PER_STEP) + shard[2:]
        place = lambda step, start, count: jnp.clip(step - start, 0, count - 1)
        self.middle = lambda s: place(s, self.first, cut)
        self.arrays, self.in_specs = [], []
        for chunk in range(CHUNKS if self.first else 0):
            spec = pl.BlockSpec(block, lambda s, chunk=chunk: (0, place(s, chunk * self.steps, self.steps), 0, 0))
            self.take([slot for sample in rows[chunk] for slot in sample], spec)
        if self.first:
            self.take([table], pl.BlockSpec((PER_STEP,) + table.shape[1:], lambda s: (place(s, 0, ends), 0, 0)))
        start = self.first + cut
        if self.last:
            spec = pl.BlockSpec((PER_STEP,) + back_table.shape[1:], lambda s: (place(s, start, ends), 0, 0))
            self.take([back_table], spec)
        self.take(weights, pl.BlockSpec((1,) + weights[0].shape[1:], lambda s: (self.middle(s), 0, 0, 0)))
        self.modes_spec = pl.BlockSpec((self.per,) + self.modes[1:], lambda s: (self.middle(s), 0, 0, 0))
        self.modes_shape = jax.ShapeDtypeStruct(self.modes, jnp.bfloat16)
        self.held = pltpu.VMEM(self.modes, jnp.bfloat16)
        self.out_specs, self.out_shape = [], []
        for chunk in range(CHUNKS if self.last else 0):
            at = lambda s, chunk=chunk: (0, 0, place(s, start + chunk * self.steps, self.steps), 0, 0)
            self.out_specs += [pl.BlockSpec((slots,) + block, at)] * 2
            self.out_shape += [jax.ShapeDtypeStruct((slots,) + shard, jnp.bfloat16)] * 2

    def take(self, arrays, spec):
        self.arrays += arrays
        self.in_specs += [spec] * len(arrays)

    def split(self, refs):
        at = CHUNKS * 2 * self.slots if self.first else 0
        shards, refs = refs[:at], refs[at:]
        table, refs = (refs[0], refs[1:]) if self.first else (None, refs)
        back_table, refs = (refs[0], refs[1:]) if self.last else (None, refs)
        count = len(self.arrays) - at - (table is not None) - (back_table is not None)
        return shards, table, back_table, refs[:count], refs[count:]

    def analyse(self, shard_refs, table_ref, held_ref):
        step = pl.program_id(0)
        for chunk in range(CHUNKS):
            refs = shard_refs[chunk * 2 * self.slots : (chunk + 1) * 2 * self.slots]

            @pl.when((step >= chunk * self.steps) & (step < (chunk + 1) * self.steps))
            def _(refs=refs):
                for at in range(PER_STEP):
                    samples = []
                    for sample in range(2):
                        rows = [flat_rows(ref[:, at]) for ref in refs[sample * self.slots : (sample + 1) * self.slots]]
                        total = dot(table_ref[at], jnp.concatenate(rows, 0))
                        samples.append(total.reshape(self.degrees, GROUP, -1))
                    held_ref[:, pl.ds(step * PER_STEP + at, 1)] = low(jnp.concatenate(samples, 1))[:, None]

    def synthesise(self, table_ref, held_ref, out_refs):
        step = pl.program_id(0) - self.first - self.cut
        for chunk in range(CHUNKS):
            refs = out_refs[2 * chunk : 2 * chunk + 2]

            @pl.when((step >= chunk * self.steps) & (step < (chunk + 1) * self.steps))
            def _(refs=refs):
                for at in range(PER_STEP):
                    modes = wide(held_ref[:, pl.ds(step * PER_STEP + at, 1)])
                    modes = modes.reshape(self.degrees, 2, GROUP, modes.shape[-1])
                    for sample, ref in enumerate(refs):
                        total = low(dot(table_ref[at], low(flat_rows(modes[:, sample]))))
                        ref[:, :, at] = total.reshape(ref.shape[:2] + ref.shape[3:])

    def in_middle(self):
        step = pl.program_id(0)
        return (step >= self.first) & (step < self.first + self.cut)

    def degree(self, at):
        return self.middle(pl.program_id(0)) * self.per + at

    def chunks(self, out):
        return [out[2 * chunk : 2 * chunk + 2] for chunk in range(CHUNKS)]


def flat_rows(modes):
    return modes.reshape(-1, modes.shape[-1])


def mix_forward(rows, table, back_table, weights, cut):
    shard = rows[0][0][0].shape
    core = Core(shard, len(rows[0][0]), len(weights) * cut, cut, rows, table, weights, back_table)

    def kernel(*refs):
        shards, table, back_table, weight_refs, (*out_refs, coeffs_ref, held_ref, mixed_ref) = core.split(refs)
        core.analyse(shards, table, held_ref)

        @pl.when(core.in_middle())
        def _():
            for at, weight_ref in enumerate(weight_refs):
                coeffs = held_ref[core.degree(at)]
                coeffs_ref[at] = coeffs
                mixed = low(dot(flat_rows(coeffs), complex_weight(weight_ref)))
                mixed_ref[core.degree(at)] = mixed.reshape(coeffs.shape)

        core.synthesise(back_table, mixed_ref, out_refs)

    out = pl.pallas_call(
        kernel,
        grid=core.grid,
        out_shape=core.out_shape + [core.modes_shape],
        in_specs=core.in_specs,
        out_specs=core.out_specs + [core.modes_spec],
        scratch_shapes=[core.held, core.held],
        cost_estimate=NO_COST,
        compiler_params=params(60),
        name="mix_forward",
    )(*core.arrays)
    return core.chunks(out), out[-1]


def mix_backward(rows, table, back_table, weights, cut, coeffs):
    shard = rows[0][0][0].shape
    core = Core(shard, len(rows[0][0]), len(weights) * cut, cut, rows, table, weights, back_table)
    weight = weights[0].shape
    grad = pl.BlockSpec((1,) + weight[1:], lambda s: (core.middle(s), 0, 0, 0))

    def kernel(*refs):
        shards, table, back_table, weight_refs, (coeffs_ref, *outs, held_ref, mixed_ref) = core.split(refs)
        core.analyse(shards, table, held_ref)

        @pl.when(core.in_middle())
        def _():
            for at, (weight_ref, target) in enumerate(zip(weight_refs, outs[-len(weights) :])):
                d_mixed = held_ref[core.degree(at)]
                d_coeffs = low(dot_along(flat_rows(d_mixed), complex_weight(weight_ref)))
                mixed_ref[core.degree(at)] = d_coeffs.reshape(d_mixed.shape)
                width = target.shape[-1]
                left, right = flat_rows(coeffs_ref[at]), flat_rows(d_mixed)
                turned_right = jnp.concatenate([right[:, width:], -right[:, :width]], 1)
                total = dot_across(
                    jnp.concatenate([left[:, :width], left[:, width:]], 0), jnp.concatenate([right, turned_right], 0)
                )
                target[0, 0] = low(total[:, :width])
                target[0, 1] = low(total[:, width:])

        core.synthesise(back_table, mixed_ref, outs[: -len(weights)])

    out = pl.pallas_call(
        kernel,
        grid=core.grid,
        out_shape=core.out_shape + [jax.ShapeDtypeStruct(weight, jnp.bfloat16)] * len(weights),
        in_specs=core.in_specs + [core.modes_spec],
        out_specs=core.out_specs + [grad] * len(weights),
        scratch_shapes=[core.held, core.held],
        cost_estimate=NO_COST,
        compiler_params=params(60),
        name="mix_backward",
    )(*core.arrays, coeffs)
    return core.chunks(out), out[-len(weights) :]


def gather_rows(shards, gate):
    count = lax.axis_size("lat")
    own = [[shard] for shard in shards]
    for step in range(1, count):
        earlier = gate(step, own)
        sent = [rows[-1] for rows in own]
        if earlier is not None:
            sent[-1] = after(sent[-1], earlier)
        own = [rows + [lax.ppermute(rows_sent, "lat", ring_pairs(count, 1))] for rows, rows_sent in zip(own, sent)]
    return [(rows, [swap_cores(slot) for slot in rows]) for rows in own]


def scatter_rows(own, other, gate=None, sent=None):
    count = lax.axis_size("lat")
    other = swap_cores(other)
    arrived = None
    for slot in range(count - 1, -1, -1):
        total = wide(own[slot]) + wide(other[slot])
        if arrived is not None:
            total = total + wide(arrived)
        total = low(total)
        if slot == 1:
            midway = total
        if slot == count - 1 and sent is not None:
            sent.append(total)
        if slot > 0:
            arrived = lax.ppermute(total, "lat", ring_pairs(count, -1))
            if slot == 2 and gate is not None:
                arrived = after(arrived, gate)
    return total, midway


def gather_weights(own):
    cut = own.shape[0] // 2
    first, last = own[:cut], own[cut:]
    return first, last, near(first), far(last)


def scatter_weights(grads):
    three = near(grads[3]), far(grads[7])
    one, two = after((grads[1], grads[6]), three)
    return three, (near(one), far(two))


def finish_weight_sum(grads, three, gate):
    from_near, from_far = after(three, gate)
    return far(low(wide(grads[2]) + wide(from_near))), near(low(wide(grads[5]) + wide(from_far)))


def sum_weights(grads, single, double):
    first = low(wide(grads[0]) + wide(single[0]) + wide(double[0]))
    last = low(wide(grads[4]) + wide(single[1]) + wide(double[1]))
    return first, last


class PartSum:
    def __init__(self, values):
        core = lax.axis_index("batch")
        half = values.shape[0] // 2
        self.mine = lax.dynamic_slice_in_dim(values, core * half, half, 0)
        self.other = swap_cores(lax.dynamic_slice_in_dim(values, (1 - core) * half, half, 0))

    def cores(self):
        return self.mine + self.other

    def chips(self, values):
        chip = lax.axis_index("lon")
        part = values.shape[0] // 4
        for_chip = lambda k: lax.dynamic_slice_in_dim(values, (chip ^ k) * part, part, 0)
        return sum(trade_pieces([for_chip(k) for k in range(4)]))

    def share(self, pieces):
        return jnp.concatenate(in_order(pieces, "lon"), 0)

    def finish(self, mine, other):
        core = lax.axis_index("batch")
        return jnp.concatenate([jnp.where(core == 0, mine, other), jnp.where(core == 0, other, mine)], 0)


def band_shards(
    inputs,
    gain_one,
    shift_one,
    spectral,
    gain_two,
    shift_two,
    w_up,
    b_up,
    w_down,
    b_down,
    crops,
    cotangent,
    run_mean,
    run_var,
    momentum,
):
    lat_count = lax.axis_size("lat")
    lon_count = lax.axis_size("lon")
    plane = lax.axis_index("lat")
    chip = lax.axis_index("lon")
    core = lax.axis_index("batch")
    rows_dev = inputs.shape[1]
    cols_dev = inputs.shape[2]
    width = inputs.shape[3]
    rows_chip = rows_dev // lon_count
    lat_rows = rows_dev * lat_count
    lon_cols = cols_dev * lon_count
    modes_dev = M // lon_count
    slots = (modes_dev + CHUNKS * PER_STEP * GROUP - 1) // (CHUNKS * PER_STEP * GROUP) * PER_STEP * GROUP
    groups = slots // GROUP
    owned = spectral.shape[0]
    cut = (owned + 3) // 4
    half = 2 * cut
    first_degree = core * (owned - half)
    skip = core * (2 * half - owned)
    by_row = (lon_count, rows_chip, cols_dev, width)

    first_hop = gather_weights(lax.dynamic_slice_in_dim(spectral, first_degree, half, 0))
    values = trade(inputs.reshape(by_row))

    across = chip ^ jnp.arange(lon_count, dtype=jnp.int32)
    in_chip = jnp.arange(CHUNKS * slots, dtype=jnp.int32)
    first_order = across[:, None] * modes_dev + in_chip[None, :]
    valid = jnp.broadcast_to(in_chip[None, :] < modes_dev, first_order.shape)
    order = jnp.where(valid, first_order, 0)
    to_modes, to_modes_back = dft_tables(lon_cols, lon_count, order.reshape(-1), valid.reshape(-1), 1)
    to_columns_back, to_columns = dft_tables(lon_cols, lon_count, order.reshape(-1), valid.reshape(-1), 2)
    first_row = (GRID_ROWS - lat_rows) // 2
    slot_plane = (plane - jnp.arange(lat_count, dtype=jnp.int32)) % lat_count
    row = across[:, None] * rows_chip + jnp.arange(rows_chip, dtype=jnp.int32)[None, :]
    row = (slot_plane[:, None] * rows_dev + row.reshape(1, -1)).reshape(-1)
    colatitude = (row.astype(jnp.float32) + (first_row + 0.5)) * (math.pi / GRID_ROWS)
    lane = jnp.arange(128, dtype=jnp.int32)
    orders = (chip * modes_dev + jnp.minimum(lane, modes_dev - 1)).astype(jnp.float32)
    owners = plane * lon_count + across
    poly = legendre(
        owners * owned + first_degree,
        skip,
        orders,
        lane < modes_dev,
        jnp.cos(colatitude),
        jnp.sin(colatitude),
        owned * lat_count * lon_count,
        cut,
    )
    analysis, synthesis = block_tables(poly, CHUNKS * slots)
    own_row = plane * rows_dev + chip * rows_chip
    angle = (own_row + jnp.arange(rows_chip, dtype=jnp.int32)).astype(jnp.float32) + (first_row + 0.5)
    quadrature = jnp.sin(angle * (math.pi / GRID_ROWS)) * ((math.pi / GRID_ROWS) * (2.0 * math.pi / math.sqrt(lon_cols)))

    def by_plane(pieces):
        return [
            jnp.stack([piece[chunk * groups : (chunk + 1) * groups] for piece in pieces], 0) for chunk in range(CHUNKS)
        ]

    def by_chip(chunks):
        traded = [trade_pieces([chunk[k] for k in range(lon_count)]) for chunk in chunks]
        return [traded[chunk][k] for k in range(lon_count) for chunk in range(CHUNKS)]

    values = after(values, (poly, analysis))
    pieces = trade_pieces(enter(quadrature, to_modes, values, gain_one, shift_one, CHUNKS * groups))
    shards_in = by_plane(pieces)
    first, last, near_first, far_last = after(first_hop, pieces[1])
    second_hop = (near(last), far(first))
    third_hop = (far(near_first), near(far_last))
    late = {2: synthesis, 3: (second_hop, to_columns, to_modes_back, to_columns_back)}
    rows_in = gather_rows(shards_in, lambda step, own: late.get(step))
    weights = [first, near_first, second_hop[1], third_hop[0], last, second_hop[0], far_last, third_hop[1]]
    partial, coeffs = mix_forward(rows_in, analysis, synthesis, weights, cut)
    sent = []
    grid = [scatter_rows(*partial[0], sent=sent)[0]]
    grads = trade(after(cotangent, sent).reshape(by_row))
    grid = by_chip(grid + [scatter_rows(*chunk, gate=grads)[0] for chunk in partial[1:]])

    where = jnp.concatenate([crops[0], own_row[None], jnp.zeros((1,), jnp.int32)])
    *d_grid, output, d_skipped, sums = feed(
        where, grid, to_columns, to_modes_back, values, grads, gain_two, shift_two, w_up, b_up, w_down, b_down
    )
    bounds = crops[0]
    count_rows = jnp.minimum(bounds[1], own_row + rows_chip) - jnp.maximum(bounds[0], own_row)
    count_cols = jnp.minimum(bounds[3], lon_cols) - jnp.maximum(bounds[2], 0)
    valid_count = (jnp.maximum(count_rows, 0) * jnp.maximum(count_cols, 0)).astype(jnp.float32)
    count_row = sums.shape[0] - 1
    sums = sums + jnp.where(jnp.arange(sums.shape[0]) == count_row, valid_count, 0.0)[:, None]

    shards_back = by_plane(trade_pieces(d_grid))
    traded = []

    def gate(step, own):
        if step == 1:
            traded.append(trade(after(output, shards_back)))
        return traded[0] if step == 2 else None

    rows_back = gather_rows(shards_back, gate)
    output = traded[0].reshape(inputs.shape)
    level = PartSum(after(sums, shards_back))
    sums = level.chips(level.cores())
    rows_back[1] = after(rows_back[1], sums)
    d_partial, d_weights = mix_backward(rows_back, analysis, synthesis, weights, cut, coeffs)
    three, single = scatter_weights(d_weights)
    d_modes, midway = zip(*[scatter_rows(*chunk) for chunk in d_partial])
    plane_pieces = after(gathered(after(sums, midway), "lat"), d_modes)
    sum_pieces = gathered(sum(in_order(plane_pieces, "lat")), "lon")
    traded = by_chip(after(d_modes, single))
    double = finish_weight_sum(d_weights, three, (traded, sum_pieces))
    sums = level.share(sum_pieces)
    other_sums = swap_cores(sums)
    d_inputs, d_norm = leave(
        quadrature, traded, to_columns_back, values, after(d_skipped, other_sums), gain_one
    )
    sums = level.finish(sums, other_sums)
    d_norm = sum_over_planes(d_norm + swap_cores(d_norm))
    norm_pieces = gathered(d_norm, "lon")
    d_inputs = wide(trade(d_inputs)).reshape(inputs.shape)
    d_norm = sum(in_order(norm_pieces, "lon"))
    halves = sum_weights(d_weights, single, after(double, norm_pieces))
    others = [swap_cores(part) for part in halves]
    own_first = [jnp.where(core == 0, mine, other) for mine, other in zip(halves, others)]
    own_last = [jnp.where(core == 0, other, mine) for mine, other in zip(halves, others)]
    own_last[0] = own_last[0][2 * half - owned :]
    d_spectral = jnp.concatenate([wide(part) for part in own_first + own_last], 0)

    hidden = w_up.shape[1]
    d_up = jnp.concatenate([sums[j * width : j * width + width] for j in range(hidden // width)], 1)
    d_down = sums[hidden : 2 * hidden]
    vectors = sums[2 * hidden :]
    pieces = hidden // width
    d_up_bias = vectors[:pieces].reshape(-1)
    d_down_bias, d_gain_two, d_shift_two, first_moment, second_moment = [vectors[pieces + j] for j in range(5)]
    count = sums[count_row, 0]
    batch_mean = first_moment / count
    batch_var = second_moment / count - batch_mean * batch_mean
    new_mean = (1.0 - momentum) * run_mean + momentum * batch_mean
    new_var = (1.0 - momentum) * run_var + momentum * batch_var
    return (
        output,
        d_inputs,
        d_norm[0],
        d_norm[1],
        d_spectral,
        d_gain_two,
        d_shift_two,
        d_up,
        d_up_bias,
        d_down,
        d_down_bias,
        new_mean,
        new_var,
    )


def fourier_tables(points, modes):
    column = jnp.arange(points, dtype=jnp.int32)
    order = jnp.arange(modes, dtype=jnp.int32)
    phase = column[:, None] * order[None, :] % points
    angle = phase.astype(jnp.float32) * (2.0 * math.pi / points)
    cosine = jnp.cos(angle)
    sine = jnp.sin(angle)
    scale = 1.0 / math.sqrt(points)
    forward_tab = jnp.stack([cosine * scale, -sine * scale], 1)
    factor = jnp.where(order == 0, 1.0, 2.0).astype(jnp.float32)
    inverse_tab = jnp.stack([(cosine * factor[None, :]).T, (-sine * factor[None, :]).T], 0)
    return (forward_tab.astype(jnp.bfloat16), inverse_tab.astype(jnp.bfloat16))


def grid_angles(rows_total):
    first_row = (GRID_ROWS - rows_total) // 2
    colatitude = (jnp.arange(rows_total, dtype=jnp.float32) + (first_row + 0.5)) * (
        math.pi / GRID_ROWS
    )
    return (jnp.cos(colatitude), jnp.sin(colatitude))


def legendre_scan(orders, cosines, sine_vals, degrees):
    order_col = orders[:, None]
    cos_row = cosines[None, :]
    log_start = 0.5 * (
        jnp.log((2.0 * order_col + 1.0) / (4.0 * math.pi))
        + lax.lgamma(order_col + 0.5)
        - lax.lgamma(order_col + 1.0)
        - 0.5 * math.log(math.pi)
    ) + order_col * jnp.log(sine_vals[None, :])
    diagonal_start = jnp.exp(log_start)
    second_start = cos_row * jnp.sqrt(2.0 * order_col + 3.0) * diagonal_start
    zeros_grid = jnp.zeros_like(diagonal_start)

    def advance(state, degree):
        before, latest = state
        upper_ratio = jnp.sqrt(
            (4.0 * degree * degree - 1.0)
            / jnp.maximum(degree * degree - order_col * order_col, 1.0)
        )
        lower_ratio = jnp.sqrt(
            jnp.maximum((degree - 1.0) * (degree - 1.0) - order_col * order_col, 0.0)
            / jnp.maximum(4.0 * (degree - 1.0) * (degree - 1.0) - 1.0, 1.0)
        )
        general = upper_ratio * (cos_row * latest - lower_ratio * before)
        current = jnp.where(
            degree < order_col,
            0.0,
            jnp.where(
                degree == order_col,
                diagonal_start,
                jnp.where(degree == order_col + 1.0, second_start, general),
            ),
        )
        return ((latest, current), current)

    ignored, stacked = lax.scan(
        advance, (zeros_grid, zeros_grid), jnp.arange(degrees).astype(cosines.dtype)
    )
    stacked = jnp.transpose(stacked, (1, 0, 2))
    degree_index = jnp.arange(degrees).astype(cosines.dtype)
    keep = (orders[:, None, None] < M) & (degree_index[None, :, None] < L)
    return jnp.where(keep, stacked, 0.0)


def mix_modes(coeffs, spectral):
    product = jnp.einsum("bmlrc,lscd->bmlrsd", coeffs, spectral, preferred_element_type=jnp.float32)
    real_part = product[:, :, :, 0, 0] - product[:, :, :, 1, 1]
    imag_part = product[:, :, :, 0, 1] + product[:, :, :, 1, 0]
    return jnp.stack([real_part, imag_part], 3).astype(jnp.bfloat16)


def coeff_back(d_mixed, spectral):
    returned = jnp.einsum(
        "bmlsd,lrcd->bmlsrc", d_mixed, spectral, preferred_element_type=jnp.float32
    )
    d_real = returned[:, :, :, 0, 0] + returned[:, :, :, 1, 1]
    d_imag = returned[:, :, :, 1, 0] - returned[:, :, :, 0, 1]
    return jnp.stack([d_real, d_imag], 3).astype(jnp.bfloat16)


def weight_back(coeffs, d_mixed):
    outer_sum = jnp.einsum(
        "bmlrc,bmlsd->lrscd", coeffs, d_mixed, preferred_element_type=jnp.float32
    )
    d_weight_real = outer_sum[:, 0, 0] + outer_sum[:, 1, 1]
    d_weight_imag = outer_sum[:, 0, 1] - outer_sum[:, 1, 0]
    return jnp.stack([d_weight_real, d_weight_imag], 1)


def degree_shards(
    inputs,
    gain_one,
    shift_one,
    spectral,
    gain_two,
    shift_two,
    w_up,
    b_up,
    w_down,
    b_down,
    crops,
    cotangent,
    run_mean,
    run_var,
    momentum,
):
    lat_count = lax.axis_size("lat")
    lon_count = lax.axis_size("lon")
    rows_dev = inputs.shape[1]
    cols_dev = inputs.shape[2]
    width = inputs.shape[3]
    lat_rows = rows_dev * lat_count
    lon_cols = cols_dev * lon_count
    modes_dev = (M + lat_count - 1) // lat_count
    modes_all = modes_dev * lat_count
    quarter = width // lon_count
    owned = spectral.shape[0]
    degrees_all = owned * lat_count * lon_count
    forward_tab, inverse_tab = fourier_tables(lon_cols, modes_all)
    cosines, sine_vals = grid_angles(lat_rows)
    orders = (lax.axis_index("lat") * modes_dev + jnp.arange(modes_dev, dtype=jnp.int32)).astype(
        jnp.float32
    )
    poly = legendre_scan(orders, cosines, sine_vals, degrees_all)
    quadrature = sine_vals * (math.pi / GRID_ROWS) * (2.0 * math.pi / math.sqrt(lon_cols))
    analysis = (poly * quadrature[None, None, :]).astype(jnp.bfloat16)
    synthesis = (
        poly.astype(jnp.bfloat16)
        .reshape(modes_dev, lat_count, lon_count, owned, lat_rows)
        .transpose(0, 2, 1, 3, 4)
    )
    input_wide = inputs.astype(jnp.float32)
    normed_one, norm_one_back = jax.vjp(layer_norm, input_wide, gain_one, shift_one)
    normed_low = normed_one.astype(jnp.bfloat16)
    fourier = jnp.einsum(
        "bijc,jrm->birmc",
        lax.all_to_all(normed_low, "lon", split_axis=3, concat_axis=2, tiled=True),
        forward_tab,
        preferred_element_type=jnp.float32,
    ).astype(jnp.bfloat16)
    portion = lax.all_to_all(fourier, "lat", split_axis=3, concat_axis=1, tiled=True)
    coeffs = jnp.einsum(
        "mli,birmc->bmlrc", analysis, portion, preferred_element_type=jnp.float32
    ).astype(jnp.bfloat16)
    coeffs = coeffs.reshape(1, modes_dev, lat_count, lon_count, owned, 2, portion.shape[4])
    owned_coeffs = lax.all_to_all(
        lax.all_to_all(coeffs, "lat", split_axis=2, concat_axis=1, tiled=True),
        "lon",
        split_axis=3,
        concat_axis=6,
        tiled=True,
    )
    coeffs_owned = owned_coeffs.reshape(1, modes_all, owned, 2, width)
    mixed_modes = mix_modes(coeffs_owned, spectral).reshape(1, modes_all, 1, 1, owned, 2, width)
    returned = lax.all_to_all(
        lax.all_to_all(mixed_modes, "lat", split_axis=1, concat_axis=3, tiled=True),
        "lon",
        split_axis=6,
        concat_axis=2,
        tiled=True,
    )
    grid_modes = jnp.einsum(
        "mjkqi,bmjkqrc->birmc", synthesis, returned, preferred_element_type=jnp.float32
    ).astype(jnp.bfloat16)
    spread = jnp.einsum(
        "birmc,rmj->bijc",
        lax.all_to_all(grid_modes, "lat", split_axis=1, concat_axis=3, tiled=True),
        inverse_tab,
        preferred_element_type=jnp.float32,
    ).astype(jnp.bfloat16)
    spectral_out = lax.all_to_all(spread, "lon", split_axis=2, concat_axis=3, tiled=True)
    skipped = input_wide + spectral_out.astype(jnp.float32)
    normed_two, norm_two_back = jax.vjp(layer_norm, skipped, gain_two, shift_two)
    normed_two_low = normed_two.astype(jnp.bfloat16)
    preact = (
        jnp.einsum("bijc,ch->bijh", normed_two_low, w_up, preferred_element_type=jnp.float32) + b_up
    )
    activated, gelu_back = jax.vjp(jax.nn.gelu, preact)
    activated_low = activated.astype(jnp.bfloat16)
    result = (
        skipped
        + jnp.einsum("bijh,hc->bijc", activated_low, w_down, preferred_element_type=jnp.float32)
        + b_down
    )
    output = result.astype(jnp.bfloat16)
    bounds = crops[0]
    row_global = lax.axis_index("lat") * rows_dev + jnp.arange(rows_dev, dtype=jnp.int32)
    col_global = lax.axis_index("lon") * cols_dev + jnp.arange(cols_dev, dtype=jnp.int32)
    inside_rows = (row_global >= bounds[0]) & (row_global < bounds[1])
    inside_cols = (col_global >= bounds[2]) & (col_global < bounds[3])
    mask_grid = (inside_rows[:, None] & inside_cols[None, :]).astype(jnp.float32)[None, :, :, None]
    valid_count = jnp.sum(mask_grid)
    first_moment = jnp.sum(mask_grid * result, (0, 1, 2))
    second_moment = jnp.sum(mask_grid * result * result, (0, 1, 2))
    grad_wide = cotangent.astype(jnp.float32)
    d_down = jnp.einsum(
        "bijh,bijc->hc", activated_low, cotangent, preferred_element_type=jnp.float32
    )
    d_down_bias = jnp.sum(grad_wide, (0, 1, 2))
    d_activated = jnp.einsum("bijc,hc->bijh", cotangent, w_down, preferred_element_type=jnp.float32)
    d_preact = gelu_back(d_activated)[0].astype(jnp.bfloat16)
    d_up = jnp.einsum("bijc,bijh->ch", normed_two_low, d_preact, preferred_element_type=jnp.float32)
    d_up_bias = jnp.sum(d_preact.astype(jnp.float32), (0, 1, 2))
    d_normed_two = jnp.einsum("bijh,ch->bijc", d_preact, w_up, preferred_element_type=jnp.float32)
    d_skipped, d_gain_two, d_shift_two = norm_two_back(d_normed_two)
    d_skipped = d_skipped + grad_wide
    d_spread = d_skipped.astype(jnp.bfloat16)
    d_grid = jnp.einsum(
        "bijc,rmj->birmc",
        lax.all_to_all(d_spread, "lon", split_axis=3, concat_axis=2, tiled=True),
        inverse_tab,
        preferred_element_type=jnp.float32,
    ).astype(jnp.bfloat16)
    d_returned = jnp.einsum(
        "mjkqi,birmc->bmjkqrc",
        synthesis,
        lax.all_to_all(d_grid, "lat", split_axis=3, concat_axis=1, tiled=True),
        preferred_element_type=jnp.float32,
    ).astype(jnp.bfloat16)
    d_mixed = lax.all_to_all(
        lax.all_to_all(d_returned, "lat", split_axis=3, concat_axis=1, tiled=True),
        "lon",
        split_axis=2,
        concat_axis=6,
        tiled=True,
    ).reshape(1, modes_all, owned, 2, width)
    d_coeffs = coeff_back(d_mixed, spectral)
    d_spectral = lax.psum(weight_back(coeffs_owned, d_mixed).astype(jnp.bfloat16), "batch").astype(
        jnp.float32
    )
    d_coeffs_wide = d_coeffs.reshape(1, modes_all, 1, 1, owned, 2, width)
    d_modes = lax.all_to_all(
        lax.all_to_all(d_coeffs_wide, "lat", split_axis=1, concat_axis=2, tiled=True),
        "lon",
        split_axis=6,
        concat_axis=3,
        tiled=True,
    ).reshape(1, modes_dev, degrees_all, 2, quarter)
    d_fourier = jnp.einsum(
        "mli,bmlrc->birmc", analysis, d_modes, preferred_element_type=jnp.float32
    ).astype(jnp.bfloat16)
    d_columns = jnp.einsum(
        "birmc,jrm->bijc",
        lax.all_to_all(d_fourier, "lat", split_axis=1, concat_axis=3, tiled=True),
        forward_tab,
        preferred_element_type=jnp.float32,
    ).astype(jnp.bfloat16)
    d_normed_one = lax.all_to_all(d_columns, "lon", split_axis=2, concat_axis=3, tiled=True).astype(
        jnp.float32
    )
    d_input_norm, d_gain_one, d_shift_one = norm_one_back(d_normed_one)
    d_inputs = d_input_norm + d_skipped
    summed = lax.psum(
        (
            d_up,
            d_down,
            d_up_bias,
            d_down_bias,
            d_gain_one,
            d_shift_one,
            d_gain_two,
            d_shift_two,
            valid_count,
            first_moment,
            second_moment,
        ),
        ("lat", "lon", "batch"),
    )
    batch_mean = summed[9] / summed[8]
    batch_var = summed[10] / summed[8] - batch_mean * batch_mean
    new_mean = (1.0 - momentum) * run_mean + momentum * batch_mean
    new_var = (1.0 - momentum) * run_var + momentum * batch_var
    return (
        output,
        d_inputs,
        summed[4],
        summed[5],
        d_spectral,
        summed[6],
        summed[7],
        summed[0],
        summed[2],
        summed[1],
        summed[3],
        new_mean,
        new_var,
    )


def shards(inputs, *rest):
    rows_dev = inputs.shape[1]
    lon_count = lax.axis_size("lon")
    banded = (
        lon_count == 4
        and lax.axis_size("batch") == 2
        and rows_dev == 2 * lon_count
        and M % lon_count == 0
        and M // lon_count <= 128
        and rest[2].shape[0] % 4 in (0, 3)
        and rows_dev * lax.axis_size("lat") <= 32
    )
    return (band_shards if banded else degree_shards)(inputs, *rest)


def solution(mesh):
    return jax.shard_map(
        shards,
        mesh=mesh,
        in_specs=(
            P("batch", "lat", "lon", None),
            P(),
            P(),
            P(("lat", "lon"), None, None, None),
            P(),
            P(),
            P(),
            P(),
            P(),
            P(),
            P("batch", None),
            P("batch", "lat", "lon", None),
            P(),
            P(),
            P(),
        ),
        out_specs=(
            P("batch", "lat", "lon", None),
            P("batch", "lat", "lon", None),
            P(),
            P(),
            P(("lat", "lon"), None, None, None),
            P(),
            P(),
            P(),
            P(),
            P(),
            P(),
            P(),
            P(),
        ),
        check_vma=False,
    )
```

```python
import math

import jax
import jax.numpy as jnp
from jax import lax
from jax.experimental import pallas as pl
from jax.experimental.pallas import tpu as pltpu
from jax.sharding import PartitionSpec as P

GRID_ROWS = 360
M = 360
L = 360


epsilon = 1e-05
GROUP = 8
CHUNKS = 2
PER_STEP = 6


def layer_norm(values, gain, shift):
    centre = values - jnp.mean(values, -1, keepdims=True)
    spread = jnp.mean(centre * centre, -1, keepdims=True)
    return centre * lax.rsqrt(spread + epsilon) * gain + shift


def xor_pairs(count, bit):
    return [(i, i ^ bit) for i in range(count)]


def ring_pairs(count, step):
    return [(i, (i + step) % count) for i in range(count)]


def swap_cores(values):
    return lax.ppermute(values, "batch", xor_pairs(2, 1))


def near(values):
    return lax.ppermute(values, "lon", xor_pairs(4, 1))


def far(values):
    return lax.ppermute(values, "lon", xor_pairs(4, 2))


def after(values, earlier):
    return lax.optimization_barrier((values, earlier))[0]


def trade(values):
    return lax.all_to_all(values, "lon", split_axis=0, concat_axis=0, tiled=True)


def cross(values, k):
    return lax.ppermute(values, "lon", xor_pairs(4, k))


def trade_pieces(pieces):
    return [pieces[0]] + [cross(pieces[k], k) for k in (1, 2, 3)]


def gathered(values, name):
    count = lax.axis_size(name)
    pairs = xor_pairs if name == "lon" else ring_pairs
    return [values] + [lax.ppermute(values, name, pairs(count, k)) for k in range(1, count)]


def in_order(pieces, name):
    at, count = lax.axis_index(name), len(pieces)
    pieces = jnp.stack(pieces, 0)
    where = lambda place: at ^ place if name == "lon" else (at - place) % count
    return [lax.dynamic_index_in_dim(pieces, where(place), 0, keepdims=False) for place in range(count)]


def sum_over_planes(values):
    return sum(in_order(gathered(values, "lat"), "lat"))


def dot(a, b):
    return jnp.dot(a, b, preferred_element_type=jnp.float32)


def dot_along(a, b):
    return lax.dot_general(a, b, (((1,), (1,)), ((), ())), preferred_element_type=jnp.float32)


def dot_across(a, b):
    return lax.dot_general(a, b, (((0,), (0,)), ((), ())), preferred_element_type=jnp.float32)


def low(values):
    return values.astype(jnp.bfloat16)


def wide(values):
    return values.astype(jnp.float32)


NO_COST = pl.CostEstimate(flops=0, transcendentals=0, bytes_accessed=0)


def params(megabytes):
    return pltpu.CompilerParams(vmem_limit_bytes=megabytes * 2**20)


def turned(cosine, sine, quarter_turns):
    turns = quarter_turns % 4
    real = jnp.where(turns == 0, cosine, jnp.where(turns == 1, -sine, jnp.where(turns == 2, -cosine, sine)))
    imag = jnp.where(turns == 0, -sine, jnp.where(turns == 1, -cosine, jnp.where(turns == 2, sine, cosine)))
    return real, imag


def dft_tables(points, parts, order, valid, axis):
    cols = points // parts
    column = jnp.arange(cols, dtype=jnp.int32)
    if axis == 1:
        order, valid, column = order[:, None], valid[:, None], column[None, :]
    else:
        order, valid, column = order[None, :], valid[None, :], column[:, None]
    angle = (order * column % points).astype(jnp.float32) * (2.0 * math.pi / points)
    cosine = jnp.where(valid, jnp.cos(angle), 0.0)
    sine = jnp.where(valid, jnp.sin(angle), 0.0)
    cosine, sine = lax.optimization_barrier((cosine, sine))
    part = jnp.arange(parts, dtype=jnp.int32)[:, None, None]
    real, imag = turned(cosine[None], sine[None], part * order[None])
    scales = (1.0 / math.sqrt(points), jnp.where(order == 0, 1.0, 2.0)[None])
    return [jnp.concatenate([low(real * scale), low(imag * scale)], axis) for scale in scales]


def legendre_kernel(cut, starts_ref, upper_ref, lower_ref, order_ref, cos_ref, diag_ref, second_ref, out_ref, all_ref):
    degrees = all_ref.shape[0]
    cosines = cos_ref[...]
    diagonal = diag_ref[...]
    second = second_ref[...]
    order = order_ref[...]

    def advance(degree, state):
        before, latest = state
        level = degree.astype(jnp.float32)
        upper = upper_ref[pl.ds(degree, 1), :]
        lower = lower_ref[pl.ds(degree, 1), :]
        general = upper * (cosines * latest - lower * before)
        current = jnp.where(
            level < order,
            0.0,
            jnp.where(level == order, diagonal, jnp.where(level == order + 1.0, second, general)),
        )
        all_ref[pl.ds(degree, 1)] = current[None]
        return latest, current

    unroll = 8 if degrees % 8 == 0 else 1

    def several(step, state):
        for at in range(unroll):
            state = advance(step * unroll + at, state)
        return state

    zeros = cosines * 0.0
    lax.fori_loop(0, degrees // unroll, several, (zeros, zeros))
    blocks = out_ref.shape[0] // (2 * cut)
    for block in range(blocks):
        for half in range(2):

            def copy(at, carry, block=block, half=half):
                degree = starts_ref[block] + half * cut + at
                value = all_ref[pl.ds(degree, 1)]
                keep = (degree < L) & (half * cut + at >= starts_ref[blocks])
                out_ref[pl.ds((at * 2 + half) * blocks + block, 1)] = jnp.where(keep, value, 0.0)
                return carry

            lax.fori_loop(0, cut, copy, 0)


def legendre(starts, skip, orders, valid, cosines, sine_vals, degrees, cut):
    order_row = orders[None, :]
    sine_col = sine_vals[:, None]
    log_start = 0.5 * (
        jnp.log((2.0 * order_row + 1.0) / (4.0 * math.pi))
        + lax.lgamma(order_row + 0.5)
        - lax.lgamma(order_row + 1.0)
        - 0.5 * math.log(math.pi)
    ) + order_row * jnp.log(sine_col)
    diagonal = jnp.where(valid[None, :], jnp.exp(log_start), 0.0)
    second = cosines[:, None] * jnp.sqrt(2.0 * order_row + 3.0) * diagonal
    degree = jnp.arange(degrees, dtype=jnp.float32)[:, None]
    upper = jnp.sqrt((4.0 * degree * degree - 1.0) / jnp.maximum(degree * degree - order_row * order_row, 1.0))
    lower = jnp.sqrt(
        jnp.maximum((degree - 1.0) * (degree - 1.0) - order_row * order_row, 0.0)
        / jnp.maximum(4.0 * (degree - 1.0) * (degree - 1.0) - 1.0, 1.0)
    )
    shape = diagonal.shape
    return pl.pallas_call(
        lambda *refs: legendre_kernel(cut, *refs),
        out_shape=jax.ShapeDtypeStruct((starts.shape[0] * 2 * cut,) + shape, jnp.float32),
        in_specs=[pl.BlockSpec(memory_space=pltpu.SMEM)] + [pl.BlockSpec(memory_space=pltpu.VMEM)] * 6,
        out_specs=pl.BlockSpec(memory_space=pltpu.VMEM),
        scratch_shapes=[pltpu.VMEM((degrees,) + shape, jnp.float32)],
        cost_estimate=NO_COST,
        compiler_params=params(24),
        name="legendre",
    )(
        jnp.concatenate([starts, skip[None]]).astype(jnp.int32),
        upper,
        lower,
        jnp.broadcast_to(order_row, shape),
        jnp.broadcast_to(cosines[:, None], shape),
        diagonal,
        second,
    )


def block_tables(poly, slots):
    degrees, rows, _ = poly.shape
    groups = slots // GROUP
    values = low(poly[:, :, :slots]).reshape(degrees, rows, groups, GROUP)

    def expand(table, depth):
        lanes = depth * GROUP
        lane = jnp.arange(lanes, dtype=jnp.int32)
        repeat = low(jnp.arange(depth, dtype=jnp.int32)[:, None] == lane[None, :] // GROUP)
        flat = table.reshape(-1, depth)
        row = jnp.arange(flat.shape[0], dtype=jnp.int32)
        same = row[:, None] % GROUP == lane[None, :] % GROUP
        return low(jnp.where(same, dot(flat, repeat), 0.0)).reshape(groups, -1, lanes)

    return expand(values.transpose(2, 0, 3, 1), rows), expand(values.transpose(2, 1, 3, 0), degrees)


def normalise(values):
    centre = values - jnp.mean(values, -1, keepdims=True)
    factor = lax.rsqrt(jnp.mean(centre * centre, -1, keepdims=True) + epsilon)
    return centre * factor, factor


def normalise_back(normal, factor, grad):
    return factor * (
        grad - jnp.mean(grad, -1, keepdims=True) - normal * jnp.mean(grad * normal, -1, keepdims=True)
    )


def column_sum(values):
    return jnp.sum(values, 0, keepdims=True)


def store_modes(totals, refs):
    groups, _, double = refs[0].shape
    width = double // 2
    slots = groups * GROUP
    for part in range(2):
        for owner, ref in enumerate(refs):
            at = (part * len(refs) + owner) * slots
            rows = [total[at : at + slots].reshape(groups, GROUP, width) for total in totals]
            ref[:, :, part * width : part * width + width] = low(jnp.concatenate(rows, 1))


def load_modes(refs, flat_ref):
    groups, _, double = refs[0].shape
    width = double // 2
    slots = groups * GROUP
    rows = flat_ref.shape[1] // width
    half = flat_ref.shape[0] // 2
    for piece, ref in enumerate(refs):
        owner, chunk = piece // CHUNKS, piece % CHUNKS
        at = (owner * CHUNKS + chunk) * slots
        modes = wide(ref[...]).reshape(groups, rows, GROUP, double)
        for row in range(rows):
            flat = low(modes[:, row].reshape(slots, double))
            lanes = slice(row * width, row * width + width)
            flat_ref[at : at + slots, lanes] = flat[:, :width]
            flat_ref[half + at : half + at + slots, lanes] = flat[:, width:]


def whole_spec(array):
    return pl.BlockSpec(array.shape, lambda *at: (0,) * len(array.shape))


def enter_kernel(weight_ref, table_ref, values_ref, gain_ref, shift_ref, *out_refs):
    totals = []
    for row in range(values_ref.shape[1]):
        total = 0.0
        for part in range(table_ref.shape[0]):
            normal, _ = normalise(wide(values_ref[part, row]))
            total += dot(table_ref[part], low(normal * gain_ref[...] + shift_ref[...]))
        totals.append(total * weight_ref[row])
    store_modes(totals, out_refs)


def enter(weight, table, values, gain, shift, groups):
    parts, rows, cols, width = values.shape
    arrays = [table, values, gain[None], shift[None]]
    return pl.pallas_call(
        enter_kernel,
        out_shape=[jax.ShapeDtypeStruct((groups, rows * GROUP, 2 * width), jnp.bfloat16)] * parts,
        in_specs=[pl.BlockSpec(memory_space=pltpu.SMEM)] + [pl.BlockSpec(memory_space=pltpu.VMEM)] * 4,
        out_specs=[pl.BlockSpec(memory_space=pltpu.VMEM)] * parts,
        cost_estimate=NO_COST,
        compiler_params=params(32),
        name="enter",
    )(weight, *arrays)


def gelu_parts(values):
    slope = math.sqrt(2.0 / math.pi)
    square = values * values
    tangent = jnp.tanh(slope * values * (1.0 + 0.044715 * square))
    half = 0.5 * (1.0 + tangent)
    grad = half + 0.5 * values * (1.0 - tangent * tangent) * slope * (1.0 + 3.0 * 0.044715 * square)
    return values * half, grad


def feed_kernel(pieces, where_ref, *refs):
    modes_refs, refs = refs[:pieces], refs[pieces:]
    (columns_ref, modes_table_ref, values_ref, cotangent_ref), refs = refs[:4], refs[4:]
    (gain_ref, shift_ref, up_ref, up_bias_ref, down_ref, down_bias_ref), refs = refs[:6], refs[6:]
    *grid_refs, output_ref, d_skipped_ref, sums_ref, flat_ref, total_ref = refs
    part, parts = pl.program_id(0), pl.num_programs(0)
    _, rows, cols, width = values_ref.shape
    hidden = up_ref.shape[-1]

    @pl.when(part == 0)
    def _():
        load_modes(modes_refs, flat_ref)
        sums_ref[...] = jnp.zeros_like(sums_ref)
        total_ref[...] = jnp.zeros_like(total_ref)

    spreads = low(dot(columns_ref[0], flat_ref[...]))
    column_at = where_ref[5] + part * cols + lax.broadcasted_iota(jnp.int32, (cols, 1), 0)
    inside_columns = (column_at >= where_ref[2]) & (column_at < where_ref[3])
    grads, sums = [], []
    for row in range(rows):
        skipped = wide(values_ref[0, row]) + wide(spreads[:, row * width : row * width + width])
        normal, factor = normalise(skipped)
        normed = low(normal * gain_ref[...] + shift_ref[...])
        activated, slope = gelu_parts(dot(normed, up_ref[...]) + up_bias_ref[...])
        activated = low(activated)
        result = skipped + dot(activated, down_ref[...]) + down_bias_ref[...]
        output_ref[0, row] = low(result)
        row_at = where_ref[4] + row
        kept = jnp.where(inside_columns & (row_at >= where_ref[0]) & (row_at < where_ref[1]), result, 0.0)

        cotangent = cotangent_ref[0, row]
        d_preact = low(dot_along(cotangent, down_ref[...]) * slope)
        d_normed = dot_along(d_preact, up_ref[...])
        d_skipped = wide(cotangent) + normalise_back(normal, factor, d_normed * gain_ref[...])
        d_skipped_ref[0, row] = d_skipped
        grads.append(low(d_skipped))
        d_bias = column_sum(wide(d_preact))
        vectors = [d_bias[:, j * width : j * width + width] for j in range(hidden // width)] + [
            column_sum(wide(cotangent)),
            column_sum(d_normed * normal),
            column_sum(d_normed),
            column_sum(kept),
            column_sum(kept * kept),
        ]
        sums.append([dot_across(normed, d_preact), dot_across(activated, cotangent)] + vectors)

    total_ref[...] += dot(modes_table_ref[0], jnp.concatenate(grads, 1))

    @pl.when(part == parts - 1)
    def _():
        store_modes([total_ref[:, row * width : row * width + width] for row in range(rows)], grid_refs)

    d_up, d_down, *vectors = [sum(terms) for terms in zip(*sums)]
    for at in range(hidden // width):
        sums_ref[at * width : at * width + width] += d_up[:, at * width : at * width + width]
    sums_ref[hidden : 2 * hidden] += d_down
    at = 2 * hidden
    for j, vector in enumerate(vectors):
        sums_ref[at + j : at + j + 1] += vector


def feed(where, modes, columns, modes_table, values, cotangent, gain, shift, w_up, b_up, w_down, b_down):
    parts, rows, cols, width = values.shape
    hidden = w_up.shape[1]
    lanes = modes_table.shape[1]
    grid = (CHUNKS * modes[0].shape[0],) + modes[0].shape[1:]
    cells = pl.BlockSpec((1, rows, cols, width), lambda p: (p, 0, 0, 0))
    by_part = lambda table: pl.BlockSpec((1,) + table.shape[1:], lambda p: (p, 0, 0))
    small = [gain[None], shift[None], w_up, b_up[None], w_down, b_down[None]]
    outs = [jax.ShapeDtypeStruct(grid, jnp.bfloat16)] * parts + [
        jax.ShapeDtypeStruct(values.shape, jnp.bfloat16),
        jax.ShapeDtypeStruct(values.shape, jnp.float32),
        jax.ShapeDtypeStruct(((2 * hidden + hidden // width + 5 + 63) // 64 * 64, width), jnp.float32),
    ]
    return pl.pallas_call(
        lambda *refs: feed_kernel(len(modes), *refs),
        grid=(parts,),
        out_shape=outs,
        in_specs=[pl.BlockSpec(memory_space=pltpu.SMEM)]
        + [whole_spec(m) for m in modes]
        + [by_part(columns), by_part(modes_table), cells, cells]
        + [whole_spec(v) for v in small],
        out_specs=[whole_spec(outs[0])] * parts + [cells, cells, whole_spec(outs[-1])],
        scratch_shapes=[pltpu.VMEM((lanes, rows * width), jnp.bfloat16), pltpu.VMEM((lanes, rows * width), jnp.float32)],
        cost_estimate=NO_COST,
        compiler_params=params(60),
        name="feed",
    )(where, *modes, columns, modes_table, values, cotangent, *small)


def leave_kernel(pieces, weight_ref, *refs):
    modes_refs, refs = refs[:pieces], refs[pieces:]
    columns_ref, values_ref, d_skipped_ref, gain_ref, out_ref, sums_ref, flat_ref = refs
    _, rows, _, width = values_ref.shape

    @pl.when(pl.program_id(0) == 0)
    def _():
        load_modes(modes_refs, flat_ref)
        sums_ref[...] = jnp.zeros_like(sums_ref)

    columns = dot(columns_ref[0], flat_ref[...])
    for row in range(rows):
        d_normed = wide(low(columns[:, row * width : row * width + width] * weight_ref[row]))
        normal, factor = normalise(wide(values_ref[0, row]))
        out_ref[0, row] = low(normalise_back(normal, factor, d_normed * gain_ref[...]) + d_skipped_ref[0, row])
        sums_ref[0:1] += column_sum(d_normed * normal)
        sums_ref[1:2] += column_sum(d_normed)


def leave(weight, modes, columns, values, d_skipped, gain):
    parts, rows, cols, width = values.shape
    cells = pl.BlockSpec((1, rows, cols, width), lambda p: (p, 0, 0, 0))
    return pl.pallas_call(
        lambda *refs: leave_kernel(len(modes), *refs),
        grid=(parts,),
        out_shape=[jax.ShapeDtypeStruct(values.shape, jnp.bfloat16), jax.ShapeDtypeStruct((8, width), jnp.float32)],
        in_specs=[pl.BlockSpec(memory_space=pltpu.SMEM)]
        + [whole_spec(m) for m in modes]
        + [
            pl.BlockSpec((1,) + columns.shape[1:], lambda p: (p, 0, 0)),
            cells,
            cells,
            pl.BlockSpec((1, width), lambda p: (0, 0)),
        ],
        out_specs=[cells, pl.BlockSpec((8, width), lambda p: (0, 0))],
        scratch_shapes=[pltpu.VMEM((columns.shape[2], rows * width), jnp.bfloat16)],
        cost_estimate=NO_COST,
        compiler_params=params(32),
        name="leave",
    )(weight, *modes, columns, values, d_skipped, gain[None])


def complex_weight(weight_ref):
    real, imag = weight_ref[0, 0], weight_ref[0, 1]
    return jnp.concatenate([jnp.concatenate([real, imag], 1), jnp.concatenate([-imag, real], 1)], 0)


class Core:
    def __init__(self, shard, slots, degrees, cut, rows, table, weights, back_table):
        self.slots, self.cut, self.degrees = slots, cut, degrees
        self.steps = shard[1] // PER_STEP
        ends = CHUNKS * self.steps
        self.first = ends if table is not None else 0
        self.last = ends if back_table is not None else 0
        self.grid = (self.first + cut + self.last,)
        self.modes = (degrees, CHUNKS * shard[1]) + shard[2:]
        self.per = degrees // cut
        block = (shard[0], PER_STEP) + shard[2:]
        place = lambda step, start, count: jnp.clip(step - start, 0, count - 1)
        self.middle = lambda s: place(s, self.first, cut)
        self.arrays, self.in_specs = [], []
        for chunk in range(CHUNKS if self.first else 0):
            spec = pl.BlockSpec(block, lambda s, chunk=chunk: (0, place(s, chunk * self.steps, self.steps), 0, 0))
            self.take([slot for sample in rows[chunk] for slot in sample], spec)
        if self.first:
            self.take([table], pl.BlockSpec((PER_STEP,) + table.shape[1:], lambda s: (place(s, 0, ends), 0, 0)))
        start = self.first + cut
        if self.last:
            spec = pl.BlockSpec((PER_STEP,) + back_table.shape[1:], lambda s: (place(s, start, ends), 0, 0))
            self.take([back_table], spec)
        self.take(weights, pl.BlockSpec((1,) + weights[0].shape[1:], lambda s: (self.middle(s), 0, 0, 0)))
        self.modes_spec = pl.BlockSpec((self.per,) + self.modes[1:], lambda s: (self.middle(s), 0, 0, 0))
        self.modes_shape = jax.ShapeDtypeStruct(self.modes, jnp.bfloat16)
        self.held = pltpu.VMEM(self.modes, jnp.bfloat16)
        self.out_specs, self.out_shape = [], []
        for chunk in range(CHUNKS if self.last else 0):
            at = lambda s, chunk=chunk: (0, 0, place(s, start + chunk * self.steps, self.steps), 0, 0)
            self.out_specs += [pl.BlockSpec((slots,) + block, at)] * 2
            self.out_shape += [jax.ShapeDtypeStruct((slots,) + shard, jnp.bfloat16)] * 2

    def take(self, arrays, spec):
        self.arrays += arrays
        self.in_specs += [spec] * len(arrays)

    def split(self, refs):
        at = CHUNKS * 2 * self.slots if self.first else 0
        shards, refs = refs[:at], refs[at:]
        table, refs = (refs[0], refs[1:]) if self.first else (None, refs)
        back_table, refs = (refs[0], refs[1:]) if self.last else (None, refs)
        count = len(self.arrays) - at - (table is not None) - (back_table is not None)
        return shards, table, back_table, refs[:count], refs[count:]

    def analyse(self, shard_refs, table_ref, held_ref):
        step = pl.program_id(0)
        for chunk in range(CHUNKS):
            refs = shard_refs[chunk * 2 * self.slots : (chunk + 1) * 2 * self.slots]

            @pl.when((step >= chunk * self.steps) & (step < (chunk + 1) * self.steps))
            def _(refs=refs):
                for at in range(PER_STEP):
                    samples = []
                    for sample in range(2):
                        rows = [flat_rows(ref[:, at]) for ref in refs[sample * self.slots : (sample + 1) * self.slots]]
                        total = dot(table_ref[at], jnp.concatenate(rows, 0))
                        samples.append(total.reshape(self.degrees, GROUP, -1))
                    held_ref[:, pl.ds(step * PER_STEP + at, 1)] = low(jnp.concatenate(samples, 1))[:, None]

    def synthesise(self, table_ref, held_ref, out_refs):
        step = pl.program_id(0) - self.first - self.cut
        for chunk in range(CHUNKS):
            refs = out_refs[2 * chunk : 2 * chunk + 2]

            @pl.when((step >= chunk * self.steps) & (step < (chunk + 1) * self.steps))
            def _(refs=refs):
                for at in range(PER_STEP):
                    modes = wide(held_ref[:, pl.ds(step * PER_STEP + at, 1)])
                    modes = modes.reshape(self.degrees, 2, GROUP, modes.shape[-1])
                    for sample, ref in enumerate(refs):
                        total = low(dot(table_ref[at], low(flat_rows(modes[:, sample]))))
                        ref[:, :, at] = total.reshape(ref.shape[:2] + ref.shape[3:])

    def in_middle(self):
        step = pl.program_id(0)
        return (step >= self.first) & (step < self.first + self.cut)

    def degree(self, at):
        return self.middle(pl.program_id(0)) * self.per + at

    def chunks(self, out):
        return [out[2 * chunk : 2 * chunk + 2] for chunk in range(CHUNKS)]


def flat_rows(modes):
    return modes.reshape(-1, modes.shape[-1])


def mix_forward(rows, table, back_table, weights, cut):
    shard = rows[0][0][0].shape
    core = Core(shard, len(rows[0][0]), len(weights) * cut, cut, rows, table, weights, back_table)

    def kernel(*refs):
        shards, table, back_table, weight_refs, (*out_refs, coeffs_ref, held_ref, mixed_ref) = core.split(refs)
        core.analyse(shards, table, held_ref)

        @pl.when(core.in_middle())
        def _():
            for at, weight_ref in enumerate(weight_refs):
                coeffs = held_ref[core.degree(at)]
                coeffs_ref[at] = coeffs
                mixed = low(dot(flat_rows(coeffs), complex_weight(weight_ref)))
                mixed_ref[core.degree(at)] = mixed.reshape(coeffs.shape)

        core.synthesise(back_table, mixed_ref, out_refs)

    out = pl.pallas_call(
        kernel,
        grid=core.grid,
        out_shape=core.out_shape + [core.modes_shape],
        in_specs=core.in_specs,
        out_specs=core.out_specs + [core.modes_spec],
        scratch_shapes=[core.held, core.held],
        cost_estimate=NO_COST,
        compiler_params=params(60),
        name="mix_forward",
    )(*core.arrays)
    return core.chunks(out), out[-1]


def mix_backward(rows, table, back_table, weights, cut, coeffs):
    shard = rows[0][0][0].shape
    core = Core(shard, len(rows[0][0]), len(weights) * cut, cut, rows, table, weights, back_table)
    weight = weights[0].shape
    grad = pl.BlockSpec((1,) + weight[1:], lambda s: (core.middle(s), 0, 0, 0))

    def kernel(*refs):
        shards, table, back_table, weight_refs, (coeffs_ref, *outs, held_ref, mixed_ref) = core.split(refs)
        core.analyse(shards, table, held_ref)

        @pl.when(core.in_middle())
        def _():
            for at, (weight_ref, target) in enumerate(zip(weight_refs, outs[-len(weights) :])):
                d_mixed = held_ref[core.degree(at)]
                d_coeffs = low(dot_along(flat_rows(d_mixed), complex_weight(weight_ref)))
                mixed_ref[core.degree(at)] = d_coeffs.reshape(d_mixed.shape)
                width = target.shape[-1]
                left, right = flat_rows(coeffs_ref[at]), flat_rows(d_mixed)
                turned_right = jnp.concatenate([right[:, width:], -right[:, :width]], 1)
                total = dot_across(
                    jnp.concatenate([left[:, :width], left[:, width:]], 0), jnp.concatenate([right, turned_right], 0)
                )
                target[0, 0] = low(total[:, :width])
                target[0, 1] = low(total[:, width:])

        core.synthesise(back_table, mixed_ref, outs[: -len(weights)])

    out = pl.pallas_call(
        kernel,
        grid=core.grid,
        out_shape=core.out_shape + [jax.ShapeDtypeStruct(weight, jnp.bfloat16)] * len(weights),
        in_specs=core.in_specs + [core.modes_spec],
        out_specs=core.out_specs + [grad] * len(weights),
        scratch_shapes=[core.held, core.held],
        cost_estimate=NO_COST,
        compiler_params=params(60),
        name="mix_backward",
    )(*core.arrays, coeffs)
    return core.chunks(out), out[-len(weights) :]


def gather_rows(shards, gate):
    count = lax.axis_size("lat")
    own = [[shard] for shard in shards]
    for step in range(1, count):
        earlier = gate(step, own)
        sent = [rows[-1] for rows in own]
        if earlier is not None:
            sent[-1] = after(sent[-1], earlier)
        own = [rows + [lax.ppermute(rows_sent, "lat", ring_pairs(count, 1))] for rows, rows_sent in zip(own, sent)]
    return [(rows, [swap_cores(slot) for slot in rows]) for rows in own]


def scatter_rows(own, other, gate=None, sent=None):
    count = lax.axis_size("lat")
    other = swap_cores(other)
    arrived = None
    for slot in range(count - 1, -1, -1):
        total = wide(own[slot]) + wide(other[slot])
        if arrived is not None:
            total = total + wide(arrived)
        total = low(total)
        if slot == 1:
            midway = total
        if slot == count - 1 and sent is not None:
            sent.append(total)
        if slot > 0:
            arrived = lax.ppermute(total, "lat", ring_pairs(count, -1))
            if slot == 2 and gate is not None:
                arrived = after(arrived, gate)
    return total, midway


def gather_weights(own):
    cut = own.shape[0] // 2
    first, last = own[:cut], own[cut:]
    return first, last, near(first), far(last)


def scatter_weights(grads):
    three = near(grads[3]), far(grads[7])
    one, two = after((grads[1], grads[6]), three)
    return three, (near(one), far(two))


def finish_weight_sum(grads, three, gate):
    from_near, from_far = after(three, gate)
    return far(low(wide(grads[2]) + wide(from_near))), near(low(wide(grads[5]) + wide(from_far)))


def sum_weights(grads, single, double):
    first = low(wide(grads[0]) + wide(single[0]) + wide(double[0]))
    last = low(wide(grads[4]) + wide(single[1]) + wide(double[1]))
    return first, last


class PartSum:
    def __init__(self, values):
        core = lax.axis_index("batch")
        half = values.shape[0] // 2
        self.mine = lax.dynamic_slice_in_dim(values, core * half, half, 0)
        self.other = swap_cores(lax.dynamic_slice_in_dim(values, (1 - core) * half, half, 0))

    def cores(self):
        return self.mine + self.other

    def chips(self, values):
        chip = lax.axis_index("lon")
        part = values.shape[0] // 4
        for_chip = lambda k: lax.dynamic_slice_in_dim(values, (chip ^ k) * part, part, 0)
        return sum(trade_pieces([for_chip(k) for k in range(4)]))

    def share(self, pieces):
        return jnp.concatenate(in_order(pieces, "lon"), 0)

    def finish(self, mine, other):
        core = lax.axis_index("batch")
        return jnp.concatenate([jnp.where(core == 0, mine, other), jnp.where(core == 0, other, mine)], 0)


def band_shards(
    inputs,
    gain_one,
    shift_one,
    spectral,
    gain_two,
    shift_two,
    w_up,
    b_up,
    w_down,
    b_down,
    crops,
    cotangent,
    run_mean,
    run_var,
    momentum,
):
    lat_count = lax.axis_size("lat")
    lon_count = lax.axis_size("lon")
    plane = lax.axis_index("lat")
    chip = lax.axis_index("lon")
    core = lax.axis_index("batch")
    rows_dev = inputs.shape[1]
    cols_dev = inputs.shape[2]
    width = inputs.shape[3]
    rows_chip = rows_dev // lon_count
    lat_rows = rows_dev * lat_count
    lon_cols = cols_dev * lon_count
    modes_dev = M // lon_count
    slots = (modes_dev + CHUNKS * PER_STEP * GROUP - 1) // (CHUNKS * PER_STEP * GROUP) * PER_STEP * GROUP
    groups = slots // GROUP
    owned = spectral.shape[0]
    cut = (owned + 3) // 4
    half = 2 * cut
    first_degree = core * (owned - half)
    skip = core * (2 * half - owned)
    by_row = (lon_count, rows_chip, cols_dev, width)

    first_hop = gather_weights(lax.dynamic_slice_in_dim(spectral, first_degree, half, 0))
    values = trade(inputs.reshape(by_row))

    across = chip ^ jnp.arange(lon_count, dtype=jnp.int32)
    in_chip = jnp.arange(CHUNKS * slots, dtype=jnp.int32)
    first_order = across[:, None] * modes_dev + in_chip[None, :]
    valid = jnp.broadcast_to(in_chip[None, :] < modes_dev, first_order.shape)
    order = jnp.where(valid, first_order, 0)
    to_modes, to_modes_back = dft_tables(lon_cols, lon_count, order.reshape(-1), valid.reshape(-1), 1)
    to_columns_back, to_columns = dft_tables(lon_cols, lon_count, order.reshape(-1), valid.reshape(-1), 2)
    first_row = (GRID_ROWS - lat_rows) // 2
    slot_plane = (plane - jnp.arange(lat_count, dtype=jnp.int32)) % lat_count
    row = across[:, None] * rows_chip + jnp.arange(rows_chip, dtype=jnp.int32)[None, :]
    row = (slot_plane[:, None] * rows_dev + row.reshape(1, -1)).reshape(-1)
    colatitude = (row.astype(jnp.float32) + (first_row + 0.5)) * (math.pi / GRID_ROWS)
    lane = jnp.arange(128, dtype=jnp.int32)
    orders = (chip * modes_dev + jnp.minimum(lane, modes_dev - 1)).astype(jnp.float32)
    owners = plane * lon_count + across
    poly = legendre(
        owners * owned + first_degree,
        skip,
        orders,
        lane < modes_dev,
        jnp.cos(colatitude),
        jnp.sin(colatitude),
        owned * lat_count * lon_count,
        cut,
    )
    analysis, synthesis = block_tables(poly, CHUNKS * slots)
    own_row = plane * rows_dev + chip * rows_chip
    angle = (own_row + jnp.arange(rows_chip, dtype=jnp.int32)).astype(jnp.float32) + (first_row + 0.5)
    quadrature = jnp.sin(angle * (math.pi / GRID_ROWS)) * ((math.pi / GRID_ROWS) * (2.0 * math.pi / math.sqrt(lon_cols)))

    def by_plane(pieces):
        return [
            jnp.stack([piece[chunk * groups : (chunk + 1) * groups] for piece in pieces], 0) for chunk in range(CHUNKS)
        ]

    def by_chip(chunks):
        traded = [trade_pieces([chunk[k] for k in range(lon_count)]) for chunk in chunks]
        return [traded[chunk][k] for k in range(lon_count) for chunk in range(CHUNKS)]

    values = after(values, (poly, analysis))
    pieces = trade_pieces(enter(quadrature, to_modes, values, gain_one, shift_one, CHUNKS * groups))
    shards_in = by_plane(pieces)
    first, last, near_first, far_last = after(first_hop, pieces[1])
    second_hop = (near(last), far(first))
    third_hop = (far(near_first), near(far_last))
    late = {2: synthesis, 3: (second_hop, to_columns, to_modes_back, to_columns_back)}
    rows_in = gather_rows(shards_in, lambda step, own: late.get(step))
    weights = [first, near_first, second_hop[1], third_hop[0], last, second_hop[0], far_last, third_hop[1]]
    partial, coeffs = mix_forward(rows_in, analysis, synthesis, weights, cut)
    sent = []
    grid = [scatter_rows(*partial[0], sent=sent)[0]]
    grads = trade(after(cotangent, sent).reshape(by_row))
    grid = by_chip(grid + [scatter_rows(*chunk, gate=grads)[0] for chunk in partial[1:]])

    where = jnp.concatenate([crops[0], own_row[None], jnp.zeros((1,), jnp.int32)])
    *d_grid, output, d_skipped, sums = feed(
        where, grid, to_columns, to_modes_back, values, grads, gain_two, shift_two, w_up, b_up, w_down, b_down
    )
    bounds = crops[0]
    count_rows = jnp.minimum(bounds[1], own_row + rows_chip) - jnp.maximum(bounds[0], own_row)
    count_cols = jnp.minimum(bounds[3], lon_cols) - jnp.maximum(bounds[2], 0)
    valid_count = (jnp.maximum(count_rows, 0) * jnp.maximum(count_cols, 0)).astype(jnp.float32)
    count_row = sums.shape[0] - 1
    sums = sums + jnp.where(jnp.arange(sums.shape[0]) == count_row, valid_count, 0.0)[:, None]

    shards_back = by_plane(trade_pieces(d_grid))
    traded = []

    def gate(step, own):
        if step == 2:
            traded.append(trade(after(output, own[0][1])))
        return traded[0] if step == 3 else None

    rows_back = gather_rows(shards_back, gate)
    output = traded[0].reshape(inputs.shape)
    level = PartSum(after(sums, shards_back))
    sums = level.chips(level.cores())
    rows_back[1] = after(rows_back[1], sums)
    d_partial, d_weights = mix_backward(rows_back, analysis, synthesis, weights, cut, coeffs)
    three, single = scatter_weights(d_weights)
    d_modes, midway = zip(*[scatter_rows(*chunk) for chunk in d_partial])
    plane_pieces = after(gathered(after(sums, midway), "lat"), d_modes)
    sum_pieces = gathered(sum(in_order(plane_pieces, "lat")), "lon")
    traded = by_chip(after(d_modes, single))
    double = finish_weight_sum(d_weights, three, (traded, sum_pieces))
    sums = level.share(sum_pieces)
    other_sums = swap_cores(sums)
    d_inputs, d_norm = leave(
        quadrature, traded, to_columns_back, values, after(d_skipped, other_sums), gain_one
    )
    sums = level.finish(sums, other_sums)
    d_norm = sum_over_planes(d_norm + swap_cores(d_norm))
    norm_pieces = gathered(d_norm, "lon")
    d_inputs = wide(trade(d_inputs)).reshape(inputs.shape)
    d_norm = sum(in_order(norm_pieces, "lon"))
    halves = sum_weights(d_weights, single, after(double, norm_pieces))
    others = [swap_cores(part) for part in halves]
    own_first = [jnp.where(core == 0, mine, other) for mine, other in zip(halves, others)]
    own_last = [jnp.where(core == 0, other, mine) for mine, other in zip(halves, others)]
    own_last[0] = own_last[0][2 * half - owned :]
    d_spectral = jnp.concatenate([wide(part) for part in own_first + own_last], 0)

    hidden = w_up.shape[1]
    d_up = jnp.concatenate([sums[j * width : j * width + width] for j in range(hidden // width)], 1)
    d_down = sums[hidden : 2 * hidden]
    vectors = sums[2 * hidden :]
    pieces = hidden // width
    d_up_bias = vectors[:pieces].reshape(-1)
    d_down_bias, d_gain_two, d_shift_two, first_moment, second_moment = [vectors[pieces + j] for j in range(5)]
    count = sums[count_row, 0]
    batch_mean = first_moment / count
    batch_var = second_moment / count - batch_mean * batch_mean
    new_mean = (1.0 - momentum) * run_mean + momentum * batch_mean
    new_var = (1.0 - momentum) * run_var + momentum * batch_var
    return (
        output,
        d_inputs,
        d_norm[0],
        d_norm[1],
        d_spectral,
        d_gain_two,
        d_shift_two,
        d_up,
        d_up_bias,
        d_down,
        d_down_bias,
        new_mean,
        new_var,
    )


def fourier_tables(points, modes):
    column = jnp.arange(points, dtype=jnp.int32)
    order = jnp.arange(modes, dtype=jnp.int32)
    phase = column[:, None] * order[None, :] % points
    angle = phase.astype(jnp.float32) * (2.0 * math.pi / points)
    cosine = jnp.cos(angle)
    sine = jnp.sin(angle)
    scale = 1.0 / math.sqrt(points)
    forward_tab = jnp.stack([cosine * scale, -sine * scale], 1)
    factor = jnp.where(order == 0, 1.0, 2.0).astype(jnp.float32)
    inverse_tab = jnp.stack([(cosine * factor[None, :]).T, (-sine * factor[None, :]).T], 0)
    return (forward_tab.astype(jnp.bfloat16), inverse_tab.astype(jnp.bfloat16))


def grid_angles(rows_total):
    first_row = (GRID_ROWS - rows_total) // 2
    colatitude = (jnp.arange(rows_total, dtype=jnp.float32) + (first_row + 0.5)) * (
        math.pi / GRID_ROWS
    )
    return (jnp.cos(colatitude), jnp.sin(colatitude))


def legendre_scan(orders, cosines, sine_vals, degrees):
    order_col = orders[:, None]
    cos_row = cosines[None, :]
    log_start = 0.5 * (
        jnp.log((2.0 * order_col + 1.0) / (4.0 * math.pi))
        + lax.lgamma(order_col + 0.5)
        - lax.lgamma(order_col + 1.0)
        - 0.5 * math.log(math.pi)
    ) + order_col * jnp.log(sine_vals[None, :])
    diagonal_start = jnp.exp(log_start)
    second_start = cos_row * jnp.sqrt(2.0 * order_col + 3.0) * diagonal_start
    zeros_grid = jnp.zeros_like(diagonal_start)

    def advance(state, degree):
        before, latest = state
        upper_ratio = jnp.sqrt(
            (4.0 * degree * degree - 1.0)
            / jnp.maximum(degree * degree - order_col * order_col, 1.0)
        )
        lower_ratio = jnp.sqrt(
            jnp.maximum((degree - 1.0) * (degree - 1.0) - order_col * order_col, 0.0)
            / jnp.maximum(4.0 * (degree - 1.0) * (degree - 1.0) - 1.0, 1.0)
        )
        general = upper_ratio * (cos_row * latest - lower_ratio * before)
        current = jnp.where(
            degree < order_col,
            0.0,
            jnp.where(
                degree == order_col,
                diagonal_start,
                jnp.where(degree == order_col + 1.0, second_start, general),
            ),
        )
        return ((latest, current), current)

    ignored, stacked = lax.scan(
        advance, (zeros_grid, zeros_grid), jnp.arange(degrees).astype(cosines.dtype)
    )
    stacked = jnp.transpose(stacked, (1, 0, 2))
    degree_index = jnp.arange(degrees).astype(cosines.dtype)
    keep = (orders[:, None, None] < M) & (degree_index[None, :, None] < L)
    return jnp.where(keep, stacked, 0.0)


def mix_modes(coeffs, spectral):
    product = jnp.einsum("bmlrc,lscd->bmlrsd", coeffs, spectral, preferred_element_type=jnp.float32)
    real_part = product[:, :, :, 0, 0] - product[:, :, :, 1, 1]
    imag_part = product[:, :, :, 0, 1] + product[:, :, :, 1, 0]
    return jnp.stack([real_part, imag_part], 3).astype(jnp.bfloat16)


def coeff_back(d_mixed, spectral):
    returned = jnp.einsum(
        "bmlsd,lrcd->bmlsrc", d_mixed, spectral, preferred_element_type=jnp.float32
    )
    d_real = returned[:, :, :, 0, 0] + returned[:, :, :, 1, 1]
    d_imag = returned[:, :, :, 1, 0] - returned[:, :, :, 0, 1]
    return jnp.stack([d_real, d_imag], 3).astype(jnp.bfloat16)


def weight_back(coeffs, d_mixed):
    outer_sum = jnp.einsum(
        "bmlrc,bmlsd->lrscd", coeffs, d_mixed, preferred_element_type=jnp.float32
    )
    d_weight_real = outer_sum[:, 0, 0] + outer_sum[:, 1, 1]
    d_weight_imag = outer_sum[:, 0, 1] - outer_sum[:, 1, 0]
    return jnp.stack([d_weight_real, d_weight_imag], 1)


def degree_shards(
    inputs,
    gain_one,
    shift_one,
    spectral,
    gain_two,
    shift_two,
    w_up,
    b_up,
    w_down,
    b_down,
    crops,
    cotangent,
    run_mean,
    run_var,
    momentum,
):
    lat_count = lax.axis_size("lat")
    lon_count = lax.axis_size("lon")
    rows_dev = inputs.shape[1]
    cols_dev = inputs.shape[2]
    width = inputs.shape[3]
    lat_rows = rows_dev * lat_count
    lon_cols = cols_dev * lon_count
    modes_dev = (M + lat_count - 1) // lat_count
    modes_all = modes_dev * lat_count
    quarter = width // lon_count
    owned = spectral.shape[0]
    degrees_all = owned * lat_count * lon_count
    forward_tab, inverse_tab = fourier_tables(lon_cols, modes_all)
    cosines, sine_vals = grid_angles(lat_rows)
    orders = (lax.axis_index("lat") * modes_dev + jnp.arange(modes_dev, dtype=jnp.int32)).astype(
        jnp.float32
    )
    poly = legendre_scan(orders, cosines, sine_vals, degrees_all)
    quadrature = sine_vals * (math.pi / GRID_ROWS) * (2.0 * math.pi / math.sqrt(lon_cols))
    analysis = (poly * quadrature[None, None, :]).astype(jnp.bfloat16)
    synthesis = (
        poly.astype(jnp.bfloat16)
        .reshape(modes_dev, lat_count, lon_count, owned, lat_rows)
        .transpose(0, 2, 1, 3, 4)
    )
    input_wide = inputs.astype(jnp.float32)
    normed_one, norm_one_back = jax.vjp(layer_norm, input_wide, gain_one, shift_one)
    normed_low = normed_one.astype(jnp.bfloat16)
    fourier = jnp.einsum(
        "bijc,jrm->birmc",
        lax.all_to_all(normed_low, "lon", split_axis=3, concat_axis=2, tiled=True),
        forward_tab,
        preferred_element_type=jnp.float32,
    ).astype(jnp.bfloat16)
    portion = lax.all_to_all(fourier, "lat", split_axis=3, concat_axis=1, tiled=True)
    coeffs = jnp.einsum(
        "mli,birmc->bmlrc", analysis, portion, preferred_element_type=jnp.float32
    ).astype(jnp.bfloat16)
    coeffs = coeffs.reshape(1, modes_dev, lat_count, lon_count, owned, 2, portion.shape[4])
    owned_coeffs = lax.all_to_all(
        lax.all_to_all(coeffs, "lat", split_axis=2, concat_axis=1, tiled=True),
        "lon",
        split_axis=3,
        concat_axis=6,
        tiled=True,
    )
    coeffs_owned = owned_coeffs.reshape(1, modes_all, owned, 2, width)
    mixed_modes = mix_modes(coeffs_owned, spectral).reshape(1, modes_all, 1, 1, owned, 2, width)
    returned = lax.all_to_all(
        lax.all_to_all(mixed_modes, "lat", split_axis=1, concat_axis=3, tiled=True),
        "lon",
        split_axis=6,
        concat_axis=2,
        tiled=True,
    )
    grid_modes = jnp.einsum(
        "mjkqi,bmjkqrc->birmc", synthesis, returned, preferred_element_type=jnp.float32
    ).astype(jnp.bfloat16)
    spread = jnp.einsum(
        "birmc,rmj->bijc",
        lax.all_to_all(grid_modes, "lat", split_axis=1, concat_axis=3, tiled=True),
        inverse_tab,
        preferred_element_type=jnp.float32,
    ).astype(jnp.bfloat16)
    spectral_out = lax.all_to_all(spread, "lon", split_axis=2, concat_axis=3, tiled=True)
    skipped = input_wide + spectral_out.astype(jnp.float32)
    normed_two, norm_two_back = jax.vjp(layer_norm, skipped, gain_two, shift_two)
    normed_two_low = normed_two.astype(jnp.bfloat16)
    preact = (
        jnp.einsum("bijc,ch->bijh", normed_two_low, w_up, preferred_element_type=jnp.float32) + b_up
    )
    activated, gelu_back = jax.vjp(jax.nn.gelu, preact)
    activated_low = activated.astype(jnp.bfloat16)
    result = (
        skipped
        + jnp.einsum("bijh,hc->bijc", activated_low, w_down, preferred_element_type=jnp.float32)
        + b_down
    )
    output = result.astype(jnp.bfloat16)
    bounds = crops[0]
    row_global = lax.axis_index("lat") * rows_dev + jnp.arange(rows_dev, dtype=jnp.int32)
    col_global = lax.axis_index("lon") * cols_dev + jnp.arange(cols_dev, dtype=jnp.int32)
    inside_rows = (row_global >= bounds[0]) & (row_global < bounds[1])
    inside_cols = (col_global >= bounds[2]) & (col_global < bounds[3])
    mask_grid = (inside_rows[:, None] & inside_cols[None, :]).astype(jnp.float32)[None, :, :, None]
    valid_count = jnp.sum(mask_grid)
    first_moment = jnp.sum(mask_grid * result, (0, 1, 2))
    second_moment = jnp.sum(mask_grid * result * result, (0, 1, 2))
    grad_wide = cotangent.astype(jnp.float32)
    d_down = jnp.einsum(
        "bijh,bijc->hc", activated_low, cotangent, preferred_element_type=jnp.float32
    )
    d_down_bias = jnp.sum(grad_wide, (0, 1, 2))
    d_activated = jnp.einsum("bijc,hc->bijh", cotangent, w_down, preferred_element_type=jnp.float32)
    d_preact = gelu_back(d_activated)[0].astype(jnp.bfloat16)
    d_up = jnp.einsum("bijc,bijh->ch", normed_two_low, d_preact, preferred_element_type=jnp.float32)
    d_up_bias = jnp.sum(d_preact.astype(jnp.float32), (0, 1, 2))
    d_normed_two = jnp.einsum("bijh,ch->bijc", d_preact, w_up, preferred_element_type=jnp.float32)
    d_skipped, d_gain_two, d_shift_two = norm_two_back(d_normed_two)
    d_skipped = d_skipped + grad_wide
    d_spread = d_skipped.astype(jnp.bfloat16)
    d_grid = jnp.einsum(
        "bijc,rmj->birmc",
        lax.all_to_all(d_spread, "lon", split_axis=3, concat_axis=2, tiled=True),
        inverse_tab,
        preferred_element_type=jnp.float32,
    ).astype(jnp.bfloat16)
    d_returned = jnp.einsum(
        "mjkqi,birmc->bmjkqrc",
        synthesis,
        lax.all_to_all(d_grid, "lat", split_axis=3, concat_axis=1, tiled=True),
        preferred_element_type=jnp.float32,
    ).astype(jnp.bfloat16)
    d_mixed = lax.all_to_all(
        lax.all_to_all(d_returned, "lat", split_axis=3, concat_axis=1, tiled=True),
        "lon",
        split_axis=2,
        concat_axis=6,
        tiled=True,
    ).reshape(1, modes_all, owned, 2, width)
    d_coeffs = coeff_back(d_mixed, spectral)
    d_spectral = lax.psum(weight_back(coeffs_owned, d_mixed).astype(jnp.bfloat16), "batch").astype(
        jnp.float32
    )
    d_coeffs_wide = d_coeffs.reshape(1, modes_all, 1, 1, owned, 2, width)
    d_modes = lax.all_to_all(
        lax.all_to_all(d_coeffs_wide, "lat", split_axis=1, concat_axis=2, tiled=True),
        "lon",
        split_axis=6,
        concat_axis=3,
        tiled=True,
    ).reshape(1, modes_dev, degrees_all, 2, quarter)
    d_fourier = jnp.einsum(
        "mli,bmlrc->birmc", analysis, d_modes, preferred_element_type=jnp.float32
    ).astype(jnp.bfloat16)
    d_columns = jnp.einsum(
        "birmc,jrm->bijc",
        lax.all_to_all(d_fourier, "lat", split_axis=1, concat_axis=3, tiled=True),
        forward_tab,
        preferred_element_type=jnp.float32,
    ).astype(jnp.bfloat16)
    d_normed_one = lax.all_to_all(d_columns, "lon", split_axis=2, concat_axis=3, tiled=True).astype(
        jnp.float32
    )
    d_input_norm, d_gain_one, d_shift_one = norm_one_back(d_normed_one)
    d_inputs = d_input_norm + d_skipped
    summed = lax.psum(
        (
            d_up,
            d_down,
            d_up_bias,
            d_down_bias,
            d_gain_one,
            d_shift_one,
            d_gain_two,
            d_shift_two,
            valid_count,
            first_moment,
            second_moment,
        ),
        ("lat", "lon", "batch"),
    )
    batch_mean = summed[9] / summed[8]
    batch_var = summed[10] / summed[8] - batch_mean * batch_mean
    new_mean = (1.0 - momentum) * run_mean + momentum * batch_mean
    new_var = (1.0 - momentum) * run_var + momentum * batch_var
    return (
        output,
        d_inputs,
        summed[4],
        summed[5],
        d_spectral,
        summed[6],
        summed[7],
        summed[0],
        summed[2],
        summed[1],
        summed[3],
        new_mean,
        new_var,
    )


def shards(inputs, *rest):
    rows_dev = inputs.shape[1]
    lon_count = lax.axis_size("lon")
    banded = (
        lon_count == 4
        and lax.axis_size("batch") == 2
        and rows_dev == 2 * lon_count
        and M % lon_count == 0
        and M // lon_count <= 128
        and rest[2].shape[0] % 4 in (0, 3)
        and rows_dev * lax.axis_size("lat") <= 32
    )
    return (band_shards if banded else degree_shards)(inputs, *rest)


def solution(mesh):
    return jax.shard_map(
        shards,
        mesh=mesh,
        in_specs=(
            P("batch", "lat", "lon", None),
            P(),
            P(),
            P(("lat", "lon"), None, None, None),
            P(),
            P(),
            P(),
            P(),
            P(),
            P(),
            P("batch", None),
            P("batch", "lat", "lon", None),
            P(),
            P(),
            P(),
        ),
        out_specs=(
            P("batch", "lat", "lon", None),
            P("batch", "lat", "lon", None),
            P(),
            P(),
            P(("lat", "lon"), None, None, None),
            P(),
            P(),
            P(),
            P(),
            P(),
            P(),
            P(),
            P(),
        ),
        check_vma=False,
    )
```
